32 devices in a mesh: dp: 8 (over y, x, core), blk: 4 (over z).
Axes of the slice: x: 2, y: 2, z: 4, core: 2. Of those that a mesh axis runs over, the one named last changes fastest.
Arguments:
- clips: bfloat16 [64, 8, 8, 8, 528], P('dp', 'blk'), may hold values from -19 to 19
- cotangent: bfloat16 [64, 4, 4, 4, 832], P('dp', 'blk'), may hold values from -19 to 19
- entry_4f: bfloat16 [2, 236544], P(None, 'blk'), may hold values from -0.25 to 0.25
- wide_4f: bfloat16 [2, 1382400], P(None, 'blk'), may hold values from -0.09375 to 0.09375
- narrow_4f: bfloat16 [2, 110592], P(None, 'blk'), may hold values from -0.21875 to 0.21875
- poolproj_4f: bfloat16 [2, 67584], P(None, 'blk'), may hold values from -0.25 to 0.25
- gain_4f: bfloat16 [2, 1024], P(None, 'blk'), may hold values from 0.099609375 to 1.8984375
- shift_4f: bfloat16 [2, 1024], P(None, 'blk'), may hold values from -2.5 to 2.5
- entry_5b: bfloat16 [2, 372736], P(None, 'blk'), may hold values from -0.21875 to 0.21875
- wide_5b: bfloat16 [2, 1382400], P(None, 'blk'), may hold values from -0.09375 to 0.09375
- narrow_5b: bfloat16 [2, 110592], P(None, 'blk'), may hold values from -0.21875 to 0.21875
- poolproj_5b: bfloat16 [2, 106496], P(None, 'blk'), may hold values from -0.21875 to 0.21875
- gain_5b: bfloat16 [2, 1024], P(None, 'blk'), may hold values from 0.099609375 to 1.8984375
- shift_5b: bfloat16 [2, 1024], P(None, 'blk'), may hold values from -2.5 to 2.5
Outputs:
- features: float32 [64, 4, 4, 4, 832], P('dp', 'blk')
- clips_grad: float32 [64, 8, 8, 8, 528], P('dp', 'blk')
- entry_4f_grad: float32 [2, 236544], P(None, 'blk')
- wide_4f_grad: float32 [2, 1382400], P(None, 'blk')
- narrow_4f_grad: float32 [2, 110592], P(None, 'blk')
- poolproj_4f_grad: float32 [2, 67584], P(None, 'blk')
- gain_4f_grad: float32 [2, 1024], P(None, 'blk')
- shift_4f_grad: float32 [2, 1024], P(None, 'blk')
- entry_5b_grad: float32 [2, 372736], P(None, 'blk')
- wide_5b_grad: float32 [2, 1382400], P(None, 'blk')
- narrow_5b_grad: float32 [2, 110592], P(None, 'blk')
- poolproj_5b_grad: float32 [2, 106496], P(None, 'blk')
- gain_5b_grad: float32 [2, 1024], P(None, 'blk')
- shift_5b_grad: float32 [2, 1024], P(None, 'blk')
The draws below stay inside these ranges and needn't reach their ends.
All inputs are finite; a program needn't handle non-finite values.
Results may differ from the reference program's by a relative error of at most 0.022.
Values may be sent and summed in bfloat16 or wider, within the bound.
No kernel may reach another device: no remote copies, remote signals or barrier semaphores. Data moves between devices by JAX's collectives and lax.ppermute only.
A program may use at most 256 MiB of HBM per device.

```python
import jax
import jax.numpy as jnp
from jax import lax

C_FIRST = 528
B0 = 256
B1R = 160
B1 = 320
B2R = 32
B2 = 128
BP = 128
HEIGHT = 8
WIDTH = 8
C_IN = 832
GAINS = 1024
FRAMES = 8
CLIPS = 64


def scaled_field(key, shape, clip_count):
    ramp = jnp.arange(clip_count, dtype=jnp.float32) / max(clip_count - 1, 1)
    noise = jnp.clip(jax.random.normal(key, shape, jnp.float32), -6.0, 6.0)
    factor = 3.0 ** ramp
    return noise * factor.reshape(-1, 1, 1, 1, 1)


def draw_clips(key, part):
    key = jax.random.fold_in(key, 11)
    shape = (CLIPS, FRAMES, HEIGHT, WIDTH, C_FIRST)
    return scaled_field(key, shape, CLIPS).astype(jnp.bfloat16)


def draw_cotangent(key, part):
    key = jax.random.fold_in(key, 12)
    shape = (CLIPS, FRAMES // 2, HEIGHT // 2, WIDTH // 2, C_IN)
    return scaled_field(key, shape, CLIPS).astype(jnp.bfloat16)


def block_scale(key, shape, split, least, top_value):
    level, own = 1.0, jax.random.fold_in(key, 6)
    for axis_at, shards_of in split:
        draws = jnp.exp(jax.random.uniform(jax.random.fold_in(own, axis_at), (shards_of,), jnp.float32, least / len(split), top_value / len(split)))
        level = level * jnp.repeat(draws, shape[axis_at] // shards_of).reshape([-1 if axis == axis_at else 1 for axis in range(len(shape))])
    return level


def gaussian(rng, shape, scale, bound, shards=(), kind=jnp.bfloat16):
    values = jax.random.normal(rng, shape, jnp.float32) * scale
    if len(shards) > 0:
        values = block_scale(rng, shape, shards, -0.22, 0.18) * values
    return jnp.clip(values, min=-bound, max=bound).astype(kind)


def setup_inputs(seed: int = 0) -> dict:
    key_of = jax.random.split(jax.random.key(seed), 15)
    return {
        "clips": draw_clips(jax.random.fold_in(key_of[14], 71), 0),
        "cotangent": draw_cotangent(jax.random.fold_in(key_of[14], 71), 0),
        "entry_4f": gaussian(key_of[2], (2, (B0 + B1R + B2R) * C_FIRST), C_FIRST ** -0.5, 0.25, ((1, 4),)),
        "wide_4f": gaussian(key_of[3], (2, B1 * 27 * B1R), (27 * B1R) ** -0.5, 0.09375, ((1, 4),)),
        "narrow_4f": gaussian(key_of[4], (2, B2 * 27 * B2R), (27 * B2R) ** -0.5, 0.21875, ((1, 4),)),
        "poolproj_4f": gaussian(key_of[5], (2, BP * C_FIRST), C_FIRST ** -0.5, 0.25, ((1, 4),)),
        "gain_4f": jnp.clip(1.0 + 0.18 * jax.random.normal(key_of[6], (2, GAINS), jnp.float32), 0.099609375, 1.8984375).astype(jnp.bfloat16),
        "shift_4f": gaussian(key_of[7], (2, GAINS), 0.5, 2.5, ((1, 4),)),
        "entry_5b": gaussian(key_of[8], (2, (B0 + B1R + B2R) * C_IN), C_IN ** -0.5, 0.21875, ((1, 4),)),
        "wide_5b": gaussian(key_of[9], (2, B1 * 27 * B1R), (27 * B1R) ** -0.5, 0.09375, ((1, 4),)),
        "narrow_5b": gaussian(key_of[10], (2, B2 * 27 * B2R), (27 * B2R) ** -0.5, 0.21875, ((1, 4),)),
        "poolproj_5b": gaussian(key_of[11], (2, BP * C_IN), C_IN ** -0.5, 0.21875, ((1, 4),)),
        "gain_5b": jnp.clip(1.0 + 0.18 * jax.random.normal(key_of[12], (2, GAINS), jnp.float32), 0.099609375, 1.8984375).astype(jnp.bfloat16),
        "shift_5b": gaussian(key_of[13], (2, GAINS), 0.5, 2.5, ((1, 4),)),
    }


@jax.custom_vjp
def low(v):
    return lax.optimization_barrier(v.astype(jnp.bfloat16)).astype(jnp.float32)

@jax.custom_vjp
def low_back(v):
    return v

def low_keep(v):
    return (low(v), None)

def low_pass(kept, grad):
    return (grad,)

def back_keep(v):
    return (v, None)

def back_low(kept, grad):
    return (low(grad),)
low.defvjp(low_keep, low_pass)
low_back.defvjp(back_keep, back_low)
EPS = 1e-05
HIGH = lax.Precision.HIGHEST

def pool_three(values):
    padded = jnp.pad(values, ((0, 0), (1, 1), (1, 1), (1, 1), (0, 0)))
    frames, height, breadth = (values.shape[1], values.shape[2], values.shape[3])
    summed = jnp.zeros(values.shape, jnp.float32)
    for tap_index in range(27):
        depth_off = tap_index // 9
        row_off = tap_index // 3 % 3
        col_off = tap_index % 3
        summed = summed + padded[:, depth_off:depth_off + frames, row_off:row_off + height, col_off:col_off + breadth, :]
    return summed / 27.0

def conv_three(values, kernel):
    shaped = kernel.reshape(3, 3, 3, kernel.shape[1], kernel.shape[2])
    return lax.conv_general_dilated(values, shaped, (1, 1, 1), 'SAME', dimension_numbers=('NDHWC', 'DHWIO', 'NDHWC'), precision=HIGH)

def pointwise(values, matrix):
    return jnp.einsum('nfhwc,cd->nfhwd', values, matrix, precision=HIGH)

def norm_silu(values, gain, shift):
    centre = lax.optimization_barrier(jnp.mean(values, axis=(0, 1, 2, 3)))
    square = lax.optimization_barrier(jnp.mean(values * values, axis=(0, 1, 2, 3)))
    scaled = (values - centre) * lax.rsqrt(square - centre * centre + EPS)
    return jax.nn.silu(scaled * gain + shift)

def unflatten(flat_entry, flat_wide, flat_narrow, flat_pool):
    reduced = B0 + B1R + B2R
    entry = flat_entry.reshape(reduced, -1).T
    wide = flat_wide.reshape(B1, 27, B1R).transpose(1, 2, 0)
    narrow = flat_narrow.reshape(B2, 27, B2R).transpose(1, 2, 0)
    poolproj = flat_pool.reshape(BP, -1).T
    return (entry, wide, narrow, poolproj)

def inception(inputs, flat_entry, flat_wide, flat_narrow, flat_pool, gain, shift):
    entry, wide, narrow, poolproj = unflatten(flat_entry, flat_wide, flat_narrow, flat_pool)
    reduced = entry.shape[1]
    inner_wide = wide.shape[1]
    direct = reduced - inner_wide - narrow.shape[1]
    wide_end = reduced + wide.shape[2]
    narrow_end = wide_end + narrow.shape[2]
    inputs_low = low(inputs)
    front = low_back(pointwise(inputs_low, entry))
    acted = norm_silu(front, gain[:reduced], shift[:reduced])
    wide_in = low(acted[..., direct:direct + inner_wide])
    narrow_in = low(acted[..., direct + inner_wide:])
    pooled = low(pool_three(inputs_low))
    wide_out = low_back(conv_three(wide_in, wide))
    narrow_out = low_back(conv_three(narrow_in, narrow))
    pool_out = low_back(pointwise(pooled, poolproj))
    return jnp.concatenate([acted[..., :direct], norm_silu(wide_out, gain[reduced:wide_end], shift[reduced:wide_end]), norm_silu(narrow_out, gain[wide_end:narrow_end], shift[wide_end:narrow_end]), norm_silu(pool_out, gain[narrow_end:], shift[narrow_end:])], axis=-1)

def pool_two(values):
    clip_count, frames, height, breadth, channels = values.shape
    return values.reshape(clip_count, frames // 2, 2, height // 2, 2, breadth // 2, 2, channels).mean(axis=(2, 4, 6))

def network(inputs, params):
    layer_fn = jax.checkpoint(inception)
    streams = []
    for stream in range(2):
        early = [tensor[stream] for tensor in params[:6]]
        late = [tensor[stream] for tensor in params[6:]]
        middle = pool_two(layer_fn(inputs[stream], early[0], early[1], early[2], early[3], early[4], early[5]))
        streams.append(layer_fn(middle, late[0], late[1], late[2], late[3], late[4], late[5]))
    return jnp.stack(streams)

def reference(clips, cotangent, entry_4f, wide_4f, narrow_4f, poolproj_4f, gain_4f, shift_4f, entry_5b, wide_5b, narrow_5b, poolproj_5b, gain_5b, shift_5b):
    params = tuple((tensor.astype(jnp.float32) for tensor in (entry_4f, wide_4f, narrow_4f, poolproj_4f, gain_4f, shift_4f, entry_5b, wide_5b, narrow_5b, poolproj_5b, gain_5b, shift_5b)))
    per_stream = clips.shape[0] // 2
    inputs = clips.astype(jnp.float32).reshape((2, per_stream) + clips.shape[1:])
    outputs, pullback = jax.vjp(network, inputs, params)
    grad_inputs, grads = pullback(cotangent.astype(jnp.float32).reshape(outputs.shape))
    return (outputs.reshape((2 * per_stream,) + outputs.shape[2:]), grad_inputs.reshape(clips.shape), grads[0], grads[1], grads[2], grads[3], grads[4], grads[5], grads[6], grads[7], grads[8], grads[9], grads[10], grads[11])
```

```python
import jax
import jax.numpy as jnp
from jax import lax
from jax.sharding import PartitionSpec as P

B0 = 256
B1R = 160
B1 = 320
B2R = 32
B2 = 128
BP = 128
INNER = B1R + B2R
REDUCED = B0 + INNER
OUTER = B1 + B2
EPS = 1e-05
BF = jnp.bfloat16
F32 = jnp.float32
DIMS = ("NDHWC", "DHWIO", "NDHWC")
SAME = ((1, 1), (1, 1), (1, 1))


def xor_pairs(axis, step):
    return [(i, i ^ step) for i in range(lax.axis_size(axis))]


def tower_steps():
    steps, step = [], 1
    while step < lax.axis_size("dp") // 2:
        steps.append(step)
        step *= 2
    return steps


def other_tower(value):
    return lax.ppermute(value, "dp", xor_pairs("dp", lax.axis_size("dp") // 2))


def blk_peers(value):
    count = lax.axis_size("blk")
    return [value] + [lax.ppermute(value, "blk", xor_pairs("blk", k)) for k in range(1, count)]


def by_place(parts):
    me, step = lax.axis_index("blk"), 1
    while step < len(parts):
        hit = (me & step) != 0
        parts = [jnp.where(hit, parts[k ^ step], parts[k]) for k in range(len(parts))]
        step *= 2
    return parts


def gather_blk(value):
    return by_place(blk_peers(value))


def exchange_blk(chunks):
    mine = by_place(chunks)
    return [mine[0]] + [
        lax.ppermute(mine[k], "blk", xor_pairs("blk", k)) for k in range(1, len(mine))
    ]


def dp_sum(value):
    for step in tower_steps():
        value = value + lax.ppermute(value, "dp", xor_pairs("dp", step))
    return value


def blk_sum(value):
    parts = blk_peers(value)
    while len(parts) > 1:
        parts = [parts[i] + parts[i + 1] for i in range(0, len(parts), 2)]
    return parts[0]


def tower_sum(value):
    return blk_sum(dp_sum(value))


def gather_shared(shard):
    rows = shard.shape[0] // 2
    odd = lax.axis_index("dp") % 2
    half = lax.dynamic_slice_in_dim(shard, odd * rows, rows, 0)
    whole = jnp.stack(gather_blk(half))
    twin = lax.ppermute(whole, "dp", xor_pairs("dp", 1))
    low = jnp.where(odd == 0, whole, twin)
    high = jnp.where(odd == 0, twin, whole)
    return jnp.concatenate([low, high], axis=1)


def frame_halo(value):
    count = lax.axis_size("blk")
    ahead = [(i, i + 1) for i in range(count - 1)]
    back = [(i + 1, i) for i in range(count - 1)]
    before = lax.ppermute(value[:, -1:], "blk", ahead)
    after = lax.ppermute(value[:, :1], "blk", back)
    return before, after


def conv(values, kernel, pads):
    return lax.conv_general_dilated(
        values, kernel, (1, 1, 1), pads, dimension_numbers=DIMS, preferred_element_type=F32
    )


def weight_grad(values, grad, pads):
    return lax.conv_general_dilated(
        values,
        grad,
        (1, 1, 1),
        pads,
        dimension_numbers=("CDHWN", "IDHWO", "DHWNC"),
        preferred_element_type=F32,
    )


def pool_rows(padded):
    v = padded.astype(F32)
    v = v[:, :-2] + v[:, 1:-1] + v[:, 2:]
    for axis in (2, 3):
        pads = [(0, 0)] * 5
        pads[axis] = (1, 1)
        v = jnp.pad(v, pads)
        size = v.shape[axis]
        v = (
            lax.slice_in_dim(v, 0, size - 2, axis=axis)
            + lax.slice_in_dim(v, 1, size - 1, axis=axis)
            + lax.slice_in_dim(v, 2, size, axis=axis)
        )
    return v / 27.0


def moments(value):
    return jnp.stack([jnp.sum(value, (0, 1, 2, 3)), jnp.sum(value * value, (0, 1, 2, 3))])


def cross(grad, scaled):
    return jnp.stack([jnp.sum(grad, (0, 1, 2, 3)), jnp.sum(grad * scaled, (0, 1, 2, 3))])


def scale_of(sums, voxels):
    centre = sums[0] / voxels
    return centre, lax.rsqrt(sums[1] / voxels - centre * centre + EPS)


def silu_slope(y):
    sigmoid = jax.nn.sigmoid(y)
    return sigmoid * (1.0 + y * (1.0 - sigmoid))


def norm_back(dy, scaled, spread, gain, sums, voxels):
    return (gain * spread * (dy - sums[0] / voxels - scaled * (sums[1] / voxels))).astype(BF)


def block_kernel(wide, narrow):
    o, p = wide.shape[0], narrow.shape[0]
    wide = wide.reshape(o, 27, B1R).transpose(1, 2, 0)
    narrow = narrow.reshape(p, 27, B2R).transpose(1, 2, 0)
    wide = jnp.pad(wide, ((0, 0), (0, B2R), (0, p)))
    narrow = jnp.pad(narrow, ((0, 0), (B1R, 0), (o, 0)))
    return (wide + narrow).reshape(3, 3, 3, INNER, o + p)


def flip(kernel):
    return jnp.swapaxes(kernel, 3, 4)[::-1, ::-1, ::-1]


def kernel_rows(grad, o):
    grad = grad.reshape(27, INNER, grad.shape[-1])
    wide = grad[:, :B1R, :o].transpose(2, 0, 1)
    narrow = grad[:, B1R:, o:].transpose(2, 0, 1)
    return wide.reshape(wide.shape[0], -1), narrow.reshape(narrow.shape[0], -1)


def reduce_rows(part):
    steps = tower_steps()
    halved = []
    value = part.astype(BF)
    axis = value.ndim - 2
    for number, step in enumerate(steps):
        if number < 2:
            rows = value.shape[axis] // 2
            high = (lax.axis_index("dp") & step) != 0
            keep = lax.dynamic_slice_in_dim(value, jnp.where(high, rows, 0), rows, axis)
            give = lax.dynamic_slice_in_dim(value, jnp.where(high, 0, rows), rows, axis)
            halved.append(step)
        else:
            keep = give = value
        got = lax.ppermute(give, "dp", xor_pairs("dp", step))
        value = (keep.astype(F32) + got.astype(F32)).astype(BF)
    return value, halved


def spread_rows(value, halved):
    stream = lax.axis_index("dp") // (lax.axis_size("dp") // 2)
    other = other_tower(value)
    both = jnp.where(stream == 0, jnp.stack([value, other]), jnp.stack([other, value]))
    for step in reversed(halved):
        got = lax.ppermute(both, "dp", xor_pairs("dp", step))
        high = (lax.axis_index("dp") & step) != 0
        both = jnp.where(
            high, jnp.concatenate([got, both], 1), jnp.concatenate([both, got], 1)
        )
    return both.astype(F32)


def reduce_own(part):
    value, halved = reduce_rows(part)
    return spread_rows(value, halved)


def reduce_blk(part):
    value, halved = reduce_rows(part)
    got = exchange_blk([value[j] for j in range(value.shape[0])])
    total = got[0].astype(F32)
    for piece in got[1:]:
        total = total + piece.astype(F32)
    return spread_rows(total.astype(BF), halved)


def on_device(clips, cotangent, *params):
    groups = lax.axis_size("dp")
    count = lax.axis_size("blk")
    stream = lax.axis_index("dp") // (groups // 2)
    place = lax.axis_index("blk")
    own = [lax.dynamic_index_in_dim(p, stream, 0, keepdims=False) for p in params]
    early, late = own[:6], own[6:]
    n, frames, height, breadth, c_first = clips.shape
    voxels = groups // 2 * count * n * frames * height * breadth
    voxels_late = voxels // 8
    c_in = cotangent.shape[4]

    def pack_front(layer, c):
        norms = jnp.concatenate([layer[4], layer[5]])
        row = jnp.pad(norms, (0, c - norms.shape[0])).reshape(1, c)
        rows = jnp.concatenate([layer[0].reshape(-1, c), layer[3].reshape(-1, c), row])
        return jnp.pad(rows, ((0, -rows.shape[0] % 32), (0, 0)))

    def unpack_front(whole):
        e, p = REDUCED // count, BP // count
        entry = whole[:, :e].reshape(REDUCED, -1)
        pool = whole[:, e : e + p].reshape(BP, -1)
        g = (REDUCED + OUTER + BP) // count
        gain = whole[:, e + p, :g].reshape(-1).astype(F32)
        shift = whole[:, e + p, g : 2 * g].reshape(-1).astype(F32)
        return jnp.concatenate([entry, pool]), gain, shift

    own_wide = B1 // count
    own_narrow = B2 // count
    own_cols = own_wide + own_narrow

    front_4, gain_4, shift_4 = unpack_front(gather_shared(pack_front(early, c_first)))
    wide_4 = gather_shared(early[1].reshape(own_wide, -1)).reshape(B1, -1)
    narrow_4 = gather_shared(early[2].reshape(own_narrow, -1)).reshape(B2, -1)
    kernel_4 = block_kernel(wide_4, narrow_4)
    front_5, gain_5, shift_5 = unpack_front(gather_shared(pack_front(late, c_in)))
    kernel_5 = block_kernel(late[1].reshape(own_wide, -1), late[2].reshape(own_narrow, -1))

    def cols_of(value, j):
        return jnp.concatenate(
            [
                value[..., B0 + j * own_wide : B0 + (j + 1) * own_wide],
                value[..., B0 + B1 + j * own_narrow : B0 + B1 + (j + 1) * own_narrow],
            ],
            axis=-1,
        )

    cot_own = by_place(exchange_blk([cols_of(cotangent, j) for j in range(count)]))
    cot_own = jnp.concatenate(cot_own, axis=1)

    def own_norms(vector):
        wide = lax.dynamic_slice_in_dim(vector, REDUCED + place * own_wide, own_wide, 0)
        narrow = lax.dynamic_slice_in_dim(vector, REDUCED + B1 + place * own_narrow, own_narrow, 0)
        return jnp.concatenate([wide, narrow])

    product = jnp.einsum("nfhwc,oc->nfhwo", clips, front_4, preferred_element_type=F32)
    front, pre_pool = product[..., :REDUCED], product[..., REDUCED:]
    centre_f4, spread_f4 = scale_of(tower_sum(moments(front)), voxels)
    before, after = frame_halo(pre_pool.astype(BF))
    pool_out = pool_rows(jnp.concatenate([before.astype(F32), pre_pool, after.astype(F32)], 1))
    scaled_f4 = (front - centre_f4) * spread_f4
    act = jax.nn.silu(scaled_f4 * gain_4[:REDUCED] + shift_4[:REDUCED])
    inner = act[..., B0:].astype(BF)
    before, after = frame_halo(inner)
    inner_pad = jnp.concatenate([before, inner, after], 1)
    branch = jnp.concatenate([conv(inner_pad, kernel_4, ((0, 0), (1, 1), (1, 1))), pool_out], 4)
    centre_b4, spread_b4 = scale_of(tower_sum(moments(branch)), voxels)
    scaled_b4 = (branch - centre_b4) * spread_b4
    y_b4 = scaled_b4 * gain_4[REDUCED:] + shift_4[REDUCED:]
    layer = jnp.concatenate([act[..., :B0], jax.nn.silu(y_b4)], 4)
    middle = layer.reshape(n, frames // 2, 2, height // 2, 2, breadth // 2, 2, c_in)
    middle = middle.mean(axis=(2, 4, 6)).astype(BF)

    product5 = jnp.einsum("nfhwc,oc->nfhwo", middle, front_5, preferred_element_type=F32)
    front5, pre_pool5 = product5[..., :REDUCED], product5[..., REDUCED:]
    before, after = frame_halo(pre_pool5.astype(BF))
    pool_out5 = pool_rows(jnp.concatenate([before.astype(F32), pre_pool5, after.astype(F32)], 1))
    centre_f5, spread_f5 = scale_of(tower_sum(moments(front5)), voxels_late)
    scaled_f5 = (front5 - centre_f5) * spread_f5
    y_f5 = scaled_f5 * gain_5[:REDUCED] + shift_5[:REDUCED]
    act5 = jax.nn.silu(y_f5)
    inner5 = jnp.concatenate(gather_blk(act5[..., B0:].astype(BF)), axis=1)
    pool_sums5 = blk_sum(moments(pool_out5))
    conv5 = conv(inner5, kernel_5, SAME)
    sums5 = dp_sum(jnp.concatenate([moments(conv5), pool_sums5], axis=1))
    gain_c5, shift_c5 = own_norms(gain_5), own_norms(shift_5)
    centre_c5, spread_c5 = scale_of(sums5[:, :own_cols], voxels_late)
    scaled_c5 = (conv5 - centre_c5) * spread_c5
    y_c5 = scaled_c5 * gain_c5 + shift_c5
    centre_p5, spread_p5 = scale_of(sums5[:, own_cols:], voxels_late)
    gain_p5, shift_p5 = gain_5[REDUCED + OUTER :], shift_5[REDUCED + OUTER :]
    scaled_p5 = (pool_out5 - centre_p5) * spread_p5
    y_p5 = scaled_p5 * gain_p5 + shift_p5

    dy_c5 = cot_own.astype(F32) * silu_slope(y_c5)
    dy_p5 = cotangent[..., B0 + OUTER :].astype(F32) * silu_slope(y_p5)
    back5 = dp_sum(jnp.concatenate([cross(dy_c5, scaled_c5), cross(dy_p5, scaled_p5)], axis=1))
    back_c5 = back5[:, :own_cols]
    back_p5 = blk_sum(back5[:, own_cols:])
    grad_c5 = norm_back(dy_c5, scaled_c5, spread_c5, gain_c5, back_c5, voxels_late)
    part5 = conv(grad_c5, flip(kernel_5), SAME)
    got = exchange_blk([part5[:, j : j + 1].astype(BF) for j in range(count)])
    inner_grad5 = got[0].astype(F32)
    for piece in got[1:]:
        inner_grad5 = inner_grad5 + piece.astype(F32)
    grad_p5 = norm_back(dy_p5, scaled_p5, spread_p5, gain_p5, back_p5, voxels_late)
    before, after = frame_halo(grad_p5)
    pool_back5 = pool_rows(jnp.concatenate([before, grad_p5, after], 1)).astype(BF)
    dy_f5 = jnp.concatenate(
        [cotangent[..., :B0].astype(F32), inner_grad5], 4
    ) * silu_slope(y_f5)
    placed = jnp.where(jnp.arange(count)[:, None, None] == place, back_c5[None], 0.0)
    placed = jnp.where(lax.axis_index("dp") % (groups // 2) == 0, placed, 0.0)
    placed = placed.transpose(1, 0, 2).reshape(2, -1)
    front_back5 = tower_sum(jnp.concatenate([cross(dy_f5, scaled_f5), placed], axis=1))
    back_all5 = front_back5[:, REDUCED:].reshape(2, count, own_cols)
    norms_5 = jnp.concatenate(
        [
            front_back5[:, :REDUCED],
            back_all5[:, :, :own_wide].reshape(2, -1),
            back_all5[:, :, own_wide:].reshape(2, -1),
            back_p5,
        ],
        axis=1,
    )
    grad_f5 = norm_back(
        dy_f5, scaled_f5, spread_f5, gain_5[:REDUCED], front_back5[:, :REDUCED], voxels_late
    )
    grad_front5 = jnp.concatenate([grad_f5, pool_back5], 4)
    grad_middle = jnp.einsum("nfhwo,oc->nfhwc", grad_front5, front_5, preferred_element_type=F32)
    front_grad_5 = jnp.einsum("nfhwo,nfhwc->oc", grad_front5, middle, preferred_element_type=F32)
    wide_grad_5, narrow_grad_5 = kernel_rows(weight_grad(inner5, grad_c5, SAME), own_wide)

    up = jnp.broadcast_to(
        grad_middle[:, :, None, :, None, :, None, :] * 0.125,
        (n, frames // 2, 2, height // 2, 2, breadth // 2, 2, c_in),
    ).reshape(n, frames, height, breadth, c_in)
    dy_b4 = up[..., B0:] * silu_slope(y_b4)
    back_b4 = tower_sum(cross(dy_b4, scaled_b4))
    grad_b4 = norm_back(dy_b4, scaled_b4, spread_b4, gain_4[REDUCED:], back_b4, voxels)
    grad_c4, grad_p4 = grad_b4[..., :OUTER], grad_b4[..., OUTER:]
    turned = flip(kernel_4)
    flat_pads = ((0, 0), (1, 1), (1, 1))
    to_before = conv(grad_c4[:, :1], turned[2:], flat_pads).astype(BF)
    to_after = conv(grad_c4[:, -1:], turned[:1], flat_pads).astype(BF)
    ahead = [(i, i + 1) for i in range(count - 1)]
    back = [(i + 1, i) for i in range(count - 1)]
    from_after = lax.ppermute(to_before, "blk", back)
    from_before = lax.ppermute(to_after, "blk", ahead)
    before, after = frame_halo(grad_p4)
    pool_back4 = pool_rows(jnp.concatenate([before, grad_p4, after], 1)).astype(BF)
    inner_grad = conv(grad_c4, turned, SAME)
    inner_grad = inner_grad.at[:, :1].add(from_before.astype(F32))
    inner_grad = inner_grad.at[:, -1:].add(from_after.astype(F32))
    wide_grad_4, narrow_grad_4 = kernel_rows(weight_grad(inner_pad, grad_c4, flat_pads), B1)
    dy_f4 = jnp.concatenate([up[..., :B0], inner_grad], 4) * silu_slope(
        scaled_f4 * gain_4[:REDUCED] + shift_4[:REDUCED]
    )
    back_f4 = tower_sum(cross(dy_f4, scaled_f4))
    norms_4 = jnp.concatenate([back_f4, back_b4], axis=1)
    grad_f4 = norm_back(dy_f4, scaled_f4, spread_f4, gain_4[:REDUCED], back_f4, voxels)
    grad_front4 = jnp.concatenate([grad_f4, pool_back4], 4)
    clips_grad = jnp.einsum("nfhwo,oc->nfhwc", grad_front4, front_4, preferred_element_type=F32)
    front_grad_4 = jnp.einsum("nfhwo,nfhwc->oc", grad_front4, clips, preferred_element_type=F32)

    feat_c = jax.nn.silu(y_c5).astype(BF)
    got = by_place(exchange_blk([feat_c[:, j : j + 1] for j in range(count)]))
    features = jnp.concatenate(
        [act5[..., :B0]]
        + [g[..., :own_wide].astype(F32) for g in got]
        + [g[..., own_wide:].astype(F32) for g in got]
        + [jax.nn.silu(y_p5)],
        axis=4,
    )

    def split_front(grad, c):
        entry = grad[:REDUCED].reshape(count, -1, c)
        pool = grad[REDUCED:].reshape(count, -1, c)
        return jnp.concatenate([entry, pool], axis=1)

    def flat(value):
        return value.reshape(2, -1)

    e = REDUCED // count
    sum_wide_5 = reduce_own(wide_grad_5)
    sum_narrow_5 = reduce_own(narrow_grad_5)
    sum_front_5 = reduce_blk(split_front(front_grad_5, c_in))
    sum_wide_4 = reduce_blk(wide_grad_4.reshape(count, own_wide, -1))
    sum_narrow_4 = reduce_blk(narrow_grad_4.reshape(count, own_narrow, -1))
    sum_front_4 = reduce_blk(split_front(front_grad_4, c_first))

    norms = jnp.stack([norms_4, norms_5])
    theirs = other_tower(norms)
    norms = jnp.where(stream == 0, jnp.stack([norms, theirs]), jnp.stack([theirs, norms]))
    extent = norms.shape[-1] // count
    norms = lax.dynamic_slice_in_dim(norms, place * extent, extent, 3)
    return (
        features,
        clips_grad,
        flat(sum_front_4[:, :e]),
        flat(sum_wide_4),
        flat(sum_narrow_4),
        flat(sum_front_4[:, e:]),
        norms[:, 0, 1],
        norms[:, 0, 0],
        flat(sum_front_5[:, :e]),
        flat(sum_wide_5),
        flat(sum_narrow_5),
        flat(sum_front_5[:, e:]),
        norms[:, 1, 1],
        norms[:, 1, 0],
    )


def solution(mesh):
    spec = P("dp", "blk", None, None, None)
    flat = P(None, "blk")
    return jax.shard_map(
        on_device,
        mesh=mesh,
        in_specs=(spec, spec) + (flat,) * 12,
        out_specs=(spec, spec) + (flat,) * 12,
        check_vma=False,
    )
```

```python
import functools

import jax
import jax.numpy as jnp
from jax import lax
from jax.experimental import pallas as pl
from jax.experimental.pallas import tpu as pltpu
from jax.sharding import PartitionSpec as P

B0 = 256
B1R = 160
B1 = 320
B2R = 32
B2 = 128
BP = 128
INNER = B1R + B2R
REDUCED = B0 + INNER
OUTER = B1 + B2
LAYER = B0 + OUTER + BP
EPS = 1e-05
BF = jnp.bfloat16
F32 = jnp.float32
TAPS = 27
NARROW_AT = 896
POOL_LANE = 64

NT = (((1,), (1,)), ((), ()))
NN = (((1,), (0,)), ((), ()))
VMEM = pl.BlockSpec(memory_space=pltpu.VMEM)
SMEM = pl.BlockSpec(memory_space=pltpu.SMEM)


def mm(a, b, dims=NN):
    return lax.dot_general(a, b, dims, preferred_element_type=F32)


def shape_of(shape, kind=F32):
    return jax.ShapeDtypeStruct(shape, kind)


def call(body, outs, *args, micros=2, scratch=()):
    specs = [SMEM if a.dtype == jnp.int32 else VMEM for a in args]
    return pl.pallas_call(
        body,
        out_shape=outs,
        in_specs=specs,
        out_specs=jax.tree.map(lambda _: VMEM, outs),
        scratch_shapes=list(scratch),
        compiler_params=pltpu.CompilerParams(vmem_limit_bytes=48 << 20),
        cost_estimate=pl.CostEstimate(
            flops=int(micros * 1.0e9), bytes_accessed=1 << 20, transcendentals=0
        ),
    )(*args)


def iota(shape, axis):
    return lax.broadcasted_iota(jnp.int32, shape, axis)


def ones_where(ok, value=1.0):
    return jnp.where(ok, value, 0.0).astype(BF)


def pool_matrix(n, side):
    r, c = iota((n, n), 0), iota((n, n), 1)
    area = side * side
    near_w = jnp.abs(r % side - c % side) <= 1
    near_h = jnp.abs((r // side) % side - (c // side) % side) <= 1
    return ones_where((r // area == c // area) & near_w & near_h)


def two_matrix(transposed):
    shape = (256, 64) if transposed else (64, 256)
    big, small = (iota(shape, 0), iota(shape, 1)) if transposed else (iota(shape, 1), iota(shape, 0))
    ok = (small // 16 == big // 64) & ((small // 4) % 4 == (big // 16) % 4)
    return ones_where(ok & (small % 4 == (big // 2) % 4), 0.125)


def exact(matrix, values):
    high = values.astype(BF)
    low = (values - high.astype(F32)).astype(BF)
    return mm(matrix, high) + mm(matrix, low)


def own_columns(place, transposed=False):
    shape = (256, LAYER) if transposed else (LAYER, 256)
    lane, col = (iota(shape, 0), iota(shape, 1)) if transposed else (iota(shape, 1), iota(shape, 0))
    wide = (lane < 80) & (col == B0 + 80 * place + lane)
    narrow = (lane >= 80) & (lane < 112) & (col == B0 + B1 + 32 * place + lane - 80)
    at = lane - 128 - POOL_LANE
    pool = (at >= 0) & (at < 32) & (col == B0 + OUTER + 32 * place + at)
    return ones_where(wide | narrow | pool)


def scaled_of(values, sums, voxels):
    centre = sums[0:1] * (1.0 / voxels)
    spread = lax.rsqrt(sums[1:2] * (1.0 / voxels) - centre * centre + EPS)
    return (values - centre) * spread, spread


def normed(values, sums, norms, voxels):
    scaled, _ = scaled_of(values, sums, voxels)
    return scaled, scaled * norms[0:1] + norms[1:2]


def silu(y):
    return y * lax.logistic(y)


def slope(y):
    sigmoid = lax.logistic(y)
    return sigmoid * (1.0 + y * (1.0 - sigmoid))


def norm_back(dy, values, sums, norms, back, voxels):
    scaled, spread = scaled_of(values, sums, voxels)
    scale = norms[0:1] * spread
    return scale * (dy - back[0:1] * (1.0 / voxels) - scaled * (back[1:2] * (1.0 / voxels)))


def add_pair(ref, lanes, first, second):
    ref[0:1, lanes] += jnp.sum(first, 0, keepdims=True)
    ref[1:2, lanes] += jnp.sum(second, 0, keepdims=True)


def shifted(a, side, j, k):
    if j == 0 and k == 0:
        return a
    rows, lanes = a.shape
    area = side * side
    r = iota((area, lanes), 0)
    w, h = r % side + k, r // side + j
    ok = (w >= 0) & (w < side) & (h >= 0) & (h < side)
    moved = pltpu.roll(a, (-(side * j + k)) % rows, 0).reshape(rows // area, area, lanes)
    return jnp.where(ok[None], moved, 0.0).reshape(rows, lanes)


def kernels_body(w_ref, fwd_ref, bwd_ref):
    places, cols = w_ref.shape[0], fwd_ref.shape[2]
    for t in range(TAPS):
        wide, narrow = [], []
        for z in range(places):
            wide.append(w_ref[z, 0:80, B1R * t : B1R * (t + 1)].astype(F32))
            for lane in (B2R * t, NARROW_AT + B2R * t):
                narrow.append(w_ref[z, 80:96, lane : lane + B2R].astype(F32))
        wide = jnp.concatenate(wide, 0)
        narrow = jnp.concatenate(narrow, 0)
        top = jnp.concatenate([wide, jnp.zeros((wide.shape[0], B2R), F32)], 1)
        low = jnp.concatenate([jnp.zeros((narrow.shape[0], B1R), F32), narrow], 1)
        rows = [top, low]
        if cols > top.shape[0] + low.shape[0]:
            rows.append(jnp.zeros((cols - top.shape[0] - low.shape[0], INNER), F32))
        block = jnp.concatenate(rows, 0)
        bwd_ref[TAPS - 1 - t] = block.astype(BF)
        fwd_ref[t] = block.T.astype(BF)


def front4_body(x_ref, w_ref, z_ref, pp_ref, m_ref):
    m_ref[...] = jnp.zeros_like(m_ref)
    for f in range(2):
        for h in range(2):
            x = x_ref[4 * h : 4 * h + 4, f].reshape(256, x_ref.shape[3])
            z = mm(x, w_ref[...], NT)
            rows = slice(256 * h, 256 * h + 256)
            z_ref[f, rows, :] = z
            pp_ref[f, rows, :] = z[:, :BP].astype(BF)
            front = z[:, BP:]
            add_pair(m_ref, slice(None), front, front * front)


def act4_body(z_ref, s_ref, n_ref, a_ref, *, voxels):
    sums, norms = s_ref[:, B0:], n_ref[:, B0:]
    for f in range(2):
        for h in range(2):
            rows = slice(256 * h, 256 * h + 256)
            _, y = normed(z_ref[f, rows, BP + B0 :], sums, norms, voxels)
            a_ref[f, rows, :] = silu(y).astype(BF)


def pool4_body(pp_ref, before_ref, after_ref, pool_ref, m_ref):
    matrix = pool_matrix(256, 8)
    m_ref[...] = jnp.zeros_like(m_ref)
    for f in range(2):
        for h in range(2):
            rows = slice(256 * h, 256 * h + 256)
            rim = before_ref if f == 0 else after_ref
            v = pp_ref[0, rows, :].astype(F32) + pp_ref[1, rows, :].astype(F32)
            v = (v + rim[rows, :].astype(F32)).astype(BF)
            out = mm(matrix, v) * (1.0 / 27.0)
            pool_ref[f, rows, :] = out
            add_pair(m_ref, slice(None), out, out * out)


def moments_body(c_ref, p_ref, m_ref):
    m_ref[:, 0:BP] = p_ref[...]
    m_ref[:, BP:] = jnp.zeros((2, OUTER), F32)
    for f in range(2):
        for h in range(2):
            c = c_ref[f, 256 * h : 256 * h + 256, :]
            add_pair(m_ref, slice(BP, None), c, c * c)


def norm4_body(z_ref, c_ref, p_ref, sf_ref, sb_ref, nf_ref, nb_ref, w_ref, mid_ref, z5_ref, m_ref, *, voxels):
    matrix = two_matrix(False)
    sf, sb, nf, nb = sf_ref[:, :B0], sb_ref[...], nf_ref[:, :B0], nb_ref[...]
    for h in range(2):
        rows, outs = slice(256 * h, 256 * h + 256), slice(64 * h, 64 * h + 64)
        pool = direct = conv = 0.0
        for f in range(2):
            pool += silu(normed(p_ref[f, rows, :], sb[:, :BP], nb[:, :BP], voxels)[1])
            direct += silu(normed(z_ref[f, rows, BP : BP + B0], sf, nf, voxels)[1])
            conv += silu(normed(c_ref[f, rows, :], sb[:, BP:], nb[:, BP:], voxels)[1])
        mid_ref[outs, :BP] = exact(matrix, pool).astype(BF)
        mid_ref[outs, BP : BP + B0] = exact(matrix, direct).astype(BF)
        mid_ref[outs, BP + B0 :] = exact(matrix, conv).astype(BF)
    z5 = mm(mid_ref[...], w_ref[...], NT)
    z5_ref[...] = z5
    m_ref[...] = jnp.zeros_like(m_ref)
    add_pair(m_ref, slice(None), z5[:, BP:], z5[:, BP:] * z5[:, BP:])


def act5_body(me_ref, z_ref, s_ref, n_ref, send_ref, *, voxels):
    _, y = normed(z_ref[:, BP + B0 :], s_ref[:, B0:], n_ref[:, B0:], voxels)
    base = jnp.concatenate([silu(y), jnp.zeros((y.shape[0], 64), F32)], 1)
    pre = z_ref[:, :BP].astype(BF)
    c, lane = iota((BP, 256), 0), iota((BP, 256), 1)
    at = lane - 128 - POOL_LANE
    for k in range(4):
        place = jnp.bitwise_xor(me_ref[0], k)
        pick = ones_where((at >= 0) & (at < 32) & (c == 32 * place + at))
        send_ref[k] = (base + mm(pre, pick)).astype(BF)


def join5_body(me_ref, r0, r1, r2, r3, a_ref, pool_ref, pre):
    pre[0] = jnp.zeros((128, 128), F32)
    pre[5] = jnp.zeros((128, 128), F32)
    for k, r in enumerate((r0, r1, r2, r3)):
        place = jnp.bitwise_xor(me_ref[0], k)
        a_ref[place] = r[:, :INNER]
        pre[place + 1] = r[:, 128:].astype(F32)
    matrix = pool_matrix(128, 4)
    lane = iota((128, 128), 1)
    ok = (lane >= POOL_LANE) & (lane < POOL_LANE + 32)
    for f in range(4):
        v = (pre[f] + pre[f + 1] + pre[f + 2]).astype(BF)
        pool_ref[f] = jnp.where(ok, mm(matrix, v) * (1.0 / 27.0), 0.0)


def moments5_body(c_ref, p_ref, m_ref):
    m_ref[...] = jnp.zeros_like(m_ref)
    for f in range(4):
        c, p = c_ref[f], p_ref[f]
        add_pair(m_ref, slice(0, 128), c, c * c)
        add_pair(m_ref, slice(128, 256), p, p * p)


def cot5_body(me_ref, cot_ref, out_ref):
    for k in range(4):
        pick = own_columns(jnp.bitwise_xor(me_ref[0], k))
        out_ref[k] = mm(cot_ref[...], pick).astype(BF)


def norm5_body(me_ref, c_ref, p_ref, s_ref, n_ref, g0, g1, g2, g3, feat_ref, dy_ref, x_ref, *, voxels):
    x_ref[...] = jnp.zeros_like(x_ref)
    for k, g in enumerate((g0, g1, g2, g3)):
        place = jnp.bitwise_xor(me_ref[0], k)
        for src, lanes in ((c_ref, slice(0, 128)), (p_ref, slice(128, 256))):
            scaled, y = normed(src[place], s_ref[:, lanes], n_ref[:, lanes], voxels)
            sigmoid = lax.logistic(y)
            feat_ref[k, :, lanes] = (y * sigmoid).astype(BF)
            dy = g[:, lanes].astype(F32) * (sigmoid * (1.0 + y * (1.0 - sigmoid)))
            dy_ref[place, :, lanes] = dy
            add_pair(x_ref, lanes, dy, dy * scaled)


def back5_body(c_ref, p_ref, s_ref, n_ref, dy_ref, b_ref, dv_ref, u_ref, *, voxels):
    matrix = pool_matrix(128, 4)
    parts = []
    for f in range(4):
        for src, lanes in ((c_ref, slice(0, 128)), (p_ref, slice(128, 256))):
            dv = norm_back(
                dy_ref[f, :, lanes], src[f], s_ref[:, lanes], n_ref[:, lanes], b_ref[:, lanes],
                voxels,
            )
            if src is c_ref:
                dv_ref[f] = dv.astype(BF)
            else:
                parts.append(dv.astype(BF).astype(F32))
    for f in range(4):
        v = sum(parts[max(f - 1, 0) : f + 2]).astype(BF)
        u_ref[f] = mm(matrix, v) * (1.0 / 27.0)


def send5_body(me_ref, part_ref, u_ref, send_ref):
    for k in range(4):
        place = jnp.bitwise_xor(me_ref[0], k)
        part = part_ref[place]
        send_ref[k, :, :128] = part[:, :128].astype(BF)
        tail = jnp.concatenate([part[:, 128:], jnp.zeros((128, 64), F32)], 1)
        send_ref[k, :, 128:] = (tail + u_ref[place]).astype(BF)


def front_back5_body(me_ref, r0, r1, r2, r3, z_ref, s_ref, n_ref, cot_ref, b_ref, dy_ref, u_ref, x_ref, *, voxels):
    x_ref[...] = jnp.zeros_like(x_ref)
    inner = 0.0
    u = 0.0
    c, lane = iota((128, BP), 0) - POOL_LANE, iota((128, BP), 1)
    for k, r in enumerate((r0, r1, r2, r3)):
        place = jnp.bitwise_xor(me_ref[0], k)
        inner = inner + r[:, :INNER].astype(F32)
        u = u + mm(r[:, 128:], ones_where((c >= 0) & (c < 32) & (lane == 32 * place + c)))
    u_ref[...] = u.astype(BF)
    for lanes, grad in ((slice(0, B0), cot_ref[...].astype(F32)), (slice(B0, REDUCED), inner)):
        at = slice(BP + lanes.start, BP + lanes.stop)
        scaled, y = normed(z_ref[:, at], s_ref[:, lanes], n_ref[:, lanes], voxels)
        dy = grad * slope(y)
        dy_ref[:, lanes] = dy
        add_pair(x_ref, lanes, dy, dy * scaled)
    first = jnp.where(me_ref[1] == 0, 1.0, 0.0)
    x_ref[:, pl.ds(pl.multiple_of(512 + 256 * me_ref[0], 128), 256)] = b_ref[...] * first


def mid_back_body(
    dy_ref, z_ref, s_ref, n_ref, b_ref, u_ref, w_ref, c_ref, p_ref, sb_ref, nb_ref,
    g_ref, gm_ref, x_ref, *, voxels,
):
    g_ref[:, :BP] = u_ref[...]
    g_ref[:, BP:] = norm_back(
        dy_ref[...], z_ref[:, BP:], s_ref[...], n_ref[...], b_ref[...], voxels / 8
    ).astype(BF)
    gm = mm(g_ref[...], w_ref[...])
    gm_ref[...] = gm
    matrix = two_matrix(True)
    x_ref[...] = jnp.zeros_like(x_ref)
    for h in range(2):
        rows = slice(256 * h, 256 * h + 256)
        block = gm[64 * h : 64 * h + 64]
        for src, lanes, at in (
            (p_ref, slice(0, BP), slice(0, BP)),
            (c_ref, slice(BP, BP + OUTER), slice(BP + B0, LAYER)),
        ):
            up = exact(matrix, block[:, at])
            for f in range(2):
                scaled, y = normed(src[f, rows, :], sb_ref[:, lanes], nb_ref[:, lanes], voxels)
                dy = up * slope(y)
                add_pair(x_ref, lanes, dy, dy * scaled)


def front_rows(total, out_ref):
    for z in range(4):
        out_ref[z, 0:112, :] = total[BP + 112 * z : BP + 112 * (z + 1)].astype(BF)
        out_ref[z, 112:144, :] = total[32 * z : 32 * (z + 1)].astype(BF)


def front_grad5_body(g_ref, mid_ref, out_ref):
    turned = g_ref[...].astype(F32).T.astype(BF)
    front_rows(mm(turned, mid_ref[...]), out_ref)


def branch_grad4_body(gm_ref, c_ref, p_ref, s_ref, n_ref, b_ref, dv_ref, dp_ref, *, voxels):
    matrix = two_matrix(True)
    for h in range(2):
        rows = slice(256 * h, 256 * h + 256)
        block = gm_ref[64 * h : 64 * h + 64, :]
        for src, dst, lanes, at in (
            (p_ref, dp_ref, slice(0, BP), slice(0, BP)),
            (c_ref, dv_ref, slice(BP, BP + OUTER), slice(BP + B0, LAYER)),
        ):
            up = exact(matrix, block[:, at])
            sums, norms, back = s_ref[:, lanes], n_ref[:, lanes], b_ref[:, lanes]
            for f in range(2):
                values = src[f, rows, :]
                _, y = normed(values, sums, norms, voxels)
                dv = norm_back(up * slope(y), values, sums, norms, back, voxels)
                dst[f, rows, :] = dv.astype(BF)


def put(out_ref, place, rows, lane, value):
    size = out_ref.shape[-1]
    done, width = 0, value.shape[1]
    while done < width:
        part, at = divmod(lane + done, size)
        step = min(width - done, size - at)
        out_ref[place, part, rows, at : at + step] = value[:, done : done + step].astype(BF)
        done += step


def taps_out(out_ref, t, grad, places):
    for z in range(places):
        put(out_ref, z, slice(0, 80), B1R * t, grad[80 * z : 80 * z + 80, :B1R])
        low = grad[80 * places + 32 * z : 80 * places + 32 * z + 32, B1R:INNER]
        put(out_ref, z, slice(80, 96), B2R * t, low[:16])
        put(out_ref, z, slice(80, 96), NARROW_AT + B2R * t, low[16:])


def wide_lanes(a):
    return jnp.concatenate([a.astype(F32), jnp.zeros((a.shape[0], 64), F32)], 1)


def kernel_grad4_body(a_ref, before_ref, after_ref, dv_ref, out_ref, patches, turned):
    out_ref[...] = jnp.zeros_like(out_ref)
    for q, a in enumerate((before_ref[...], a_ref[0], a_ref[1], after_ref[...])):
        a = wide_lanes(a)
        for n in range(9):
            patches[q, :, 256 * n : 256 * n + 256] = shifted(a, 8, n // 3 - 1, n % 3 - 1).astype(BF)
    for f in range(2):
        turned[:, 512 * f : 512 * f + 512] = dv_ref[f].astype(F32).T.astype(BF)
    for t in range(TAPS):
        i, n = t // 9, t % 9
        window = patches[i : i + 2, :, 256 * n : 256 * n + 256].reshape(1024, 256)
        taps_out(out_ref, t, mm(turned[...], window), 4)


def kernel_grad5_body(a_ref, dv_ref, out_ref, patches, turned):
    out_ref[...] = jnp.zeros_like(out_ref)
    for q in (0, 5):
        patches[q] = jnp.zeros(patches.shape[1:], BF)
    for q in range(4):
        a = wide_lanes(a_ref[q])
        for n in range(9):
            patches[q + 1, :, 256 * n : 256 * n + 256] = shifted(a, 4, n // 3 - 1, n % 3 - 1).astype(BF)
        turned[:, 128 * q : 128 * q + 128] = dv_ref[q].astype(F32).T.astype(BF)
    for t in range(TAPS):
        i, n = t // 9, t % 9
        window = patches[i : i + 4, :, 256 * n : 256 * n + 256].reshape(512, 256)
        taps_out(out_ref, t, mm(turned[...], window), 1)


def front_back4_body(
    gm_ref, z_ref, s_ref, n_ref, own_ref, before_ref, after_ref, dp_ref, dy_ref, u_ref, x_ref, *, voxels
):
    two, pool = two_matrix(True), pool_matrix(256, 8)
    x_ref[...] = jnp.zeros_like(x_ref)
    for h in range(2):
        rows = slice(256 * h, 256 * h + 256)
        up = exact(two, gm_ref[64 * h : 64 * h + 64, BP : BP + B0])
        for f in range(2):
            rim = before_ref if f == 0 else after_ref
            v = dp_ref[0, rows, :].astype(F32) + dp_ref[1, rows, :].astype(F32)
            v = (v + rim[rows, :BP].astype(F32)).astype(BF)
            u_ref[f, rows, :] = (mm(pool, v) * (1.0 / 27.0)).astype(BF)
            inner = own_ref[f, rows, :] + rim[rows, BP:].astype(F32)
            for lanes, grad in ((slice(0, B0), up), (slice(B0, REDUCED), inner)):
                at = slice(BP + lanes.start, BP + lanes.stop)
                scaled, y = normed(z_ref[f, rows, at], s_ref[:, lanes], n_ref[:, lanes], voxels)
                dy = grad * slope(y)
                dy_ref[f, rows, lanes] = dy
                add_pair(x_ref, lanes, dy, dy * scaled)


def front_grad4_body(z_ref, s_ref, n_ref, dy_ref, b_ref, u_ref, x_ref, g_ref, out_ref, *, voxels):
    total = 0.0
    for f in range(2):
        for h in range(2):
            rows = slice(256 * h, 256 * h + 256)
            g_ref[f, rows, :BP] = u_ref[f, rows, :]
            g_ref[f, rows, BP:] = norm_back(
                dy_ref[f, rows, :], z_ref[f, rows, BP:], s_ref[...], n_ref[...], b_ref[...], voxels
            ).astype(BF)
        turned = g_ref[f].astype(F32).T.astype(BF)
        total = total + mm(turned, x_ref[:, f].reshape(512, x_ref.shape[3]))
    front_rows(total, out_ref)


def clips_grad_body(g_ref, w_ref, out_ref):
    for f in range(2):
        for h in range(2):
            grad = mm(g_ref[f, 256 * h : 256 * h + 256, :], w_ref[...])
            out_ref[4 * h : 4 * h + 4, f] = grad.reshape(4, 64, out_ref.shape[3])


def features_body(me_ref, z_ref, s_ref, n_ref, r0, r1, r2, r3, out_ref, *, voxels):
    rest = 0.0
    for k, r in enumerate((r0, r1, r2, r3)):
        rest = rest + mm(r[...], own_columns(jnp.bitwise_xor(me_ref[0], k), True))
    _, y = normed(z_ref[:, BP : BP + B0], s_ref[:, :B0], n_ref[:, :B0], voxels)
    out_ref[:, :B0] = silu(y)
    out_ref[:, B0:] = rest[:, B0:]


def xor_pairs(axis, step):
    return [(i, i ^ step) for i in range(lax.axis_size(axis))]


def tower_steps():
    steps, step = [], 1
    while step < lax.axis_size("dp") // 2:
        steps.append(step)
        step *= 2
    return steps


def other_tower(value):
    return lax.ppermute(value, "dp", xor_pairs("dp", lax.axis_size("dp") // 2))


def blk_peers(value):
    count = lax.axis_size("blk")
    return [value] + [lax.ppermute(value, "blk", xor_pairs("blk", k)) for k in range(1, count)]


def by_place(parts):
    me, step = lax.axis_index("blk"), 1
    while step < len(parts):
        hit = (me & step) != 0
        parts = [jnp.where(hit, parts[k ^ step], parts[k]) for k in range(len(parts))]
        step *= 2
    return parts


def swap_blk(mine):
    return [mine[0]] + [
        lax.ppermute(mine[k], "blk", xor_pairs("blk", k)) for k in range(1, lax.axis_size("blk"))
    ]


def dp_sum(value):
    for step in tower_steps():
        value = value + lax.ppermute(value, "dp", xor_pairs("dp", step))
    return value


def blk_sum(value):
    parts = blk_peers(value)
    while len(parts) > 1:
        parts = [parts[i] + parts[i + 1] for i in range(0, len(parts), 2)]
    return parts[0]


def tower_sum(value):
    return blk_sum(dp_sum(value))


def gather_shared(shard):
    rows = shard.shape[0] // 2
    odd = lax.axis_index("dp") % 2
    half = lax.dynamic_slice_in_dim(shard, odd * rows, rows, 0)
    whole = jnp.stack(by_place(blk_peers(half)))
    twin = lax.ppermute(whole, "dp", xor_pairs("dp", 1))
    low = jnp.where(odd == 0, whole, twin)
    high = jnp.where(odd == 0, twin, whole)
    return jnp.concatenate([low, high], axis=1)


def rim_swap(first, last):
    count = lax.axis_size("blk")
    ahead = [(i, i + 1) for i in range(count - 1)]
    back = [(i + 1, i) for i in range(count - 1)]
    return lax.ppermute(last, "blk", ahead), lax.ppermute(first, "blk", back)


def reduce_rows(value, axis):
    halved = []
    for number, step in enumerate(tower_steps()):
        if number < 2:
            rows = value.shape[axis] // 2
            high = (lax.axis_index("dp") & step) != 0
            keep = lax.dynamic_slice_in_dim(value, jnp.where(high, rows, 0), rows, axis)
            give = lax.dynamic_slice_in_dim(value, jnp.where(high, 0, rows), rows, axis)
            halved.append(step)
        else:
            keep = give = value
        got = lax.ppermute(give, "dp", xor_pairs("dp", step))
        value = (keep.astype(F32) + got.astype(F32)).astype(BF)
    return value, halved


def reduce_blk(value):
    count = value.shape[0]
    got = swap_blk(by_place([value[j] for j in range(count)]))
    total = got[0].astype(F32)
    for piece in got[1:]:
        total = total + piece.astype(F32)
    return total.astype(BF)


def spread_rows(value, halved):
    stream = lax.axis_index("dp") // (lax.axis_size("dp") // 2)
    other = other_tower(value)
    both = jnp.where(stream == 0, jnp.stack([value, other]), jnp.stack([other, value]))
    for step in reversed(halved):
        got = lax.ppermute(both, "dp", xor_pairs("dp", step))
        high = (lax.axis_index("dp") & step) != 0
        both = jnp.where(
            high, jnp.concatenate([got, both], 1), jnp.concatenate([both, got], 1)
        )
    return both


def branch_rows(both):
    lanes = both.transpose(0, 2, 1, 3).reshape(2, 96, -1)
    wide = lanes[:, :80, : TAPS * B1R].astype(F32).reshape(2, -1)
    size = TAPS * B2R
    narrow = [lanes[:, 80:, :size], lanes[:, 80:, NARROW_AT : NARROW_AT + size]]
    return wide, jnp.concatenate(narrow, 1).astype(F32).reshape(2, -1)


def pick_row(param, stream):
    size = param.shape[1]
    return lax.dynamic_index_in_dim(param.reshape(2, size // 128, 128), stream, 0, keepdims=False)


def on_device(clips, cotangent, *params):
    groups = lax.axis_size("dp")
    count = lax.axis_size("blk")
    stream = lax.axis_index("dp") // (groups // 2)
    place = lax.axis_index("blk")
    me = jnp.stack([place, lax.axis_index("dp") % (groups // 2)]).astype(jnp.int32)
    own = [pick_row(p, stream) for p in params]
    early, late = own[:6], own[6:]
    n, frames, height, breadth, c_first = clips.shape
    voxels = groups // 2 * count * n * frames * height * breadth
    late_voxels = voxels // 8
    x = clips.reshape(n, frames, height * breadth, c_first)
    e, p = REDUCED // count, BP // count
    g = (REDUCED + OUTER + BP) // count

    def pack_front(layer, c):
        norms = jnp.concatenate([layer[4].reshape(-1), layer[5].reshape(-1)])
        row = jnp.pad(norms, (0, c - 2 * g)).reshape(1, c)
        rows = jnp.concatenate([layer[0].reshape(e, c), layer[3].reshape(p, c), row])
        return jnp.pad(rows, ((0, 160 - e - p - 1), (0, 0)))

    def unpack_front(whole):
        c = whole.shape[2]
        entry = whole[:, :e].reshape(REDUCED, c)
        pool = whole[:, e : e + p].reshape(BP, c)
        gain = whole[:, e + p, :g].reshape(-1)
        shift = whole[:, e + p, g : 2 * g].reshape(-1)
        norms = jnp.stack([gain, shift]).astype(F32)
        tail = norms[:, REDUCED + OUTER :]
        branch = jnp.concatenate([tail, norms[:, REDUCED : REDUCED + OUTER]], 1)
        return jnp.concatenate([pool, entry]), norms[:, :REDUCED], branch, norms

    def pack_branch(layer):
        wide = layer[1].reshape(80, -1)
        narrow = layer[2].reshape(32, -1)
        gap = jnp.zeros((16, NARROW_AT - narrow.shape[1]), BF)
        low = jnp.concatenate([narrow[:16], gap, narrow[16:]], 1)
        low = jnp.pad(low, ((0, 0), (0, wide.shape[1] - low.shape[1])))
        return jnp.concatenate([wide, low])

    def kernels(packed, cols):
        return call(
            kernels_body,
            (shape_of((TAPS, INNER, cols), BF), shape_of((TAPS, cols, INNER), BF)),
            packed,
            micros=6,
        )

    front_4, nf4, nb4, _ = unpack_front(gather_shared(pack_front(early, c_first)))
    fwd_4, bwd_4 = kernels(gather_shared(pack_branch(early)), OUTER)
    front_5, nf5, _, norms_5 = unpack_front(gather_shared(pack_front(late, LAYER)))
    front_5 = jnp.concatenate([front_5[:, LAYER - BP :], front_5[:, : LAYER - BP]], 1)
    fwd_5, bwd_5 = kernels(pack_branch(late)[None], 128)
    n5 = jnp.concatenate(
        [
            lax.dynamic_slice_in_dim(norms_5, REDUCED + place * 80, 80, 1),
            lax.dynamic_slice_in_dim(norms_5, REDUCED + B1 + place * 32, 32, 1),
            jnp.zeros((2, 16 + POOL_LANE), F32),
            lax.dynamic_slice_in_dim(norms_5, REDUCED + OUTER + place * 32, 32, 1),
            jnp.zeros((2, 96 - POOL_LANE), F32),
        ],
        axis=1,
    )
    cot = cotangent.reshape(128, LAYER)
    cot_mine = call(cot5_body, shape_of((4, 128, 256), BF), me, cot, micros=2)
    cots = swap_blk([cot_mine[k] for k in range(4)])

    def conv(values, kernel, pads):
        return lax.conv_general_dilated(
            values,
            kernel.reshape(3, 3, 3, *kernel.shape[1:]) if kernel.shape[0] == TAPS else kernel,
            (1, 1, 1),
            pads,
            dimension_numbers=("DNHWC", "DHWIO", "DNHWC"),
            preferred_element_type=F32,
        )

    flat_pads = ((0, 0), (1, 1), (1, 1))
    same = ((1, 1), (1, 1), (1, 1))
    at4 = functools.partial(functools.partial, voxels=voxels)
    at5 = functools.partial(functools.partial, voxels=late_voxels)

    z, pre, m = call(
        front4_body,
        (shape_of((2, 512, 576)), shape_of((2, 512, BP), BF), shape_of((2, REDUCED))),
        x, front_4, micros=4,
    )
    sf4 = tower_sum(m)
    pre_before, pre_after = rim_swap(pre[0], pre[1])
    pool, m_pool = call(
        pool4_body, (shape_of((2, 512, BP)), shape_of((2, BP))), pre, pre_before, pre_after, micros=2
    )
    a = call(at4(act4_body), shape_of((2, 512, INNER), BF), z, sf4, nf4, micros=2)
    before, after = rim_swap(a[0], a[1])
    a_pad = jnp.concatenate([before[None], a, after[None]]).reshape(4, n, height, breadth, INNER)
    c = conv(a_pad, fwd_4, flat_pads).reshape(2, 512, OUTER)
    sb4 = tower_sum(call(moments_body, shape_of((2, 576)), c, m_pool, micros=1))

    mid, z5, m = call(
        at4(norm4_body),
        (shape_of((128, LAYER), BF), shape_of((128, 576)), shape_of((2, REDUCED))),
        z, c, pool, sf4, sb4, nf4, nb4, front_5, micros=4,
    )
    sf5 = tower_sum(m)
    send = call(at5(act5_body), shape_of((4, 128, 256), BF), me, z5, sf5, nf5, micros=1)
    a5, pool5 = call(
        join5_body,
        (shape_of((4, 128, INNER), BF), shape_of((4, 128, 128))),
        me, *swap_blk([send[k] for k in range(4)]),
        micros=1, scratch=[pltpu.VMEM((6, 128, 128), F32)],
    )
    small = (4, n, height // 2, breadth // 2, -1)
    c5 = conv(a5.reshape(small), fwd_5, same).reshape(4, 128, 128)
    s5 = dp_sum(call(moments5_body, shape_of((2, 256)), c5, pool5, micros=1))
    feat, dy5, m = call(
        at5(norm5_body),
        (shape_of((4, 128, 256), BF), shape_of((4, 128, 256)), shape_of((2, 256))),
        me, c5, pool5, s5, n5, *cots, micros=1,
    )

    b5 = dp_sum(m)
    dv5, u5 = call(
        at5(back5_body),
        (shape_of((4, 128, 128), BF), shape_of((4, 128, 128))),
        c5, pool5, s5, n5, dy5, b5, micros=1,
    )
    part = conv(dv5.reshape(small), bwd_5, same).reshape(4, 128, INNER)
    send = call(send5_body, shape_of((4, 128, 256), BF), me, part, u5, micros=1)
    dyf5, u5, m = call(
        at5(front_back5_body),
        (shape_of((128, REDUCED)), shape_of((128, BP), BF), shape_of((2, 1536))),
        me, *swap_blk([send[k] for k in range(4)]), z5, sf5, nf5, cot[:, :B0], b5, micros=1,
    )
    back5 = tower_sum(m)
    bf5 = back5[:, :REDUCED]
    g5, gm, m = call(
        at4(mid_back_body),
        (shape_of((128, 576), BF), shape_of((128, LAYER)), shape_of((2, 576))),
        dyf5, z5, sf5, nf5, bf5, u5, front_5, c, pool, sb4, nb4, micros=4,
    )
    bb4 = tower_sum(m)

    dv, dp = call(
        at4(branch_grad4_body),
        (shape_of((2, 512, OUTER), BF), shape_of((2, 512, BP), BF)),
        gm, c, pool, sb4, nb4, bb4, micros=3,
    )
    image = (1, n, height, breadth, OUTER)
    turned = bwd_4.reshape(3, 3, 3, OUTER, INNER)
    rim_first = conv(dv[0].reshape(image), turned[2:], flat_pads).reshape(512, INNER)
    rim_last = conv(dv[1].reshape(image), turned[:1], flat_pads).reshape(512, INNER)
    got_before, got_after = rim_swap(
        jnp.concatenate([dp[0], rim_first.astype(BF)], 1),
        jnp.concatenate([dp[1], rim_last.astype(BF)], 1),
    )
    inner = conv(dv.reshape(2, n, height, breadth, OUTER), bwd_4, same).reshape(2, 512, INNER)
    dyf4, u4, m = call(
        at4(front_back4_body),
        (shape_of((2, 512, REDUCED)), shape_of((2, 512, BP), BF), shape_of((2, REDUCED))),
        gm, z, sf4, nf4, inner, got_before, got_after, dp, micros=4,
    )
    bf4 = tower_sum(m)
    g4, front_part4 = call(
        at4(front_grad4_body),
        (shape_of((2, 512, 576), BF), shape_of((4, 144, c_first), BF)),
        z, sf4, nf4, dyf4, bf4, u4, x, micros=4,
    )
    clips_grad = call(
        clips_grad_body, shape_of((n, frames, height * breadth, c_first)), g4, front_4, micros=3
    ).reshape(clips.shape)

    got = swap_blk([feat[k] for k in range(4)])
    features = call(
        at5(features_body), shape_of((128, LAYER)), me, z5, sf5, nf5, *got, micros=2
    ).reshape(cotangent.shape)

    front_part5 = call(front_grad5_body, shape_of((4, 144, LAYER), BF), g5, mid, micros=2)
    front_part5 = jnp.concatenate([front_part5[..., BP:], front_part5[..., :BP]], 2)
    branch_part5 = call(
        kernel_grad5_body,
        shape_of((1, 4, 96, 1152), BF),
        a5, dv5,
        micros=6,
        scratch=[pltpu.VMEM((6, 128, 2304), BF), pltpu.VMEM((128, 512), BF)],
    )[0]
    branch_part4 = call(
        kernel_grad4_body,
        shape_of((4, 4, 96, 1152), BF),
        a, before, after, dv,
        micros=10,
        scratch=[pltpu.VMEM((4, 512, 2304), BF), pltpu.VMEM((OUTER, 1024), BF)],
    )

    def front_sums(part):
        value, halved = reduce_rows(part, 1)
        both = spread_rows(reduce_blk(value), halved).astype(F32)
        return both[:, :e].reshape(2, -1), both[:, e:].reshape(2, -1)

    wide_5, narrow_5 = branch_rows(spread_rows(*reduce_rows(branch_part5, 0)))
    entry_5, poolproj_5 = front_sums(front_part5)
    value, halved = reduce_rows(branch_part4, 1)
    wide_4, narrow_4 = branch_rows(spread_rows(reduce_blk(value), halved))
    entry_4, poolproj_4 = front_sums(front_part4)

    all5 = back5[:, 512:].reshape(2, count, 256)
    norms4 = jnp.concatenate([bf4, bb4[:, BP:], bb4[:, :BP]], 1)
    norms5 = jnp.concatenate(
        [
            bf5,
            all5[:, :, :80].reshape(2, -1),
            all5[:, :, 80:112].reshape(2, -1),
            all5[:, :, 128 + POOL_LANE : 160 + POOL_LANE].reshape(2, -1),
        ],
        axis=1,
    )
    norms = jnp.stack([norms4, norms5])
    theirs = other_tower(norms)
    norms = jnp.where(stream == 0, jnp.stack([norms, theirs]), jnp.stack([theirs, norms]))
    norms = lax.dynamic_slice_in_dim(norms, place * g, g, 3)
    return (
        features, clips_grad,
        entry_4, wide_4, narrow_4, poolproj_4, norms[:, 0, 1], norms[:, 0, 0],
        entry_5, wide_5, narrow_5, poolproj_5, norms[:, 1, 1], norms[:, 1, 0],
    )


def solution(mesh):
    spec = P("dp", "blk", None, None, None)
    flat = P(None, "blk")
    return jax.shard_map(
        on_device,
        mesh=mesh,
        in_specs=(spec, spec) + (flat,) * 12,
        out_specs=(spec, spec) + (flat,) * 12,
        check_vma=False,
    )
```

```python
import functools

import jax
import jax.numpy as jnp
from jax import lax
from jax.experimental import pallas as pl
from jax.experimental.pallas import tpu as pltpu
from jax.sharding import PartitionSpec as P

B0 = 256
B1R = 160
B1 = 320
B2R = 32
B2 = 128
BP = 128
INNER = B1R + B2R
REDUCED = B0 + INNER
OUTER = B1 + B2
LAYER = B0 + OUTER + BP
EPS = 1e-05
BF = jnp.bfloat16
F32 = jnp.float32
TAPS = 27
NARROW_AT = 896
POOL_LANE = 64

NT = (((1,), (1,)), ((), ()))
NN = (((1,), (0,)), ((), ()))
VMEM = pl.BlockSpec(memory_space=pltpu.VMEM)
SMEM = pl.BlockSpec(memory_space=pltpu.SMEM)


def mm(a, b, dims=NN):
    return lax.dot_general(a, b, dims, preferred_element_type=F32)


def shape_of(shape, kind=F32):
    return jax.ShapeDtypeStruct(shape, kind)


def call(body, outs, *args, micros=2, scratch=(), mib=12, lazy=()):
    def whole(*refs):
        bufs, sems = refs[len(refs) - len(lazy) - 1 : -1], refs[-1]
        copies = [
            pltpu.make_async_copy(refs[i], bufs[n], sems.at[n]) for n, i in enumerate(lazy)
        ]
        for copy in copies:
            copy.start()
        for copy in copies:
            copy.wait()
        ins = list(refs[: len(args)])
        for n, i in enumerate(lazy):
            ins[i] = bufs[n]
        body(*ins, *refs[len(args) : len(refs) - len(lazy) - 1])

    lazy = [i % len(args) for i in lazy]
    specs = [SMEM if a.dtype == jnp.int32 else VMEM for a in args]
    scratch = list(scratch)
    for i in lazy:
        specs[i] = pl.BlockSpec(memory_space=pl.ANY)
        scratch.append(pltpu.VMEM(args[i].shape, args[i].dtype))
        mib += args[i].size * 4 // (1 << 20) + 1
    if lazy:
        scratch.append(pltpu.SemaphoreType.DMA((len(lazy),)))
    return pl.pallas_call(
        whole if lazy else body,
        out_shape=outs,
        in_specs=specs,
        out_specs=jax.tree.map(lambda _: VMEM, outs),
        scratch_shapes=scratch,
        compiler_params=pltpu.CompilerParams(vmem_limit_bytes=min(mib, 40) << 20),
        cost_estimate=pl.CostEstimate(
            flops=int(micros * 1.0e9), bytes_accessed=1 << 20, transcendentals=0
        ),
    )(*args)


def iota(shape, axis):
    return lax.broadcasted_iota(jnp.int32, shape, axis)


def ones_where(ok, value=1.0):
    return jnp.where(ok, value, 0.0).astype(BF)


def pool_matrix(n, side):
    r, c = iota((n, n), 0), iota((n, n), 1)
    area = side * side
    near_w = jnp.abs(r % side - c % side) <= 1
    near_h = jnp.abs((r // side) % side - (c // side) % side) <= 1
    return ones_where((r // area == c // area) & near_w & near_h)


def turn_matrix(n, area):
    r, c = iota((n, n), 0), iota((n, n), 1)
    return ones_where((r // area == c // area) & (r % area + c % area == area - 1))


def two_matrix(transposed):
    shape = (256, 64) if transposed else (64, 256)
    big, small = (iota(shape, 0), iota(shape, 1)) if transposed else (iota(shape, 1), iota(shape, 0))
    ok = (small // 16 == big // 64) & ((small // 4) % 4 == (big // 16) % 4)
    return ones_where(ok & (small % 4 == (big // 2) % 4), 0.125)


def exact(matrix, values):
    high = values.astype(BF)
    low = (values - high.astype(F32)).astype(BF)
    return mm(matrix, high) + mm(matrix, low)


def own_columns(place, transposed=False):
    shape = (256, LAYER) if transposed else (LAYER, 256)
    lane, col = (iota(shape, 0), iota(shape, 1)) if transposed else (iota(shape, 1), iota(shape, 0))
    wide = (lane < 80) & (col == B0 + 80 * place + lane)
    narrow = (lane >= 80) & (lane < 112) & (col == B0 + B1 + 32 * place + lane - 80)
    at = lane - 128 - POOL_LANE
    pool = (at >= 0) & (at < 32) & (col == B0 + OUTER + 32 * place + at)
    return ones_where(wide | narrow | pool)


def scaled_of(values, sums, voxels):
    centre = sums[0:1] * (1.0 / voxels)
    spread = lax.rsqrt(sums[1:2] * (1.0 / voxels) - centre * centre + EPS)
    return (values - centre) * spread, spread


def normed(values, sums, norms, voxels):
    scaled, _ = scaled_of(values, sums, voxels)
    return scaled, scaled * norms[0:1] + norms[1:2]


def silu(y):
    return y * lax.logistic(y)


def slope(y):
    sigmoid = lax.logistic(y)
    return sigmoid * (1.0 + y * (1.0 - sigmoid))


def norm_back(dy, values, sums, norms, back, voxels):
    scaled, spread = scaled_of(values, sums, voxels)
    scale = norms[0:1] * spread
    return scale * (dy - back[0:1] * (1.0 / voxels) - scaled * (back[1:2] * (1.0 / voxels)))


def add_pair(ref, lanes, first, second):
    ref[0:1, lanes] += jnp.sum(first, 0, keepdims=True)
    ref[1:2, lanes] += jnp.sum(second, 0, keepdims=True)


def shifted(a, side, j, k):
    if j == 0 and k == 0:
        return a
    rows, lanes = a.shape
    area = side * side
    r = iota((area, lanes), 0)
    w, h = r % side + k, r // side + j
    ok = (w >= 0) & (w < side) & (h >= 0) & (h < side)
    moved = pltpu.roll(a, (-(side * j + k)) % rows, 0).reshape(rows // area, area, lanes)
    return jnp.where(ok[None], moved, 0.0).reshape(rows, lanes)


def assemble(me_ref, pieces, buf):
    half = pieces[0].shape[0] // 2
    buf[me_ref[0]] = pieces[0][...]
    for k in range(1, 4):
        place = jnp.bitwise_xor(me_ref[0], k)
        buf[place, pl.ds(pl.multiple_of(half * me_ref[2], half), half), :] = pieces[k][...]
        buf[place, pl.ds(pl.multiple_of(half * (1 - me_ref[2]), half), half), :] = pieces[k + 3][...]


def tap_block(shards, t):
    wide, narrow = [], []
    for w in shards:
        wide.append(w[0:80, B1R * t : B1R * (t + 1)].astype(F32))
        for lane in (B2R * t, NARROW_AT + B2R * t):
            narrow.append(w[80:96, lane : lane + B2R].astype(F32))
    wide = jnp.concatenate(wide, 0)
    narrow = jnp.concatenate(narrow, 0)
    top = jnp.concatenate([wide, jnp.zeros((wide.shape[0], B2R), F32)], 1)
    low = jnp.concatenate([jnp.zeros((narrow.shape[0], B1R), F32), narrow], 1)
    return jnp.concatenate([top, low], 0).astype(BF)


def kernels4_body(me_ref, mine_ref, twin_ref, all_ref, first_ref, last_ref, buf):
    buf[:, pl.ds(pl.multiple_of(48 * me_ref[2], 16), 48), :] = mine_ref[...]
    buf[:, pl.ds(pl.multiple_of(48 * (1 - me_ref[2]), 16), 48), :] = twin_ref[...]
    for t in range(TAPS):
        block = tap_block([buf.at[z] for z in range(4)], t)
        all_ref[t] = block
        if t < 9:
            first_ref[t] = block
        if t >= 18:
            last_ref[t - 18] = block


def kernels5_body(w_ref, all_ref):
    for t in range(TAPS):
        all_ref[t] = jnp.concatenate([tap_block([w_ref], t), jnp.zeros((16, INNER), BF)], 0)


def front_parts(buf, matrix_ref, norms_ref):
    for z in range(4):
        matrix_ref[32 * z : 32 * (z + 1), :] = buf[z, 112:144, :]
        matrix_ref[BP + 112 * z : BP + 112 * (z + 1), :] = buf[z, 0:112, :]
        row = buf[z, 144:160, :].astype(F32)[0:1]
        norms_ref[0:1, 256 * z : 256 * (z + 1)] = row[:, :256]
        norms_ref[1:2, 256 * z : 256 * (z + 1)] = row[:, 256:512]


def total_of(parts):
    return (parts[0][...] + parts[1][...]) + (parts[2][...] + parts[3][...])


def front5_body(me_ref, p0, p1, p2, p3, t1, t2, t3, w_ref, n_ref, own_ref, buf):
    assemble(me_ref, (p0, p1, p2, p3, t1, t2, t3), buf)
    front_parts(buf, w_ref, n_ref)
    norms = n_ref[...]
    own = jnp.zeros((2, 256), F32)
    gap = jnp.zeros((2, 16 + POOL_LANE), F32)
    for z in range(4):
        wide = norms[:, REDUCED + 80 * z : REDUCED + 80 * (z + 1)]
        narrow = norms[:, REDUCED + B1 + 32 * z : REDUCED + B1 + 32 * (z + 1)]
        pool = norms[:, REDUCED + OUTER + 32 * z : REDUCED + OUTER + 32 * (z + 1)]
        block = jnp.concatenate([wide, narrow, gap, pool, jnp.zeros((2, 32), F32)], 1)
        own = jnp.where(me_ref[0] == z, block, own)
    own_ref[...] = own


def front4_body(me_ref, x_ref, p0, p1, p2, p3, t1, t2, t3, z_ref, pp_ref, m_ref, w_ref, nf_ref, nb_ref, buf, n_ref):
    assemble(me_ref, (p0, p1, p2, p3, t1, t2, t3), buf)
    front_parts(buf, w_ref, n_ref)
    nf_ref[...] = n_ref[:, :REDUCED]
    nb_ref[:, :BP] = n_ref[:, REDUCED + OUTER :]
    nb_ref[:, BP:] = n_ref[:, REDUCED : REDUCED + OUTER]
    m_ref[...] = jnp.zeros_like(m_ref)
    for f in range(2):
        for h in range(2):
            x = x_ref[4 * h : 4 * h + 4, f].reshape(256, x_ref.shape[3])
            z = mm(x, w_ref[...], NT)
            rows = slice(256 * h, 256 * h + 256)
            z_ref[f, rows, :] = z
            pp_ref[f, rows, :] = z[:, :BP].astype(BF)
            front = z[:, BP:]
            add_pair(m_ref, slice(None), front, front * front)


def act4_body(z_ref, s0, s1, s2, s3, n_ref, a_ref, s_ref, *, voxels):
    s_ref[...] = total_of((s0, s1, s2, s3))
    sums, norms = s_ref[:, B0:], n_ref[:, B0:]
    for f in range(2):
        for h in range(2):
            rows = slice(256 * h, 256 * h + 256)
            _, y = normed(z_ref[f, rows, BP + B0 :], sums, norms, voxels)
            a_ref[f, rows, :] = silu(y).astype(BF)


def pool4_body(pp_ref, before_ref, after_ref, pool_ref, m_ref):
    matrix = pool_matrix(256, 8)
    m_ref[...] = jnp.zeros_like(m_ref)
    for f in range(2):
        for h in range(2):
            rows = slice(256 * h, 256 * h + 256)
            rim = before_ref if f == 0 else after_ref
            v = pp_ref[0, rows, :].astype(F32) + pp_ref[1, rows, :].astype(F32)
            v = (v + rim[rows, :].astype(F32)).astype(BF)
            out = mm(matrix, v) * (1.0 / 27.0)
            pool_ref[f, rows, :] = out
            add_pair(m_ref, slice(None), out, out * out)


def moments_body(c_ref, p_ref, m_ref):
    m_ref[:, 0:BP] = p_ref[...]
    m_ref[:, BP:] = jnp.zeros((2, OUTER), F32)
    for f in range(2):
        for h in range(2):
            c = c_ref[f, 256 * h : 256 * h + 256, :]
            add_pair(m_ref, slice(BP, None), c, c * c)


def norm4_body(
    z_ref, c_ref, p_ref, sf_ref, s0, s1, s2, s3, nf_ref, nb_ref, w_ref, mid_ref, z5_ref, m_ref, sb_ref, *, voxels
):
    sb_ref[...] = total_of((s0, s1, s2, s3))
    matrix = two_matrix(False)
    sf, sb, nf, nb = sf_ref[:, :B0], sb_ref[...], nf_ref[:, :B0], nb_ref[...]
    for h in range(2):
        rows, outs = slice(256 * h, 256 * h + 256), slice(64 * h, 64 * h + 64)
        pool = direct = conv = 0.0
        for f in range(2):
            pool += silu(normed(p_ref[f, rows, :], sb[:, :BP], nb[:, :BP], voxels)[1])
            direct += silu(normed(z_ref[f, rows, BP : BP + B0], sf, nf, voxels)[1])
            conv += silu(normed(c_ref[f, rows, :], sb[:, BP:], nb[:, BP:], voxels)[1])
        mid_ref[outs, :BP] = exact(matrix, pool).astype(BF)
        mid_ref[outs, BP : BP + B0] = exact(matrix, direct).astype(BF)
        mid_ref[outs, BP + B0 :] = exact(matrix, conv).astype(BF)
    z5 = mm(mid_ref[...], w_ref[...], NT)
    z5_ref[...] = z5
    m_ref[...] = jnp.zeros_like(m_ref)
    add_pair(m_ref, slice(None), z5[:, BP:], z5[:, BP:] * z5[:, BP:])


def act5_body(me_ref, z_ref, s0, s1, s2, s3, n_ref, send_ref, s_ref, *, voxels):
    s_ref[...] = total_of((s0, s1, s2, s3))
    _, y = normed(z_ref[:, BP + B0 :], s_ref[:, B0:], n_ref[:, B0:REDUCED], voxels)
    base = jnp.concatenate([silu(y), jnp.zeros((y.shape[0], 64), F32)], 1)
    pre = z_ref[:, :BP].astype(BF)
    c, lane = iota((BP, 256), 0), iota((BP, 256), 1)
    at = lane - 128 - POOL_LANE
    for k in range(4):
        place = jnp.bitwise_xor(me_ref[0], k)
        pick = ones_where((at >= 0) & (at < 32) & (c == 32 * place + at))
        send_ref[k] = (base + mm(pre, pick)).astype(BF)


def join5_body(me_ref, r0, r1, r2, r3, a_ref, pool_ref, pre):
    pre[0] = jnp.zeros((128, 128), F32)
    pre[5] = jnp.zeros((128, 128), F32)
    for k, r in enumerate((r0, r1, r2, r3)):
        place = jnp.bitwise_xor(me_ref[0], k)
        a_ref[place] = r[:, :INNER]
        pre[place + 1] = r[:, 128:].astype(F32)
    matrix = pool_matrix(128, 4)
    lane = iota((128, 128), 1)
    ok = (lane >= POOL_LANE) & (lane < POOL_LANE + 32)
    for f in range(4):
        v = (pre[f] + pre[f + 1] + pre[f + 2]).astype(BF)
        pool_ref[f] = jnp.where(ok, mm(matrix, v) * (1.0 / 27.0), 0.0)


def moments5_body(c_ref, p_ref, m_ref):
    m_ref[...] = jnp.zeros_like(m_ref)
    for f in range(4):
        c, p = c_ref[f], p_ref[f]
        add_pair(m_ref, slice(0, 128), c, c * c)
        add_pair(m_ref, slice(128, 256), p, p * p)


def cot5_body(me_ref, cot_ref, out_ref):
    for k in range(4):
        pick = own_columns(jnp.bitwise_xor(me_ref[0], k))
        out_ref[k] = mm(cot_ref[...], pick).astype(BF)


def norm5_body(me_ref, c_ref, p_ref, s_ref, n_ref, g0, g1, g2, g3, feat_ref, dy_ref, x_ref, *, voxels):
    x_ref[...] = jnp.zeros_like(x_ref)
    for k, g in enumerate((g0, g1, g2, g3)):
        place = jnp.bitwise_xor(me_ref[0], k)
        for src, lanes in ((c_ref, slice(0, 128)), (p_ref, slice(128, 256))):
            scaled, y = normed(src[place], s_ref[:, lanes], n_ref[:, lanes], voxels)
            sigmoid = lax.logistic(y)
            feat_ref[k, :, lanes] = (y * sigmoid).astype(BF)
            dy = g[:, lanes].astype(F32) * (sigmoid * (1.0 + y * (1.0 - sigmoid)))
            dy_ref[place, :, lanes] = dy
            add_pair(x_ref, lanes, dy, dy * scaled)


def back5_body(c_ref, p_ref, s_ref, n_ref, dy_ref, b_ref, dv_ref, turned_ref, u_ref, *, voxels):
    matrix, turn = pool_matrix(128, 4), turn_matrix(128, 16)
    parts = []
    for f in range(4):
        for src, lanes in ((c_ref, slice(0, 128)), (p_ref, slice(128, 256))):
            dv = norm_back(
                dy_ref[f, :, lanes], src[f], s_ref[:, lanes], n_ref[:, lanes], b_ref[:, lanes],
                voxels,
            )
            if src is c_ref:
                dv_ref[f] = dv.astype(BF)
                turned_ref[3 - f] = mm(turn, dv.astype(BF)).astype(BF)
            else:
                parts.append(dv.astype(BF).astype(F32))
    for f in range(4):
        v = sum(parts[max(f - 1, 0) : f + 2]).astype(BF)
        u_ref[f] = mm(matrix, v) * (1.0 / 27.0)


def send5_body(me_ref, part_ref, u_ref, send_ref):
    turn = turn_matrix(128, 16)
    for k in range(4):
        place = jnp.bitwise_xor(me_ref[0], k)
        part = mm(turn, part_ref[3 - place].astype(BF))
        send_ref[k, :, :128] = part[:, :128].astype(BF)
        tail = jnp.concatenate([part[:, 128:], jnp.zeros((128, 64), F32)], 1)
        send_ref[k, :, 128:] = (tail + u_ref[place]).astype(BF)


def front_back5_body(me_ref, r0, r1, r2, r3, z_ref, s_ref, n_ref, cot_ref, b_ref, dy_ref, u_ref, x_ref, *, voxels):
    x_ref[...] = jnp.zeros_like(x_ref)
    inner = 0.0
    u = 0.0
    c, lane = iota((128, BP), 0) - POOL_LANE, iota((128, BP), 1)
    for k, r in enumerate((r0, r1, r2, r3)):
        place = jnp.bitwise_xor(me_ref[0], k)
        inner = inner + r[:, :INNER].astype(F32)
        u = u + mm(r[:, 128:], ones_where((c >= 0) & (c < 32) & (lane == 32 * place + c)))
    u_ref[...] = u.astype(BF)
    for lanes, grad in ((slice(0, B0), cot_ref[...].astype(F32)), (slice(B0, REDUCED), inner)):
        at = slice(BP + lanes.start, BP + lanes.stop)
        scaled, y = normed(z_ref[:, at], s_ref[:, lanes], n_ref[:, lanes], voxels)
        dy = grad * slope(y)
        dy_ref[:, lanes] = dy
        add_pair(x_ref, lanes, dy, dy * scaled)
    first = jnp.where(me_ref[1] == 0, 1.0, 0.0)
    x_ref[:, pl.ds(pl.multiple_of(512 + 256 * me_ref[0], 128), 256)] = b_ref[...] * first


def mid_back_body(
    dy_ref, z_ref, s_ref, n_ref, b0, b1, b2, b3, u_ref, w_ref, c_ref, p_ref, sb_ref, nb_ref,
    g_ref, gm_ref, x_ref, back_ref, *, voxels,
):
    back_ref[...] = total_of((b0, b1, b2, b3))
    g_ref[:, :BP] = u_ref[...]
    g_ref[:, BP:] = norm_back(
        dy_ref[...], z_ref[:, BP:], s_ref[...], n_ref[:, :REDUCED], back_ref[:, :REDUCED], voxels / 8
    ).astype(BF)
    gm = mm(g_ref[...], w_ref[...])
    gm_ref[...] = gm
    matrix = two_matrix(True)
    x_ref[...] = jnp.zeros_like(x_ref)
    for h in range(2):
        rows = slice(256 * h, 256 * h + 256)
        block = gm[64 * h : 64 * h + 64]
        for src, lanes, at in (
            (p_ref, slice(0, BP), slice(0, BP)),
            (c_ref, slice(BP, BP + OUTER), slice(BP + B0, LAYER)),
        ):
            up = exact(matrix, block[:, at])
            for f in range(2):
                scaled, y = normed(src[f, rows, :], sb_ref[:, lanes], nb_ref[:, lanes], voxels)
                dy = up * slope(y)
                add_pair(x_ref, lanes, dy, dy * scaled)


def front_rows(total, out_ref):
    gap = jnp.zeros((4, total.shape[1]), F32)
    for z in range(4):
        for q in range(4):
            entry, pool = BP + 112 * z + 28 * q, 32 * z + 8 * q
            block = [total[entry : entry + 28], gap, total[pool : pool + 8]]
            out_ref[q, z] = jnp.concatenate(block, 0).astype(BF)


def front_grad5_body(g_ref, mid_ref, out_ref):
    turned = g_ref[...].astype(F32).T.astype(BF)
    front_rows(mm(turned, mid_ref[...]), out_ref)


def branch_grad4_body(
    gm_ref, c_ref, p_ref, s_ref, n_ref, b0, b1, b2, b3, dv_ref, dp_ref, turned_ref, b_ref, *, voxels
):
    turn = turn_matrix(256, 64)
    b_ref[...] = total_of((b0, b1, b2, b3))
    matrix = two_matrix(True)
    for h in range(2):
        rows = slice(256 * h, 256 * h + 256)
        block = gm_ref[64 * h : 64 * h + 64, :]
        for src, dst, lanes, at in (
            (p_ref, dp_ref, slice(0, BP), slice(0, BP)),
            (c_ref, dv_ref, slice(BP, BP + OUTER), slice(BP + B0, LAYER)),
        ):
            up = exact(matrix, block[:, at])
            sums, norms, back = s_ref[:, lanes], n_ref[:, lanes], b_ref[:, lanes]
            for f in range(2):
                values = src[f, rows, :]
                _, y = normed(values, sums, norms, voxels)
                dv = norm_back(up * slope(y), values, sums, norms, back, voxels)
                dst[f, rows, :] = dv.astype(BF)
                if dst is dv_ref:
                    turned_ref[1 - f, rows, :] = mm(turn, dv.astype(BF)).astype(BF)


def put(out_ref, place, rows, lane, value):
    size = out_ref.shape[-1]
    done, width = 0, value.shape[1]
    while done < width:
        part, at = divmod(lane + done, size)
        step = min(width - done, size - at)
        out_ref[part, place, rows, at : at + step] = value[:, done : done + step].astype(BF)
        done += step


def taps_out(out_ref, t, grad, slots):
    places = len(slots)
    for z, slot in enumerate(slots):
        put(out_ref, slot, slice(0, 80), B1R * t, grad[80 * z : 80 * z + 80, :B1R])
        low = grad[80 * places + 32 * z : 80 * places + 32 * z + 32, B1R:INNER]
        put(out_ref, slot, slice(80, 96), B2R * t, low[:16])
        put(out_ref, slot, slice(80, 96), NARROW_AT + B2R * t, low[16:])


def wide_lanes(a):
    return jnp.concatenate([a.astype(F32), jnp.zeros((a.shape[0], 64), F32)], 1)


def kernel_grad4_body(me_ref, a_ref, before_ref, after_ref, dv_ref, out_ref, patches, turned):
    out_ref[...] = jnp.zeros_like(out_ref)
    for q, a in enumerate((before_ref[...], a_ref[0], a_ref[1], after_ref[...])):
        a = wide_lanes(a)
        for n in range(9):
            patches[q, :, 256 * n : 256 * n + 256] = shifted(a, 8, n // 3 - 1, n % 3 - 1).astype(BF)
    for f in range(2):
        turned[:, 512 * f : 512 * f + 512] = dv_ref[f].astype(F32).T.astype(BF)
    for t in range(TAPS):
        i, n = t // 9, t % 9
        window = patches[i : i + 2, :, 256 * n : 256 * n + 256].reshape(1024, 256)
        slots = [jnp.bitwise_xor(me_ref[0], z) for z in range(4)]
        taps_out(out_ref, t, mm(turned[...], window), slots)


def kernel_grad5_body(a_ref, dv_ref, out_ref, patches, turned):
    out_ref[...] = jnp.zeros_like(out_ref)
    for q in (0, 5):
        patches[q] = jnp.zeros(patches.shape[1:], BF)
    for q in range(4):
        a = wide_lanes(a_ref[q])
        for n in range(9):
            patches[q + 1, :, 256 * n : 256 * n + 256] = shifted(a, 4, n // 3 - 1, n % 3 - 1).astype(BF)
        turned[:, 128 * q : 128 * q + 128] = dv_ref[q].astype(F32).T.astype(BF)
    for t in range(TAPS):
        i, n = t // 9, t % 9
        window = patches[i : i + 4, :, 256 * n : 256 * n + 256].reshape(512, 256)
        taps_out(out_ref, t, mm(turned[...], window), [0])


def front_back4_body(
    gm_ref, z_ref, s_ref, n_ref, own_ref, before_ref, after_ref, dp_ref, dy_ref, u_ref, x_ref, *, voxels
):
    two, pool, turn = two_matrix(True), pool_matrix(256, 8), turn_matrix(256, 64)
    x_ref[...] = jnp.zeros_like(x_ref)
    for h in range(2):
        rows = slice(256 * h, 256 * h + 256)
        up = exact(two, gm_ref[64 * h : 64 * h + 64, BP : BP + B0])
        for f in range(2):
            rim = before_ref if f == 0 else after_ref
            v = dp_ref[0, rows, :].astype(F32) + dp_ref[1, rows, :].astype(F32)
            v = (v + rim[rows, :BP].astype(F32)).astype(BF)
            u_ref[f, rows, :] = (mm(pool, v) * (1.0 / 27.0)).astype(BF)
            inner = exact(turn, own_ref[1 - f, rows, :] + rim[rows, BP:].astype(F32))
            for lanes, grad in ((slice(0, B0), up), (slice(B0, REDUCED), inner)):
                at = slice(BP + lanes.start, BP + lanes.stop)
                scaled, y = normed(z_ref[f, rows, at], s_ref[:, lanes], n_ref[:, lanes], voxels)
                dy = grad * slope(y)
                dy_ref[f, rows, lanes] = dy
                add_pair(x_ref, lanes, dy, dy * scaled)


def front_grad4_body(z_ref, s_ref, n_ref, dy_ref, b0, b1, b2, b3, u_ref, x_ref, g_ref, out_ref, b_ref, *, voxels):
    b_ref[...] = total_of((b0, b1, b2, b3))
    total = 0.0
    for f in range(2):
        for h in range(2):
            rows = slice(256 * h, 256 * h + 256)
            g_ref[f, rows, :BP] = u_ref[f, rows, :]
            g_ref[f, rows, BP:] = norm_back(
                dy_ref[f, rows, :], z_ref[f, rows, BP:], s_ref[...], n_ref[...], b_ref[...], voxels
            ).astype(BF)
        turned = g_ref[f].astype(F32).T.astype(BF)
        total = total + mm(turned, x_ref[:, f].reshape(512, x_ref.shape[3]))
    front_rows(total, out_ref)


def clips_grad_body(g_ref, w_ref, out_ref):
    for f in range(2):
        for h in range(2):
            grad = mm(g_ref[f, 256 * h : 256 * h + 256, :], w_ref[...])
            out_ref[4 * h : 4 * h + 4, f] = grad.reshape(4, 64, out_ref.shape[3])


def lines(buf, first, count, starts, width):
    out = []
    for r in range(4):
        rows = pl.ds(first + r, count, stride=4)
        part = []
        for at in starts:
            tiles = [buf[at + n, rows, :] for n in range(-(-width // 128))]
            part.append(jnp.concatenate(tiles, 1)[:, :width])
        out.append(jnp.concatenate(part, 0) if len(part) > 1 else part[0])
    return jnp.concatenate(out, 1)


def rows_body(both_ref, wide_ref, narrow_ref, buf):
    wide, narrow = [], []
    for t in range(2):
        for q in range(4):
            for n in range(9):
                buf[9 * q + n] = both_ref[t, q, :, 128 * n : 128 * (n + 1)].astype(F32)
        wide.append(lines(buf, 0, 20, (0,), TAPS * B1R))
        narrow.append(lines(buf, 80, 4, (0, NARROW_AT // 128), TAPS * B2R))
    for pair, out_ref in ((wide, wide_ref), (narrow, narrow_ref)):
        count, size = pair[0].shape
        for n in range(count):
            rows = [part[n : n + 1] for part in pair]
            out_ref[:, size * n : size * (n + 1)] = jnp.concatenate(rows, 0)


def features_body(me_ref, z_ref, s_ref, n_ref, r0, r1, r2, r3, out_ref, *, voxels):
    rest = 0.0
    for k, r in enumerate((r0, r1, r2, r3)):
        rest = rest + mm(r[...], own_columns(jnp.bitwise_xor(me_ref[0], k), True))
    _, y = normed(z_ref[:, BP : BP + B0], s_ref[:, :B0], n_ref[:, :B0], voxels)
    out_ref[:, :B0] = silu(y)
    out_ref[:, B0:] = rest[:, B0:]


def xor_pairs(axis, step):
    return [(i, i ^ step) for i in range(lax.axis_size(axis))]


def tower_steps():
    steps, step = [], 1
    while step < lax.axis_size("dp") // 2:
        steps.append(step)
        step *= 2
    return steps


def other_tower(value):
    return lax.ppermute(value, "dp", xor_pairs("dp", lax.axis_size("dp") // 2))


def blk_peers(value):
    count = lax.axis_size("blk")
    return [value] + [lax.ppermute(value, "blk", xor_pairs("blk", k)) for k in range(1, count)]


def by_place(parts):
    me, step = lax.axis_index("blk"), 1
    while step < len(parts):
        hit = (me & step) != 0
        parts = [jnp.where(hit, parts[k ^ step], parts[k]) for k in range(len(parts))]
        step *= 2
    return parts


def swap_blk(mine):
    return [mine[0]] + [
        lax.ppermute(mine[k], "blk", xor_pairs("blk", k)) for k in range(1, lax.axis_size("blk"))
    ]


def dp_sum(value):
    for step in tower_steps():
        value = value + lax.ppermute(value, "dp", xor_pairs("dp", step))
    return value


def tower_parts(value):
    return blk_peers(dp_sum(value))


def gather_pieces(shard, first=None):
    rows = shard.shape[0] // 2
    odd = lax.axis_index("dp") % 2
    half = lax.dynamic_slice_in_dim(shard, odd * rows, rows, 0)
    mine = blk_peers(half)[1:]
    if first is not None:
        mine = after(mine, first)
    twins = [lax.ppermute(piece, "dp", xor_pairs("dp", 1)) for piece in mine]
    return [shard] + mine + twins


def fours():
    return [list(range(i, i + 4)) for i in range(0, lax.axis_size("dp"), 4)]


def scatter_four(value):
    value = lax.psum_scatter(
        value, "dp", scatter_dimension=0, axis_index_groups=fours(), tiled=False
    )
    for step in tower_steps()[2:]:
        got = lax.ppermute(value, "dp", xor_pairs("dp", step))
        value = (value.astype(F32) + got.astype(F32)).astype(BF)
    return value


def gather_eight(value):
    half = lax.axis_size("dp") // 2
    groups = [
        [b + i for i in range(4)] + [half + b + i for i in range(4)] for b in range(0, half, 4)
    ]
    return lax.all_gather(value, "dp", axis_index_groups=groups, tiled=False)


def spread_square(value):
    half = lax.axis_size("dp") // 2
    dp = lax.axis_index("dp")
    side = lax.ppermute(value, "dp", xor_pairs("dp", 2))
    other = other_tower(value)
    corner = jnp.concatenate(
        [
            lax.ppermute(other[:48], "dp", xor_pairs("dp", 2)),
            other_tower(side[48:]),
        ]
    )
    right = dp // 2 % 2 == 1
    ours = jnp.where(right, jnp.stack([side, value]), jnp.stack([value, side]))
    theirs = jnp.where(right, jnp.stack([corner, other]), jnp.stack([other, corner]))
    both = jnp.where(dp // half == 0, jnp.stack([ours, theirs]), jnp.stack([theirs, ours]))
    twin = lax.ppermute(both, "dp", xor_pairs("dp", 1))
    pair = jnp.where(dp % 2 == 0, jnp.stack([both, twin], 2), jnp.stack([twin, both], 2))
    return pair.reshape(2, 4, *value.shape)


def after(values, first):
    values, _ = lax.optimization_barrier((values, first))
    return values


def rim_swap(first, last):
    count = lax.axis_size("blk")
    ahead = [(i, i + 1) for i in range(count - 1)]
    back = [(i + 1, i) for i in range(count - 1)]
    return lax.ppermute(last, "blk", ahead), lax.ppermute(first, "blk", back)


def step_rows(value, axis, step):
    if step in tower_steps()[:2]:
        rows = value.shape[axis] // 2
        high = (lax.axis_index("dp") & step) != 0
        keep = lax.dynamic_slice_in_dim(value, jnp.where(high, rows, 0), rows, axis)
        give = lax.dynamic_slice_in_dim(value, jnp.where(high, 0, rows), rows, axis)
    else:
        keep = give = value
    got = lax.ppermute(give, "dp", xor_pairs("dp", step))
    return (keep.astype(F32) + got.astype(F32)).astype(BF)


def reduce_rows(value, axis, steps=None):
    for step in tower_steps() if steps is None else steps:
        value = step_rows(value, axis, step)
    return value


def reduce_blk(value):
    count = value.shape[0]
    got = swap_blk(by_place([value[j] for j in range(count)]))
    total = got[0].astype(F32)
    for piece in got[1:]:
        total = total + piece.astype(F32)
    return total.astype(BF)


def spread_rows(value):
    stream = lax.axis_index("dp") // (lax.axis_size("dp") // 2)
    other = other_tower(value)
    both = jnp.where(stream == 0, jnp.stack([value, other]), jnp.stack([other, value]))
    for step in (2, 1):
        got = lax.ppermute(both, "dp", xor_pairs("dp", step))
        high = (lax.axis_index("dp") & step) != 0
        both = jnp.where(
            high, jnp.concatenate([got, both], 1), jnp.concatenate([both, got], 1)
        )
    return both


def branch_rows(both):
    return call(
        rows_body,
        (shape_of((2, 80 * TAPS * B1R)), shape_of((2, 32 * TAPS * B2R))),
        both,
        micros=3, mib=24, scratch=[pltpu.VMEM((36, 96, 128), F32)],
    )


def pick_row(param, stream):
    size = param.shape[1]
    return lax.dynamic_index_in_dim(param.reshape(2, size // 128, 128), stream, 0, keepdims=False)


def on_device(clips, cotangent, *params):
    groups = lax.axis_size("dp")
    count = lax.axis_size("blk")
    stream = lax.axis_index("dp") // (groups // 2)
    place = lax.axis_index("blk")
    index = lax.axis_index("dp")
    me = jnp.stack([place, index % (groups // 2), index % 2, index // 2 % 2]).astype(jnp.int32)
    own = [pick_row(p, stream) for p in params]
    early, late = own[:6], own[6:]
    n, frames, height, breadth, c_first = clips.shape
    voxels = groups // 2 * count * n * frames * height * breadth
    late_voxels = voxels // 8
    x = clips.reshape(n, frames, height * breadth, c_first)
    e, p = REDUCED // count, BP // count
    g = (REDUCED + OUTER + BP) // count

    def pack_front(layer, c, turn=0):
        norms = jnp.concatenate([layer[4].reshape(-1), layer[5].reshape(-1)])
        row = jnp.pad(norms, (0, c - 2 * g)).reshape(1, c)
        rows = jnp.concatenate([layer[0].reshape(e, c), layer[3].reshape(p, c)])
        if turn:
            rows = jnp.concatenate([rows[:, c - turn :], rows[:, : c - turn]], 1)
        return jnp.pad(jnp.concatenate([rows, row]), ((0, 160 - e - p - 1), (0, 0)))

    def pack_branch(layer):
        wide = layer[1].reshape(80, -1)
        narrow = layer[2].reshape(32, -1)
        gap = jnp.zeros((16, NARROW_AT - narrow.shape[1]), BF)
        low = jnp.concatenate([narrow[:16], gap, narrow[16:]], 1)
        low = jnp.pad(low, ((0, 0), (0, 4608 - low.shape[1])))
        return jnp.concatenate([jnp.pad(wide, ((0, 0), (0, 4608 - wide.shape[1]))), low])

    pieces = gather_pieces(pack_front(early, c_first))
    packed = after(pack_branch(early), pieces[0])
    packed = lax.dynamic_slice_in_dim(packed, index % 2 * 48, 48, 0)
    packed = lax.all_gather(packed, "blk", tiled=False)
    late = after(late, pieces[0])
    taps_5 = call(kernels5_body, shape_of((TAPS, 128, INNER), BF), pack_branch(late), micros=2)
    x = after(x, taps_5)
    z, pre, m, front_4, nf4, nb4 = call(
        front4_body,
        (
            shape_of((2, 512, 576)), shape_of((2, 512, BP), BF), shape_of((2, REDUCED)),
            shape_of((576, c_first), BF), shape_of((2, REDUCED)), shape_of((2, 576)),
        ),
        me, x, *pieces, micros=4,
        scratch=[pltpu.VMEM((4, 160, c_first), BF), pltpu.VMEM((2, 1024), F32)],
    )
    late, cotangent = after((late, cotangent), m)
    late_front = pack_front(late, LAYER, BP)
    cot = cotangent.reshape(128, LAYER)
    cot_mine = call(cot5_body, shape_of((4, 128, 256), BF), me, cot, micros=2)

    def conv(values, kernel, pads, order):
        return lax.conv_general_dilated(
            values,
            kernel.reshape(-1, 3, 3, *kernel.shape[1:]),
            (1, 1, 1),
            pads,
            dimension_numbers=("DNHWC", order, "DNHWC"),
            preferred_element_type=F32,
        )

    forth, back = "DHWOI", "DHWIO"
    flat_pads = ((0, 0), (1, 1), (1, 1))
    same = ((1, 1), (1, 1), (1, 1))
    at4 = functools.partial(functools.partial, voxels=voxels)
    at5 = functools.partial(functools.partial, voxels=late_voxels)

    parts = tower_parts(m)
    z_then = after(z, (late_front, cot_mine))
    a, sf4 = call(
        at4(act4_body),
        (shape_of((2, 512, INNER), BF), shape_of((2, REDUCED))),
        z_then, *parts, nf4, micros=2,
    )
    before, behind = rim_swap(a[0], a[1])
    rims = after(pre, (before, behind))
    pre_before, pre_after = rim_swap(rims[0], rims[1])
    pool, m_pool = call(
        pool4_body, (shape_of((2, 512, BP)), shape_of((2, BP))), pre, pre_before, pre_after, micros=2
    )
    packed = after(packed, (before, behind))
    twin = lax.ppermute(packed, "dp", xor_pairs("dp", 1))
    taps_4, taps_first, taps_last = call(
        kernels4_body,
        (
            shape_of((TAPS, OUTER, INNER), BF),
            shape_of((9, OUTER, INNER), BF), shape_of((9, OUTER, INNER), BF),
        ),
        me, packed, twin, micros=5, mib=16, scratch=[pltpu.VMEM((4, 96, 4608), BF)],
    )
    late_front = after(late_front, (before, behind, taps_4))
    a_pad = jnp.concatenate([before[None], a, behind[None]]).reshape(4, n, height, breadth, INNER)
    c = conv(a_pad, taps_4, flat_pads, forth).reshape(2, 512, OUTER)
    front_5, n5f, n5 = call(
        front5_body,
        (shape_of((576, LAYER), BF), shape_of((2, 1024)), shape_of((2, 256))),
        me, *gather_pieces(late_front, c), micros=1, scratch=[pltpu.VMEM((4, 160, LAYER), BF)],
    )
    cots = swap_blk([after(cot_mine, c)[k] for k in range(4)])
    parts = tower_parts(call(moments_body, shape_of((2, 576)), c, m_pool, micros=1))

    mid, z5, m, sb4 = call(
        at4(norm4_body),
        (shape_of((128, LAYER), BF), shape_of((128, 576)), shape_of((2, REDUCED)), shape_of((2, 576))),
        z, c, pool, sf4, *parts, nf4, nb4, front_5, micros=4, lazy=(0, 2, 3, 8, 9, 10),
    )
    send, sf5 = call(
        at5(act5_body),
        (shape_of((4, 128, 256), BF), shape_of((2, REDUCED))),
        me, z5, *tower_parts(m), n5f, micros=1,
    )
    a5, pool5 = call(
        join5_body,
        (shape_of((4, 128, INNER), BF), shape_of((4, 128, 128))),
        me, *swap_blk([send[k] for k in range(4)]),
        micros=1, scratch=[pltpu.VMEM((6, 128, 128), F32)],
    )
    small = (4, n, height // 2, breadth // 2, -1)
    c5 = conv(a5.reshape(small), taps_5, same, forth).reshape(4, 128, 128)
    s5 = dp_sum(call(moments5_body, shape_of((2, 256)), c5, pool5, micros=1))
    feat, dy5, m = call(
        at5(norm5_body),
        (shape_of((4, 128, 256), BF), shape_of((4, 128, 256)), shape_of((2, 256))),
        me, c5, pool5, s5, n5, *cots, micros=1, lazy=(2, 4, 5, 6, 7, 8),
    )

    b5 = dp_sum(m)
    dv5, turned5, u5 = call(
        at5(back5_body),
        (shape_of((4, 128, 128), BF), shape_of((4, 128, 128), BF), shape_of((4, 128, 128))),
        c5, pool5, s5, n5, dy5, b5, micros=1, lazy=(0, 1, 2, 3, 4),
    )
    part = conv(turned5.reshape(small), taps_5, same, back).reshape(4, 128, INNER)
    send = call(send5_body, shape_of((4, 128, 256), BF), me, part, u5, micros=1)
    dv5 = after(dv5, send)
    branch_part5 = call(
        kernel_grad5_body,
        shape_of((4, 1, 96, 1152), BF),
        a5, dv5,
        micros=2, mib=16,
        scratch=[pltpu.VMEM((6, 128, 2304), BF), pltpu.VMEM((128, 512), BF)],
    )
    z5 = after(z5, branch_part5)
    branch_5 = scatter_four(branch_part5)
    dyf5, u5, m = call(
        at5(front_back5_body),
        (shape_of((128, REDUCED)), shape_of((128, BP), BF), shape_of((2, 1536))),
        me, *swap_blk([send[k] for k in range(4)]), z5, sf5, n5f, cot[:, :B0], b5, micros=1,
        lazy=(5, 6, 7, 8, 9),
    )
    parts = tower_parts(m)
    g5, gm, m, back5 = call(
        at4(mid_back_body),
        (shape_of((128, 576), BF), shape_of((128, LAYER)), shape_of((2, 576)), shape_of((2, 1536))),
        dyf5, z5, sf5, n5f, *parts, u5, front_5, c, pool, sb4, nb4, micros=4,
        lazy=(0, 1, 2, 3, 8, 9, 10, 11, 12, 13),
    )

    parts = tower_parts(m)
    front_part5 = call(
        front_grad5_body, shape_of((4, 4, 40, LAYER), BF), after(g5, parts[0]), mid, micros=1
    )
    front_part5 = jnp.concatenate([front_part5[..., BP:], front_part5[..., :BP]], 3)
    gm = after(gm, front_part5)
    front_5_sum = scatter_four(front_part5)
    dv, dp, turned4, bb4 = call(
        at4(branch_grad4_body),
        (
            shape_of((2, 512, OUTER), BF), shape_of((2, 512, BP), BF),
            shape_of((2, 512, OUTER), BF), shape_of((2, 576)),
        ),
        gm, c, pool, sb4, nb4, *parts, micros=3, lazy=(0, 1, 2, 3, 4),
    )
    branch_part4 = call(
        kernel_grad4_body,
        shape_of((4, 4, 96, 1152), BF),
        me, a, before, behind, dv,
        micros=8, mib=24,
        scratch=[pltpu.VMEM((4, 512, 2304), BF), pltpu.VMEM((OUTER, 1024), BF)],
    )
    turned4 = after(turned4, branch_part4)
    branch_part4 = scatter_four(branch_part4)
    image = (1, n, height, breadth, OUTER)
    rim_first = conv(turned4[1].reshape(image), taps_first, flat_pads, back).reshape(512, INNER)
    rim_last = conv(turned4[0].reshape(image), taps_last, flat_pads, back).reshape(512, INNER)
    got_before, got_after = rim_swap(
        jnp.concatenate([dp[0], rim_first.astype(BF)], 1),
        jnp.concatenate([dp[1], rim_last.astype(BF)], 1),
    )
    turned4 = after(turned4, (rim_first, rim_last))
    front_5_own = reduce_blk(after(front_5_sum, turned4))
    inner = conv(turned4.reshape(2, n, height, breadth, OUTER), taps_4, same, back)
    dyf4, u4, m = call(
        at4(front_back4_body),
        (shape_of((2, 512, REDUCED)), shape_of((2, 512, BP), BF), shape_of((2, REDUCED))),
        after(gm, front_5_own), z, sf4, nf4, inner.reshape(2, 512, INNER), got_before, got_after, dp, micros=4,
        lazy=(0, 1, 2, 3, 7),
    )
    parts = tower_parts(m)
    g4, front_part4, bf4 = call(
        at4(front_grad4_body),
        (shape_of((2, 512, 576), BF), shape_of((4, 4, 40, c_first), BF), shape_of((2, REDUCED))),
        z, sf4, nf4, dyf4, *parts, u4, x, micros=4, lazy=(1, 2),
    )
    clips_grad = call(
        clips_grad_body, shape_of((n, frames, height * breadth, c_first)), g4, front_4, micros=3
    ).reshape(clips.shape)

    feat = after(feat, dv)
    got = swap_blk([feat[k] for k in range(4)])
    features = call(
        at5(features_body), shape_of((128, LAYER)), me, z5, sf5, n5f, *got, micros=2
    ).reshape(cotangent.shape)

    def front_out(both):
        both = both.astype(F32)
        return both[:, :, :28].reshape(2, -1), both[:, :, 32:].reshape(2, -1)

    branch_4 = after(branch_part4, front_part4)
    branch_4 = sum(piece.astype(F32) for piece in swap_blk([branch_4[k] for k in range(4)])).astype(BF)
    front_4 = after(reduce_rows(front_part4, 0)[0], branch_4)
    front_5 = jnp.pad(front_5_own, ((0, 0), (0, 1152 - LAYER)))
    both5 = gather_eight(jnp.concatenate([after(branch_5, m)[0], front_5])).reshape(2, 4, 136, 1152)
    both5 = after(both5, branch_4)
    wide_5, narrow_5 = branch_rows(both5[:, :, :96])
    entry_5, poolproj_5 = front_out(both5[:, :, 96:, :LAYER])
    wide_4, narrow_4 = branch_rows(spread_square(branch_4))
    entry_4, poolproj_4 = front_out(spread_rows(reduce_blk(front_4)[None]))

    all5 = back5[:, 512:].reshape(2, count, 256)
    norms4 = jnp.concatenate([bf4, bb4[:, BP:], bb4[:, :BP]], 1)
    norms5 = jnp.concatenate(
        [
            back5[:, :REDUCED],
            all5[:, :, :80].reshape(2, -1),
            all5[:, :, 80:112].reshape(2, -1),
            all5[:, :, 128 + POOL_LANE : 160 + POOL_LANE].reshape(2, -1),
        ],
        axis=1,
    )
    norms = jnp.stack([norms4, norms5])
    theirs = other_tower(norms)
    norms = jnp.where(stream == 0, jnp.stack([norms, theirs]), jnp.stack([theirs, norms]))
    norms = lax.dynamic_slice_in_dim(norms, place * g, g, 3)
    return (
        features, clips_grad,
        entry_4, wide_4, narrow_4, poolproj_4, norms[:, 0, 1], norms[:, 0, 0],
        entry_5, wide_5, narrow_5, poolproj_5, norms[:, 1, 1], norms[:, 1, 0],
    )


def solution(mesh):
    spec = P("dp", "blk", None, None, None)
    flat = P(None, "blk")
    return jax.shard_map(
        on_device,
        mesh=mesh,
        in_specs=(spec, spec) + (flat,) * 12,
        out_specs=(spec, spec) + (flat,) * 12,
        check_vma=False,
    )
```

```python
import functools

import jax
import jax.numpy as jnp
from jax import lax
from jax.experimental import pallas as pl
from jax.experimental.pallas import tpu as pltpu
from jax.sharding import PartitionSpec as P

B0 = 256
B1R = 160
B1 = 320
B2R = 32
B2 = 128
BP = 128
INNER = B1R + B2R
REDUCED = B0 + INNER
OUTER = B1 + B2
LAYER = B0 + OUTER + BP
EPS = 1e-05
BF = jnp.bfloat16
F32 = jnp.float32
TAPS = 27
NARROW_AT = 896
POOL_LANE = 64

NT = (((1,), (1,)), ((), ()))
NN = (((1,), (0,)), ((), ()))
VMEM = pl.BlockSpec(memory_space=pltpu.VMEM)
SMEM = pl.BlockSpec(memory_space=pltpu.SMEM)


def mm(a, b, dims=NN):
    return lax.dot_general(a, b, dims, preferred_element_type=F32)


def shape_of(shape, kind=F32):
    return jax.ShapeDtypeStruct(shape, kind)


def call(body, outs, *args, micros=2, scratch=(), mib=6, lazy=(), away=()):
    def whole(*refs):
        bufs, sems = refs[len(refs) - len(lazy) - 1 : -1], refs[-1]
        copies = [
            pltpu.make_async_copy(refs[i], bufs[n], sems.at[n]) for n, i in enumerate(lazy)
        ]
        for copy in copies:
            copy.start()
        for copy in copies:
            copy.wait()
        ins = list(refs[: len(args)])
        for n, i in enumerate(lazy):
            ins[i] = bufs[n]
        body(*ins, *refs[len(args) : len(refs) - len(lazy) - 1])

    lazy = [i % len(args) for i in lazy]
    specs = [SMEM if a.dtype == jnp.int32 else VMEM for a in args]
    scratch, size = list(scratch), 0
    for i in lazy:
        specs[i] = pl.BlockSpec(memory_space=pl.ANY)
        scratch.append(pltpu.VMEM(args[i].shape, args[i].dtype))
        size += args[i].size * args[i].dtype.itemsize
    if lazy:
        scratch.append(pltpu.SemaphoreType.DMA((len(lazy),)))
    spots = [VMEM] * (len(outs) if isinstance(outs, tuple) else 1)
    for i in away:
        spots[i] = pl.BlockSpec(memory_space=pl.ANY)
    return pl.pallas_call(
        whole if lazy else body,
        out_shape=outs,
        in_specs=specs,
        out_specs=spots if isinstance(outs, tuple) else spots[0],
        scratch_shapes=scratch,
        compiler_params=pltpu.CompilerParams(vmem_limit_bytes=(mib << 20) + 5 * size // 4),
        cost_estimate=pl.CostEstimate(
            flops=int(micros * 1.0e9), bytes_accessed=1 << 20 if micros else 0, transcendentals=0
        ),
    )(*args)


def iota(shape, axis):
    return lax.broadcasted_iota(jnp.int32, shape, axis)


def ones_where(ok, value=1.0):
    return jnp.where(ok, value, 0.0).astype(BF)


def pool_matrix(n, side):
    r, c = iota((n, n), 0), iota((n, n), 1)
    area = side * side
    near_w = jnp.abs(r % side - c % side) <= 1
    near_h = jnp.abs((r // side) % side - (c // side) % side) <= 1
    return ones_where((r // area == c // area) & near_w & near_h)


def turn_matrix(n, area):
    r, c = iota((n, n), 0), iota((n, n), 1)
    return ones_where((r // area == c // area) & (r % area + c % area == area - 1))


def two_matrix(transposed):
    shape = (256, 64) if transposed else (64, 256)
    big, small = (iota(shape, 0), iota(shape, 1)) if transposed else (iota(shape, 1), iota(shape, 0))
    ok = (small // 16 == big // 64) & ((small // 4) % 4 == (big // 16) % 4)
    return ones_where(ok & (small % 4 == (big // 2) % 4), 0.125)


def exact(matrix, values):
    high = values.astype(BF)
    low = (values - high.astype(F32)).astype(BF)
    return mm(matrix, high) + mm(matrix, low)


def own_columns(place, transposed=False):
    shape = (256, LAYER) if transposed else (LAYER, 256)
    lane, col = (iota(shape, 0), iota(shape, 1)) if transposed else (iota(shape, 1), iota(shape, 0))
    wide = (lane < 80) & (col == B0 + 80 * place + lane)
    narrow = (lane >= 80) & (lane < 112) & (col == B0 + B1 + 32 * place + lane - 80)
    at = lane - 128 - POOL_LANE
    pool = (at >= 0) & (at < 32) & (col == B0 + OUTER + 32 * place + at)
    return ones_where(wide | narrow | pool)


def scaled_of(values, sums, voxels):
    centre = sums[0:1] * (1.0 / voxels)
    spread = lax.rsqrt(sums[1:2] * (1.0 / voxels) - centre * centre + EPS)
    return (values - centre) * spread, spread


def normed(values, sums, norms, voxels):
    scaled, _ = scaled_of(values, sums, voxels)
    return scaled, scaled * norms[0:1] + norms[1:2]


def silu(y):
    return y * lax.logistic(y)


def slope(y):
    sigmoid = lax.logistic(y)
    return sigmoid * (1.0 + y * (1.0 - sigmoid))


def norm_back(dy, values, sums, norms, back, voxels):
    scaled, spread = scaled_of(values, sums, voxels)
    scale = norms[0:1] * spread
    return scale * (dy - back[0:1] * (1.0 / voxels) - scaled * (back[1:2] * (1.0 / voxels)))


def add_pair(ref, lanes, first, second):
    ref[0:1, lanes] += jnp.sum(first, 0, keepdims=True)
    ref[1:2, lanes] += jnp.sum(second, 0, keepdims=True)


def shifted(a, side, j, k):
    if j == 0 and k == 0:
        return a
    rows, lanes = a.shape
    area = side * side
    r = iota((area, lanes), 0)
    w, h = r % side + k, r // side + j
    ok = (w >= 0) & (w < side) & (h >= 0) & (h < side)
    moved = pltpu.roll(a, (-(side * j + k)) % rows, 0).reshape(rows // area, area, lanes)
    return jnp.where(ok[None], moved, 0.0).reshape(rows, lanes)


def assemble(me_ref, pieces, buf):
    half = pieces[0].shape[0] // 2
    buf[me_ref[0]] = pieces[0][...]
    for k in range(1, 4):
        place = jnp.bitwise_xor(me_ref[0], k)
        buf[place, pl.ds(pl.multiple_of(half * me_ref[2], half), half), :] = pieces[k][...]
        buf[place, pl.ds(pl.multiple_of(half * (1 - me_ref[2]), half), half), :] = pieces[k + 3][...]


def tap_block(shards, t):
    wide, narrow = [], []
    for w in shards:
        wide.append(w[0:80, B1R * t : B1R * (t + 1)].astype(F32))
        for lane in (B2R * t, NARROW_AT + B2R * t):
            narrow.append(w[80:96, lane : lane + B2R].astype(F32))
    wide = jnp.concatenate(wide, 0)
    narrow = jnp.concatenate(narrow, 0)
    top = jnp.concatenate([wide, jnp.zeros((wide.shape[0], B2R), F32)], 1)
    low = jnp.concatenate([jnp.zeros((narrow.shape[0], B1R), F32), narrow], 1)
    return jnp.concatenate([top, low], 0).astype(BF)


def kernels4_body(me_ref, mine_ref, twin_ref, all_ref, first_ref, last_ref, buf, sems):
    first = pltpu.make_async_copy(all_ref.at[0:9], first_ref, sems.at[0])
    last = pltpu.make_async_copy(all_ref.at[18:27], last_ref, sems.at[1])
    buf[:, pl.ds(pl.multiple_of(48 * me_ref[2], 16), 48), :] = mine_ref[:, :48, :]
    buf[:, pl.ds(pl.multiple_of(48 * (1 - me_ref[2]), 16), 48), :] = twin_ref[:, :48, :]
    for t in range(TAPS):
        all_ref[t] = tap_block([buf.at[z] for z in range(4)], t)
        if t == 8:
            first.start()
    last.start()
    first.wait()
    last.wait()


def kernels5_body(w_ref, all_ref):
    for t in range(TAPS):
        all_ref[t] = jnp.concatenate([tap_block([w_ref], t), jnp.zeros((16, INNER), BF)], 0)


def front_parts(buf, matrix_ref, norms_ref):
    for z in range(4):
        matrix_ref[32 * z : 32 * (z + 1), :] = buf[z, 112:144, :]
        matrix_ref[BP + 112 * z : BP + 112 * (z + 1), :] = buf[z, 0:112, :]
        row = buf[z, 144:160, :].astype(F32)[0:1]
        norms_ref[0:1, 256 * z : 256 * (z + 1)] = row[:, :256]
        norms_ref[1:2, 256 * z : 256 * (z + 1)] = row[:, 256:512]


def total_of(parts):
    return (parts[0][...] + parts[1][...]) + (parts[2][...] + parts[3][...])


def front5_body(me_ref, mine_ref, twin_ref, w_ref, n_ref, own_ref, buf):
    for src, odd in ((mine_ref, me_ref[2]), (twin_ref, 1 - me_ref[2])):
        for j in range(5):
            rows = pl.ds(pl.multiple_of(80 * odd + 16 * j, 16), 16)
            buf[:, rows, :] = src[:, 48:64, LAYER * j : LAYER * (j + 1)]
    front_parts(buf, w_ref, n_ref)
    norms = n_ref[...]
    own = jnp.zeros((2, 256), F32)
    gap = jnp.zeros((2, 16 + POOL_LANE), F32)
    for z in range(4):
        wide = norms[:, REDUCED + 80 * z : REDUCED + 80 * (z + 1)]
        narrow = norms[:, REDUCED + B1 + 32 * z : REDUCED + B1 + 32 * (z + 1)]
        pool = norms[:, REDUCED + OUTER + 32 * z : REDUCED + OUTER + 32 * (z + 1)]
        block = jnp.concatenate([wide, narrow, gap, pool, jnp.zeros((2, 32), F32)], 1)
        own = jnp.where(me_ref[0] == z, block, own)
    own_ref[...] = own


def front4_body(me_ref, x_ref, p0, p1, p2, p3, t1, t2, t3, z_ref, m_ref, w_ref, nf_ref, nb_ref, buf, n_ref):
    assemble(me_ref, (p0, p1, p2, p3, t1, t2, t3), buf)
    front_parts(buf, w_ref, n_ref)
    nf_ref[...] = n_ref[:, :REDUCED]
    nb_ref[:, :BP] = n_ref[:, REDUCED + OUTER :]
    nb_ref[:, BP:] = n_ref[:, REDUCED : REDUCED + OUTER]
    m_ref[...] = jnp.zeros_like(m_ref)
    for f in range(2):
        for h in range(2):
            x = x_ref[4 * h : 4 * h + 4, f].reshape(256, x_ref.shape[3])
            z = mm(x, w_ref[...], NT)
            rows = slice(256 * h, 256 * h + 256)
            z_ref[f, rows, :] = z
            front = z[:, BP:]
            add_pair(m_ref, slice(None), front, front * front)


def act4_body(z_ref, s0, s1, s2, s3, n_ref, a_ref, rim_ref, s_ref, *, voxels):
    s_ref[...] = total_of((s0, s1, s2, s3))
    sums, norms = s_ref[:, B0:], n_ref[:, B0:]
    for f in range(2):
        for h in range(2):
            rows = slice(256 * h, 256 * h + 256)
            _, y = normed(z_ref[f, rows, BP + B0 :], sums, norms, voxels)
            a_ref[f, rows, :] = silu(y).astype(BF)
            rim_ref[f, rows, :BP] = z_ref[f, rows, :BP].astype(BF)
            rim_ref[f, rows, BP:] = silu(y).astype(BF)


def pool4_body(pp_ref, before_ref, after_ref, pool_ref, m_ref):
    matrix = pool_matrix(256, 8)
    m_ref[...] = jnp.zeros_like(m_ref)
    for f in range(2):
        for h in range(2):
            rows = slice(256 * h, 256 * h + 256)
            rim = before_ref if f == 0 else after_ref
            v = pp_ref[0, rows, :BP].astype(F32) + pp_ref[1, rows, :BP].astype(F32)
            v = (v + rim[rows, :BP].astype(F32)).astype(BF)
            out = mm(matrix, v) * (1.0 / 27.0)
            pool_ref[f, rows, :] = out
            add_pair(m_ref, slice(None), out, out * out)


def moments_body(c_ref, p_ref, m_ref):
    m_ref[:, 0:BP] = p_ref[...]
    m_ref[:, BP:] = jnp.zeros((2, OUTER), F32)
    for f in range(2):
        for h in range(2):
            c = c_ref[f, 256 * h : 256 * h + 256, :]
            add_pair(m_ref, slice(BP, None), c, c * c)


def norm4_body(
    z_ref, c_ref, p_ref, sf_ref, s0, s1, s2, s3, nf_ref, nb_ref, w_ref, mid_ref, z5_ref, m_ref, sb_ref, *, voxels
):
    sb_ref[...] = total_of((s0, s1, s2, s3))
    matrix = two_matrix(False)
    sf, sb, nf, nb = sf_ref[:, :B0], sb_ref[...], nf_ref[:, :B0], nb_ref[...]
    for h in range(2):
        rows, outs = slice(256 * h, 256 * h + 256), slice(64 * h, 64 * h + 64)
        pool = direct = conv = 0.0
        for f in range(2):
            pool += silu(normed(p_ref[f, rows, :], sb[:, :BP], nb[:, :BP], voxels)[1])
            direct += silu(normed(z_ref[f, rows, BP : BP + B0], sf, nf, voxels)[1])
            conv += silu(normed(c_ref[f, rows, :], sb[:, BP:], nb[:, BP:], voxels)[1])
        mid_ref[outs, :BP] = exact(matrix, pool).astype(BF)
        mid_ref[outs, BP : BP + B0] = exact(matrix, direct).astype(BF)
        mid_ref[outs, BP + B0 :] = exact(matrix, conv).astype(BF)
    z5 = mm(mid_ref[...], w_ref[...], NT)
    z5_ref[...] = z5
    m_ref[...] = jnp.zeros_like(m_ref)
    add_pair(m_ref, slice(None), z5[:, BP:], z5[:, BP:] * z5[:, BP:])


def act5_body(me_ref, z_ref, s0, s1, s2, s3, n_ref, send_ref, s_ref, *, voxels):
    s_ref[...] = total_of((s0, s1, s2, s3))
    _, y = normed(z_ref[:, BP + B0 :], s_ref[:, B0:], n_ref[:, B0:REDUCED], voxels)
    base = jnp.concatenate([silu(y), jnp.zeros((y.shape[0], 64), F32)], 1)
    pre = z_ref[:, :BP].astype(BF)
    c, lane = iota((BP, 256), 0), iota((BP, 256), 1)
    at = lane - 128 - POOL_LANE
    for k in range(4):
        place = jnp.bitwise_xor(me_ref[0], k)
        pick = ones_where((at >= 0) & (at < 32) & (c == 32 * place + at))
        send_ref[k] = (base + mm(pre, pick)).astype(BF)


def join5_body(me_ref, r0, r1, r2, r3, a_ref, pool_ref, pre):
    pre[0] = jnp.zeros((128, 128), F32)
    pre[5] = jnp.zeros((128, 128), F32)
    for k, r in enumerate((r0, r1, r2, r3)):
        place = jnp.bitwise_xor(me_ref[0], k)
        a_ref[place] = r[:, :INNER]
        pre[place + 1] = r[:, 128:].astype(F32)
    matrix = pool_matrix(128, 4)
    lane = iota((128, 128), 1)
    ok = (lane >= POOL_LANE) & (lane < POOL_LANE + 32)
    for f in range(4):
        v = (pre[f] + pre[f + 1] + pre[f + 2]).astype(BF)
        pool_ref[f] = jnp.where(ok, mm(matrix, v) * (1.0 / 27.0), 0.0)


def moments5_body(c_ref, p_ref, m_ref):
    m_ref[...] = jnp.zeros_like(m_ref)
    for f in range(4):
        c, p = c_ref[f], p_ref[f]
        add_pair(m_ref, slice(0, 128), c, c * c)
        add_pair(m_ref, slice(128, 256), p, p * p)


def cot5_body(me_ref, cot_ref, out_ref):
    for k in range(4):
        pick = own_columns(jnp.bitwise_xor(me_ref[0], k))
        out_ref[k] = mm(cot_ref[...], pick).astype(BF)


def norm5_body(me_ref, c_ref, p_ref, s_ref, n_ref, g0, g1, g2, g3, feat_ref, dy_ref, x_ref, *, voxels):
    x_ref[...] = jnp.zeros_like(x_ref)
    feat_ref[...] = jnp.zeros_like(feat_ref)
    for k, g in enumerate((g0, g1, g2, g3)):
        place = jnp.bitwise_xor(me_ref[0], k)
        for src, lanes in ((c_ref, slice(0, 128)), (p_ref, slice(128, 256))):
            scaled, y = normed(src[place], s_ref[:, lanes], n_ref[:, lanes], voxels)
            sigmoid = lax.logistic(y)
            value = (y * sigmoid).astype(BF)
            for j in range(4):
                at = slice(256 * j + lanes.start, 256 * j + lanes.stop)
                feat_ref[k, 0:32, at] = value[32 * j : 32 * j + 32]
            dy = g[:, lanes].astype(F32) * (sigmoid * (1.0 + y * (1.0 - sigmoid)))
            dy_ref[place, :, lanes] = dy
            add_pair(x_ref, lanes, dy, dy * scaled)


def back5_body(c_ref, p_ref, s_ref, n_ref, dy_ref, b_ref, dv_ref, turned_ref, u_ref, *, voxels):
    matrix, turn = pool_matrix(128, 4), turn_matrix(128, 16)
    parts = []
    for f in range(4):
        for src, lanes in ((c_ref, slice(0, 128)), (p_ref, slice(128, 256))):
            dv = norm_back(
                dy_ref[f, :, lanes], src[f], s_ref[:, lanes], n_ref[:, lanes], b_ref[:, lanes],
                voxels,
            )
            if src is c_ref:
                dv_ref[f] = dv.astype(BF)
                turned_ref[3 - f] = mm(turn, dv.astype(BF)).astype(BF)
            else:
                parts.append(dv.astype(BF).astype(F32))
    for f in range(4):
        v = sum(parts[max(f - 1, 0) : f + 2]).astype(BF)
        u_ref[f] = mm(matrix, v) * (1.0 / 27.0)


def send5_body(me_ref, part_ref, u_ref, send_ref):
    turn = turn_matrix(128, 16)
    for k in range(4):
        place = jnp.bitwise_xor(me_ref[0], k)
        part = mm(turn, part_ref[3 - place].astype(BF))
        send_ref[k, :, :128] = part[:, :128].astype(BF)
        tail = jnp.concatenate([part[:, 128:], jnp.zeros((128, 64), F32)], 1)
        send_ref[k, :, 128:] = (tail + u_ref[place]).astype(BF)


def front_back5_body(me_ref, r0, r1, r2, r3, z_ref, s_ref, n_ref, cot_ref, b_ref, dy_ref, u_ref, x_ref, *, voxels):
    x_ref[...] = jnp.zeros_like(x_ref)
    inner = 0.0
    u = 0.0
    c, lane = iota((128, BP), 0) - POOL_LANE, iota((128, BP), 1)
    for k, r in enumerate((r0, r1, r2, r3)):
        place = jnp.bitwise_xor(me_ref[0], k)
        inner = inner + r[:, :INNER].astype(F32)
        u = u + mm(r[:, 128:], ones_where((c >= 0) & (c < 32) & (lane == 32 * place + c)))
    u_ref[...] = u.astype(BF)
    for lanes, grad in ((slice(0, B0), cot_ref[...].astype(F32)), (slice(B0, REDUCED), inner)):
        at = slice(BP + lanes.start, BP + lanes.stop)
        scaled, y = normed(z_ref[:, at], s_ref[:, lanes], n_ref[:, lanes], voxels)
        dy = grad * slope(y)
        dy_ref[:, lanes] = dy
        add_pair(x_ref, lanes, dy, dy * scaled)
    first = jnp.where(me_ref[1] == 0, 1.0, 0.0)
    x_ref[:, pl.ds(pl.multiple_of(512 + 256 * me_ref[0], 128), 256)] = b_ref[...] * first


def mid_back_body(
    dy_ref, z_ref, s_ref, n_ref, b0, b1, b2, b3, u_ref, w_ref, c_ref, p_ref, sb_ref, nb_ref,
    g_ref, gm_ref, x_ref, back_ref, *, voxels,
):
    back_ref[...] = total_of((b0, b1, b2, b3))
    g_ref[:, :BP] = u_ref[...]
    g_ref[:, BP:] = norm_back(
        dy_ref[...], z_ref[:, BP:], s_ref[...], n_ref[:, :REDUCED], back_ref[:, :REDUCED], voxels / 8
    ).astype(BF)
    gm = mm(g_ref[...], w_ref[...])
    gm_ref[...] = gm
    matrix = two_matrix(True)
    x_ref[...] = jnp.zeros_like(x_ref)
    for h in range(2):
        rows = slice(256 * h, 256 * h + 256)
        block = gm[64 * h : 64 * h + 64]
        for src, lanes, at in (
            (p_ref, slice(0, BP), slice(0, BP)),
            (c_ref, slice(BP, BP + OUTER), slice(BP + B0, LAYER)),
        ):
            up = exact(matrix, block[:, at])
            for f in range(2):
                scaled, y = normed(src[f, rows, :], sb_ref[:, lanes], nb_ref[:, lanes], voxels)
                dy = up * slope(y)
                add_pair(x_ref, lanes, dy, dy * scaled)


def front_rows(total, out_ref):
    gap = jnp.zeros((4, total.shape[1]), F32)
    for z in range(4):
        for q in range(4):
            entry, pool = BP + 112 * z + 28 * q, 32 * z + 8 * q
            block = [total[entry : entry + 28], gap, total[pool : pool + 8]]
            out_ref[q, z] = jnp.concatenate(block, 0).astype(BF)


def front_grad5_body(g_ref, mid_ref, out_ref):
    turned = g_ref[...].astype(F32).T.astype(BF)
    front_rows(mm(turned, mid_ref[...]), out_ref)


def branch_grad4_body(
    gm_ref, c_ref, p_ref, s_ref, n_ref, b0, b1, b2, b3, dv_ref, dp_ref, turned_ref, b_ref, *, voxels
):
    turn = turn_matrix(256, 64)
    b_ref[...] = total_of((b0, b1, b2, b3))
    matrix = two_matrix(True)
    for h in range(2):
        rows = slice(256 * h, 256 * h + 256)
        block = gm_ref[64 * h : 64 * h + 64, :]
        for src, dst, lanes, at in (
            (p_ref, dp_ref, slice(0, BP), slice(0, BP)),
            (c_ref, dv_ref, slice(BP, BP + OUTER), slice(BP + B0, LAYER)),
        ):
            up = exact(matrix, block[:, at])
            sums, norms, back = s_ref[:, lanes], n_ref[:, lanes], b_ref[:, lanes]
            for f in range(2):
                values = src[f, rows, :]
                _, y = normed(values, sums, norms, voxels)
                dv = norm_back(up * slope(y), values, sums, norms, back, voxels)
                dst[f, rows, :] = dv.astype(BF)
                if dst is dv_ref:
                    turned_ref[1 - f, rows, :] = mm(turn, dv.astype(BF)).astype(BF)


def put(out_ref, place, rows, lane, value):
    size = out_ref.shape[-1]
    done, width = 0, value.shape[1]
    while done < width:
        part, at = divmod(lane + done, size)
        step = min(width - done, size - at)
        out_ref[part, place, rows, at : at + step] = value[:, done : done + step].astype(BF)
        done += step


def taps_out(out_ref, t, grad, slots):
    places = len(slots)
    for z, slot in enumerate(slots):
        put(out_ref, slot, slice(0, 80), B1R * t, grad[80 * z : 80 * z + 80, :B1R])
        low = grad[80 * places + 32 * z : 80 * places + 32 * z + 32, B1R:INNER]
        put(out_ref, slot, slice(80, 96), B2R * t, low[:16])
        put(out_ref, slot, slice(80, 96), NARROW_AT + B2R * t, low[16:])


def wide_lanes(a):
    return jnp.concatenate([a.astype(F32), jnp.zeros((a.shape[0], 64), F32)], 1)


def kernel_grad4_body(me_ref, a_ref, before_ref, after_ref, dv_ref, out_ref, patches, turned):
    out_ref[...] = jnp.zeros_like(out_ref)
    for q, a in enumerate((before_ref[...], a_ref[0], a_ref[1], after_ref[...])):
        a = wide_lanes(a)
        for n in range(9):
            patches[q, :, 256 * n : 256 * n + 256] = shifted(a, 8, n // 3 - 1, n % 3 - 1).astype(BF)
    for f in range(2):
        turned[:, 512 * f : 512 * f + 512] = dv_ref[f].astype(F32).T.astype(BF)
    for t in range(TAPS):
        i, n = t // 9, t % 9
        window = patches[i : i + 2, :, 256 * n : 256 * n + 256].reshape(1024, 256)
        slots = [jnp.bitwise_xor(me_ref[0], z) for z in range(4)]
        taps_out(out_ref, t, mm(turned[...], window), slots)


def kernel_grad5_body(a_ref, dv_ref, out_ref, patches, turned):
    out_ref[...] = jnp.zeros_like(out_ref)
    for q in (0, 5):
        patches[q] = jnp.zeros(patches.shape[1:], BF)
    for q in range(4):
        a = wide_lanes(a_ref[q])
        for n in range(9):
            patches[q + 1, :, 256 * n : 256 * n + 256] = shifted(a, 4, n // 3 - 1, n % 3 - 1).astype(BF)
        turned[:, 128 * q : 128 * q + 128] = dv_ref[q].astype(F32).T.astype(BF)
    for t in range(TAPS):
        i, n = t // 9, t % 9
        window = patches[i : i + 4, :, 256 * n : 256 * n + 256].reshape(512, 256)
        taps_out(out_ref, t, mm(turned[...], window), [0])


def front_back4_body(
    gm_ref, z_ref, s_ref, n_ref, own_ref, before_ref, after_ref, dp_ref, dy_ref, u_ref, x_ref, *, voxels
):
    two, pool, turn = two_matrix(True), pool_matrix(256, 8), turn_matrix(256, 64)
    x_ref[...] = jnp.zeros_like(x_ref)
    for h in range(2):
        rows = slice(256 * h, 256 * h + 256)
        up = exact(two, gm_ref[64 * h : 64 * h + 64, BP : BP + B0])
        for f in range(2):
            rim = before_ref if f == 0 else after_ref
            v = dp_ref[0, rows, :].astype(F32) + dp_ref[1, rows, :].astype(F32)
            v = (v + rim[rows, :BP].astype(F32)).astype(BF)
            u_ref[f, rows, :] = (mm(pool, v) * (1.0 / 27.0)).astype(BF)
            inner = exact(turn, own_ref[1 - f, rows, :] + rim[rows, BP:].astype(F32))
            for lanes, grad in ((slice(0, B0), up), (slice(B0, REDUCED), inner)):
                at = slice(BP + lanes.start, BP + lanes.stop)
                scaled, y = normed(z_ref[f, rows, at], s_ref[:, lanes], n_ref[:, lanes], voxels)
                dy = grad * slope(y)
                dy_ref[f, rows, lanes] = dy
                add_pair(x_ref, lanes, dy, dy * scaled)


def front_grad4_body(z_ref, s_ref, n_ref, dy_ref, b0, b1, b2, b3, u_ref, x_ref, g_ref, out_ref, b_ref, *, voxels):
    b_ref[...] = total_of((b0, b1, b2, b3))
    total = 0.0
    for f in range(2):
        for h in range(2):
            rows = slice(256 * h, 256 * h + 256)
            g_ref[f, rows, :BP] = u_ref[f, rows, :]
            g_ref[f, rows, BP:] = norm_back(
                dy_ref[f, rows, :], z_ref[f, rows, BP:], s_ref[...], n_ref[...], b_ref[...], voxels
            ).astype(BF)
        turned = g_ref[f].astype(F32).T.astype(BF)
        total = total + mm(turned, x_ref[:, f].reshape(512, x_ref.shape[3]))
    front_rows(total, out_ref)


def clips_grad_body(g_ref, w_ref, out_ref):
    for f in range(2):
        for h in range(2):
            grad = mm(g_ref[f, 256 * h : 256 * h + 256, :], w_ref[...])
            out_ref[4 * h : 4 * h + 4, f] = grad.reshape(4, 64, out_ref.shape[3])


def lines(buf, first, count, starts, width):
    out = []
    for r in range(4):
        rows = pl.ds(first + r, count, stride=4)
        part = []
        for at in starts:
            tiles = [buf[at + n, rows, :] for n in range(-(-width // 128))]
            part.append(jnp.concatenate(tiles, 1)[:, :width])
        out.append(jnp.concatenate(part, 0) if len(part) > 1 else part[0])
    return jnp.concatenate(out, 1)


def rows_body(both_ref, wide_ref, narrow_ref, buf):
    wide, narrow = [], []
    for t in range(2):
        for q in range(4):
            for n in range(9):
                buf[9 * q + n] = both_ref[t, q, :, 128 * n : 128 * (n + 1)].astype(F32)
        wide.append(lines(buf, 0, 20, (0,), TAPS * B1R))
        narrow.append(lines(buf, 80, 4, (0, NARROW_AT // 128), TAPS * B2R))
    for pair, out_ref in ((wide, wide_ref), (narrow, narrow_ref)):
        count, size = pair[0].shape
        for n in range(count):
            rows = [part[n : n + 1] for part in pair]
            out_ref[:, size * n : size * (n + 1)] = jnp.concatenate(rows, 0)


def features_body(me_ref, z_ref, s_ref, n_ref, r0, r1, r2, r3, out_ref, *, voxels):
    rest = 0.0
    for k, r in enumerate((r0, r1, r2, r3)):
        block = jnp.concatenate([r[0:32, 256 * j : 256 * (j + 1)] for j in range(4)], 0)
        rest = rest + mm(block, own_columns(jnp.bitwise_xor(me_ref[0], k), True))
    _, y = normed(z_ref[:, BP : BP + B0], s_ref[:, :B0], n_ref[:, :B0], voxels)
    out_ref[:, :B0] = silu(y)
    out_ref[:, B0:] = rest[:, B0:]


def xor_pairs(axis, step):
    return [(i, i ^ step) for i in range(lax.axis_size(axis))]


def tower_steps():
    steps, step = [], 1
    while step < lax.axis_size("dp") // 2:
        steps.append(step)
        step *= 2
    return steps


def other_tower(value):
    return lax.ppermute(value, "dp", xor_pairs("dp", lax.axis_size("dp") // 2))


def blk_peers(value):
    count = lax.axis_size("blk")
    return [value] + [lax.ppermute(value, "blk", xor_pairs("blk", k)) for k in range(1, count)]


def by_place(parts):
    me, step = lax.axis_index("blk"), 1
    while step < len(parts):
        hit = (me & step) != 0
        parts = [jnp.where(hit, parts[k ^ step], parts[k]) for k in range(len(parts))]
        step *= 2
    return parts


def swap_blk(mine):
    return [mine[0]] + [
        lax.ppermute(mine[k], "blk", xor_pairs("blk", k)) for k in range(1, lax.axis_size("blk"))
    ]


def dp_sum(value):
    for step in tower_steps():
        value = value + lax.ppermute(value, "dp", xor_pairs("dp", step))
    return value


def tower_parts(value):
    return blk_peers(dp_sum(value))


def gather_pieces(shard):
    rows = shard.shape[0] // 2
    odd = lax.axis_index("dp") % 2
    half = lax.dynamic_slice_in_dim(shard, odd * rows, rows, 0)
    mine = blk_peers(half)[1:]
    twins = [lax.ppermute(piece, "dp", xor_pairs("dp", 1)) for piece in mine]
    return [shard] + mine + twins


def fours():
    return [list(range(i, i + 4)) for i in range(0, lax.axis_size("dp"), 4)]


def scatter_four(value):
    value = lax.psum_scatter(
        value, "dp", scatter_dimension=0, axis_index_groups=fours(), tiled=False
    )
    for step in tower_steps()[2:]:
        got = lax.ppermute(value, "dp", xor_pairs("dp", step))
        value = (value.astype(F32) + got.astype(F32)).astype(BF)
    return value


def gather_eight(value):
    half = lax.axis_size("dp") // 2
    groups = [
        [b + i for i in range(4)] + [half + b + i for i in range(4)] for b in range(0, half, 4)
    ]
    return lax.all_gather(value, "dp", axis_index_groups=groups, tiled=False)


def spread_square(value):
    half = lax.axis_size("dp") // 2
    dp = lax.axis_index("dp")
    side = lax.ppermute(value, "dp", xor_pairs("dp", 2))
    other = other_tower(value)
    corner = jnp.concatenate(
        [
            lax.ppermute(other[:48], "dp", xor_pairs("dp", 2)),
            other_tower(side[48:]),
        ]
    )
    right = dp // 2 % 2 == 1
    ours = jnp.where(right, jnp.stack([side, value]), jnp.stack([value, side]))
    theirs = jnp.where(right, jnp.stack([corner, other]), jnp.stack([other, corner]))
    both = jnp.where(dp // half == 0, jnp.stack([ours, theirs]), jnp.stack([theirs, ours]))
    twin = lax.ppermute(both, "dp", xor_pairs("dp", 1))
    pair = jnp.where(dp % 2 == 0, jnp.stack([both, twin], 2), jnp.stack([twin, both], 2))
    return pair.reshape(2, 4, *value.shape)


def after(values, first):
    values, _ = lax.optimization_barrier((values, first))
    return values


def rim_swap(first, last):
    count = lax.axis_size("blk")
    ahead = [(i, i + 1) for i in range(count - 1)]
    back = [(i + 1, i) for i in range(count - 1)]
    return lax.ppermute(last, "blk", ahead), lax.ppermute(first, "blk", back)


def step_rows(value, axis, step):
    if step in tower_steps()[:2]:
        rows = value.shape[axis] // 2
        high = (lax.axis_index("dp") & step) != 0
        keep = lax.dynamic_slice_in_dim(value, jnp.where(high, rows, 0), rows, axis)
        give = lax.dynamic_slice_in_dim(value, jnp.where(high, 0, rows), rows, axis)
    else:
        keep = give = value
    got = lax.ppermute(give, "dp", xor_pairs("dp", step))
    return (keep.astype(F32) + got.astype(F32)).astype(BF)


def reduce_rows(value, axis, steps=None):
    for step in tower_steps() if steps is None else steps:
        value = step_rows(value, axis, step)
    return value


def reduce_blk(value):
    count = value.shape[0]
    got = swap_blk(by_place([value[j] for j in range(count)]))
    total = got[0].astype(F32)
    for piece in got[1:]:
        total = total + piece.astype(F32)
    return total.astype(BF)


def spread_rows(value):
    stream = lax.axis_index("dp") // (lax.axis_size("dp") // 2)
    other = other_tower(value)
    both = jnp.where(stream == 0, jnp.stack([value, other]), jnp.stack([other, value]))
    for step in (2, 1):
        got = lax.ppermute(both, "dp", xor_pairs("dp", step))
        high = (lax.axis_index("dp") & step) != 0
        both = jnp.where(
            high, jnp.concatenate([got, both], 1), jnp.concatenate([both, got], 1)
        )
    return both


def branch_rows(both):
    return call(
        rows_body,
        (shape_of((2, 80 * TAPS * B1R)), shape_of((2, 32 * TAPS * B2R))),
        both,
        micros=3, mib=16, scratch=[pltpu.VMEM((36, 96, 128), F32)],
    )


def pick_row(param, stream):
    size = param.shape[1]
    return lax.dynamic_index_in_dim(param.reshape(2, size // 128, 128), stream, 0, keepdims=False)


def on_device(clips, cotangent, *params):
    groups = lax.axis_size("dp")
    count = lax.axis_size("blk")
    stream = lax.axis_index("dp") // (groups // 2)
    place = lax.axis_index("blk")
    index = lax.axis_index("dp")
    me = jnp.stack([place, index % (groups // 2), index % 2, index // 2 % 2]).astype(jnp.int32)
    own = [pick_row(p, stream) for p in params]
    early, late = own[:6], own[6:]
    n, frames, height, breadth, c_first = clips.shape
    voxels = groups // 2 * count * n * frames * height * breadth
    late_voxels = voxels // 8
    x = clips.reshape(n, frames, height * breadth, c_first)
    e, p = REDUCED // count, BP // count
    g = (REDUCED + OUTER + BP) // count

    def pack_front(layer, c, turn=0):
        norms = jnp.concatenate([layer[4].reshape(-1), layer[5].reshape(-1)])
        row = jnp.pad(norms, (0, c - 2 * g)).reshape(1, c)
        rows = jnp.concatenate([layer[0].reshape(e, c), layer[3].reshape(p, c)])
        if turn:
            rows = jnp.concatenate([rows[:, c - turn :], rows[:, : c - turn]], 1)
        return jnp.pad(jnp.concatenate([rows, row]), ((0, 160 - e - p - 1), (0, 0)))

    def pack_branch(layer):
        wide = layer[1].reshape(80, -1)
        narrow = layer[2].reshape(32, -1)
        gap = jnp.zeros((16, NARROW_AT - narrow.shape[1]), BF)
        low = jnp.concatenate([narrow[:16], gap, narrow[16:]], 1)
        low = jnp.pad(low, ((0, 0), (0, wide.shape[1] - low.shape[1])))
        return jnp.concatenate([wide, low])

    packed = lax.dynamic_slice_in_dim(pack_branch(early), index % 2 * 48, 48, 0)
    pieces = gather_pieces(pack_front(after(early, packed), c_first))
    late_front = lax.dynamic_slice_in_dim(pack_front(late, LAYER, BP), index % 2 * 80, 80, 0)
    late_front = late_front.reshape(5, 16, LAYER).transpose(1, 0, 2).reshape(16, 5 * LAYER)
    late_front = jnp.pad(late_front, ((0, 0), (0, packed.shape[1] - 5 * LAYER)))
    packed = jnp.concatenate([packed, late_front])
    packed = lax.all_gather(packed, "blk", tiled=False)
    late = after(late, pieces[0])
    taps_5 = call(kernels5_body, shape_of((TAPS, 128, INNER), BF), pack_branch(late), micros=2)
    x = after(x, taps_5)
    z, m, front_4, nf4, nb4 = call(
        front4_body,
        (
            shape_of((2, 512, 576)), shape_of((2, REDUCED)), shape_of((576, c_first), BF),
            shape_of((2, REDUCED)), shape_of((2, 576)),
        ),
        me, x, *pieces, micros=0,
        scratch=[pltpu.VMEM((4, 160, c_first), BF), pltpu.VMEM((2, 1024), F32)],
    )
    late, cotangent = after((late, cotangent), m)
    cot = cotangent.reshape(128, LAYER)
    cot_mine = call(cot5_body, shape_of((4, 128, 256), BF), me, cot, micros=2)

    def conv(values, kernel, pads, order):
        return lax.conv_general_dilated(
            values,
            kernel.reshape(-1, 3, 3, *kernel.shape[1:]),
            (1, 1, 1),
            pads,
            dimension_numbers=("DNHWC", order, "DNHWC"),
            preferred_element_type=F32,
        )

    forth, back = "DHWOI", "DHWIO"
    flat_pads = ((0, 0), (1, 1), (1, 1))
    same = ((1, 1), (1, 1), (1, 1))
    at4 = functools.partial(functools.partial, voxels=voxels)
    at5 = functools.partial(functools.partial, voxels=late_voxels)

    parts = tower_parts(m)
    z_then = after(z, cot_mine)
    a, rims, sf4 = call(
        at4(act4_body),
        (shape_of((2, 512, INNER), BF), shape_of((2, 512, BP + INNER), BF), shape_of((2, REDUCED))),
        z_then, *parts, nf4, micros=0,
    )
    before, behind = rim_swap(rims[0], rims[1])
    packed = after(packed, a)
    twin = lax.ppermute(packed, "dp", xor_pairs("dp", 1))
    taps_4, taps_first, taps_last = call(
        kernels4_body,
        (
            shape_of((TAPS, OUTER, INNER), BF),
            shape_of((9, OUTER, INNER), BF), shape_of((9, OUTER, INNER), BF),
        ),
        me, packed, twin, micros=5, mib=12, away=(1, 2),
        scratch=[pltpu.VMEM((4, 96, 4320), BF), pltpu.SemaphoreType.DMA((2,))],
    )
    before, behind = after((before, behind), taps_4)
    pool, m_pool = call(
        pool4_body, (shape_of((2, 512, BP)), shape_of((2, BP))), rims, before, behind, micros=2
    )
    before, behind = before[:, BP:], behind[:, BP:]
    a_pad = jnp.concatenate([before[None], a, behind[None]]).reshape(4, n, height, breadth, INNER)
    c = conv(a_pad, taps_4, flat_pads, forth).reshape(2, 512, OUTER)
    front_5, n5f, n5 = call(
        front5_body,
        (shape_of((576, LAYER), BF), shape_of((2, 1024)), shape_of((2, 256))),
        me, packed, twin, micros=1, scratch=[pltpu.VMEM((4, 160, LAYER), BF)],
    )
    cots = swap_blk([after(cot_mine, c)[k] for k in range(4)])
    parts = tower_parts(call(moments_body, shape_of((2, 576)), c, m_pool, micros=1))

    mid, z5, m, sb4 = call(
        at4(norm4_body),
        (shape_of((128, LAYER), BF), shape_of((128, 576)), shape_of((2, REDUCED)), shape_of((2, 576))),
        z, c, pool, sf4, *parts, nf4, nb4, front_5, micros=4, lazy=(0, 2, 3, 8, 9, 10),
    )
    send, sf5 = call(
        at5(act5_body),
        (shape_of((4, 128, 256), BF), shape_of((2, REDUCED))),
        me, z5, *tower_parts(m), n5f, micros=1,
    )
    a5, pool5 = call(
        join5_body,
        (shape_of((4, 128, INNER), BF), shape_of((4, 128, 128))),
        me, *swap_blk([send[k] for k in range(4)]),
        micros=1, scratch=[pltpu.VMEM((6, 128, 128), F32)],
    )
    small = (4, n, height // 2, breadth // 2, -1)
    c5 = conv(a5.reshape(small), taps_5, same, forth).reshape(4, 128, 128)
    s5 = dp_sum(call(moments5_body, shape_of((2, 256)), c5, pool5, micros=1))
    feat, dy5, m = call(
        at5(norm5_body),
        (shape_of((4, 40, 1024), BF), shape_of((4, 128, 256)), shape_of((2, 256))),
        me, c5, pool5, s5, n5, *cots, micros=1, lazy=(2, 4, 5, 6, 7, 8),
    )

    b5 = dp_sum(m)
    dv5, turned5, u5 = call(
        at5(back5_body),
        (shape_of((4, 128, 128), BF), shape_of((4, 128, 128), BF), shape_of((4, 128, 128))),
        c5, pool5, s5, n5, dy5, b5, micros=1, lazy=(0, 1, 2, 3, 4),
    )
    part = conv(turned5.reshape(small), taps_5, same, back).reshape(4, 128, INNER)
    send = call(send5_body, shape_of((4, 128, 256), BF), me, part, u5, micros=1)
    dv5 = after(dv5, send)
    branch_part5 = call(
        kernel_grad5_body,
        shape_of((4, 1, 96, 1152), BF),
        a5, dv5,
        micros=2, mib=16,
        scratch=[pltpu.VMEM((6, 128, 2304), BF), pltpu.VMEM((128, 512), BF)],
    )
    z5 = after(z5, branch_part5)
    branch_5 = scatter_four(branch_part5)
    dyf5, u5, m = call(
        at5(front_back5_body),
        (shape_of((128, REDUCED)), shape_of((128, BP), BF), shape_of((2, 1536))),
        me, *swap_blk([send[k] for k in range(4)]), z5, sf5, n5f, cot[:, :B0], b5, micros=1,
        lazy=(5, 6, 7, 8, 9),
    )
    parts = tower_parts(m)
    g5, gm, m, back5 = call(
        at4(mid_back_body),
        (shape_of((128, 576), BF), shape_of((128, LAYER)), shape_of((2, 576)), shape_of((2, 1536))),
        dyf5, z5, sf5, n5f, *parts, u5, front_5, c, pool, sb4, nb4, micros=4,
        lazy=(0, 1, 2, 3, 8, 9, 10, 11, 12, 13),
    )

    parts = tower_parts(m)
    front_part5 = call(
        front_grad5_body, shape_of((4, 4, 40, LAYER), BF), after(g5, parts[0]), mid, micros=1
    )
    front_part5 = jnp.concatenate([front_part5[..., BP:], front_part5[..., :BP]], 3)
    front_5_sum = step_rows(front_part5, 0, 1)
    gm = after(gm, front_5_sum)
    both5 = gather_eight(after(branch_5, parts[0])[0]).reshape(2, 4, 96, 1152)
    dv, dp, turned4, bb4 = call(
        at4(branch_grad4_body),
        (
            shape_of((2, 512, OUTER), BF), shape_of((2, 512, BP), BF),
            shape_of((2, 512, OUTER), BF), shape_of((2, 576)),
        ),
        gm, c, pool, sb4, nb4, *parts, micros=3, lazy=(0, 1, 2, 3, 4),
    )
    image = (1, n, height, breadth, OUTER)
    rim_first = conv(turned4[1].reshape(image), taps_first, flat_pads, back).reshape(512, INNER)
    rim_last = conv(turned4[0].reshape(image), taps_last, flat_pads, back).reshape(512, INNER)
    rim_first = jnp.concatenate([dp[0], rim_first.astype(BF)], 1)
    rim_last = jnp.concatenate([dp[1], rim_last.astype(BF)], 1)
    got_before, got_after = rim_swap(rim_first, rim_last)
    branch_part4 = call(
        kernel_grad4_body,
        shape_of((4, 4, 96, 1152), BF),
        me, a, before, behind, after(dv, (rim_first, rim_last)),
        micros=8, mib=20,
        scratch=[pltpu.VMEM((4, 512, 2304), BF), pltpu.VMEM((OUTER, 1024), BF)],
    )
    turned4 = after(turned4, (branch_part4, both5))
    branch_part4 = scatter_four(branch_part4)
    front_5_sum = reduce_rows(front_5_sum, 0, tower_steps()[1:])[0]
    inner = conv(turned4.reshape(2, n, height, breadth, OUTER), taps_4, same, back)
    dyf4, u4, m = call(
        at4(front_back4_body),
        (shape_of((2, 512, REDUCED)), shape_of((2, 512, BP), BF), shape_of((2, REDUCED))),
        gm, z, sf4, nf4, inner.reshape(2, 512, INNER), got_before, got_after, dp, micros=4,
        lazy=(0, 1, 2, 3, 5, 6, 7),
    )
    parts = tower_parts(m)
    branch_4 = after(branch_part4, parts[3])
    wide_5, narrow_5 = branch_rows(both5)
    z = after(z, (front_5_sum, wide_5, narrow_5))
    g4, front_part4, bf4 = call(
        at4(front_grad4_body),
        (shape_of((2, 512, 576), BF), shape_of((4, 4, 40, c_first), BF), shape_of((2, REDUCED))),
        z, sf4, nf4, dyf4, *parts, u4, x, micros=4, lazy=(1, 2),
    )
    clips_grad = call(
        clips_grad_body, shape_of((n, frames, height * breadth, c_first)), g4, front_4, micros=3
    ).reshape(clips.shape)

    def front_out(both):
        both = both.astype(F32)
        return both[:, :, :28].reshape(2, -1), both[:, :, 32:].reshape(2, -1)

    branch_4 = sum(piece.astype(F32) for piece in swap_blk([branch_4[k] for k in range(4)])).astype(BF)
    fronts = reduce_rows(front_part4, 0)[0]
    fronts = jnp.concatenate([fronts, jnp.zeros((4, 40, 48), BF), front_5_sum], 2)
    fronts = by_place([after(fronts, branch_4)[j] for j in range(count)])
    fronts = sum(piece.astype(F32) for piece in swap_blk(fronts)).astype(BF)
    feat = after(feat, fronts)
    got = swap_blk([feat[k] for k in range(4)])
    fronts = spread_rows(fronts[None])
    wide_4, narrow_4 = branch_rows(spread_square(branch_4))
    entry_4, poolproj_4 = front_out(fronts[..., :c_first])
    entry_5, poolproj_5 = front_out(fronts[..., c_first + 48 :])

    features = call(
        at5(features_body), shape_of((128, LAYER)), me, z5, sf5, n5f, *got, micros=2
    ).reshape(cotangent.shape)

    all5 = back5[:, 512:].reshape(2, count, 256)
    norms4 = jnp.concatenate([bf4, bb4[:, BP:], bb4[:, :BP]], 1)
    norms5 = jnp.concatenate(
        [
            back5[:, :REDUCED],
            all5[:, :, :80].reshape(2, -1),
            all5[:, :, 80:112].reshape(2, -1),
            all5[:, :, 128 + POOL_LANE : 160 + POOL_LANE].reshape(2, -1),
        ],
        axis=1,
    )
    norms = jnp.stack([norms4, norms5])
    theirs = other_tower(norms)
    norms = jnp.where(stream == 0, jnp.stack([norms, theirs]), jnp.stack([theirs, norms]))
    norms = lax.dynamic_slice_in_dim(norms, place * g, g, 3)
    return (
        features, clips_grad,
        entry_4, wide_4, narrow_4, poolproj_4, norms[:, 0, 1], norms[:, 0, 0],
        entry_5, wide_5, narrow_5, poolproj_5, norms[:, 1, 1], norms[:, 1, 0],
    )


def solution(mesh):
    spec = P("dp", "blk", None, None, None)
    flat = P(None, "blk")
    return jax.shard_map(
        on_device,
        mesh=mesh,
        in_specs=(spec, spec) + (flat,) * 12,
        out_specs=(spec, spec) + (flat,) * 12,
        check_vma=False,
    )
```

```python
import functools

import jax
import jax.numpy as jnp
from jax import lax
from jax.experimental import pallas as pl
from jax.experimental.pallas import tpu as pltpu
from jax.sharding import PartitionSpec as P

B0 = 256
B1R = 160
B1 = 320
B2R = 32
B2 = 128
BP = 128
INNER = B1R + B2R
REDUCED = B0 + INNER
OUTER = B1 + B2
LAYER = B0 + OUTER + BP
EPS = 1e-05
BF = jnp.bfloat16
F32 = jnp.float32
TAPS = 27
NARROW_AT = 896
POOL_LANE = 64

NT = (((1,), (1,)), ((), ()))
NN = (((1,), (0,)), ((), ()))
VMEM = pl.BlockSpec(memory_space=pltpu.VMEM)
SMEM = pl.BlockSpec(memory_space=pltpu.SMEM)


def mm(a, b, dims=NN):
    return lax.dot_general(a, b, dims, preferred_element_type=F32)


def shape_of(shape, kind=F32):
    return jax.ShapeDtypeStruct(shape, kind)


def call(body, outs, *args, micros=2, scratch=(), mib=6, lazy=(), away=()):
    def whole(*refs):
        bufs, sems = refs[len(refs) - len(lazy) - 1 : -1], refs[-1]
        copies = [
            pltpu.make_async_copy(refs[i], bufs[n], sems.at[n]) for n, i in enumerate(lazy)
        ]
        for copy in copies:
            copy.start()
        for copy in copies:
            copy.wait()
        ins = list(refs[: len(args)])
        for n, i in enumerate(lazy):
            ins[i] = bufs[n]
        body(*ins, *refs[len(args) : len(refs) - len(lazy) - 1])

    lazy = [i % len(args) for i in lazy]
    specs = [SMEM if a.dtype == jnp.int32 else VMEM for a in args]
    scratch, size = list(scratch), 0
    for i in lazy:
        specs[i] = pl.BlockSpec(memory_space=pl.ANY)
        scratch.append(pltpu.VMEM(args[i].shape, args[i].dtype))
        size += args[i].size * args[i].dtype.itemsize
    if lazy:
        scratch.append(pltpu.SemaphoreType.DMA((len(lazy),)))
    spots = [VMEM] * (len(outs) if isinstance(outs, tuple) else 1)
    for i in away:
        spots[i] = pl.BlockSpec(memory_space=pltpu.HBM)
    return pl.pallas_call(
        whole if lazy else body,
        out_shape=outs,
        in_specs=specs,
        out_specs=spots if isinstance(outs, tuple) else spots[0],
        scratch_shapes=scratch,
        compiler_params=pltpu.CompilerParams(vmem_limit_bytes=(mib << 20) + 5 * size // 4),
        cost_estimate=pl.CostEstimate(
            flops=int(micros * 1.0e9), bytes_accessed=1 << 20 if micros else 0, transcendentals=0
        ),
    )(*args)


def iota(shape, axis):
    return lax.broadcasted_iota(jnp.int32, shape, axis)


def ones_where(ok, value=1.0):
    return jnp.where(ok, value, 0.0).astype(BF)


def pool_matrix(n, side):
    r, c = iota((n, n), 0), iota((n, n), 1)
    area = side * side
    near_w = jnp.abs(r % side - c % side) <= 1
    near_h = jnp.abs((r // side) % side - (c // side) % side) <= 1
    return ones_where((r // area == c // area) & near_w & near_h)


def turn_matrix(n, area):
    r, c = iota((n, n), 0), iota((n, n), 1)
    return ones_where((r // area == c // area) & (r % area + c % area == area - 1))


def two_matrix(transposed):
    shape = (256, 64) if transposed else (64, 256)
    big, small = (iota(shape, 0), iota(shape, 1)) if transposed else (iota(shape, 1), iota(shape, 0))
    ok = (small // 16 == big // 64) & ((small // 4) % 4 == (big // 16) % 4)
    return ones_where(ok & (small % 4 == (big // 2) % 4), 0.125)


def exact(matrix, values):
    high = values.astype(BF)
    low = (values - high.astype(F32)).astype(BF)
    return mm(matrix, high) + mm(matrix, low)


def own_columns(place, transposed=False):
    shape = (256, LAYER) if transposed else (LAYER, 256)
    lane, col = (iota(shape, 0), iota(shape, 1)) if transposed else (iota(shape, 1), iota(shape, 0))
    wide = (lane < 80) & (col == B0 + 80 * place + lane)
    narrow = (lane >= 80) & (lane < 112) & (col == B0 + B1 + 32 * place + lane - 80)
    at = lane - 128 - POOL_LANE
    pool = (at >= 0) & (at < 32) & (col == B0 + OUTER + 32 * place + at)
    return ones_where(wide | narrow | pool)


def scaled_of(values, sums, voxels):
    centre = sums[0:1] * (1.0 / voxels)
    spread = lax.rsqrt(sums[1:2] * (1.0 / voxels) - centre * centre + EPS)
    return (values - centre) * spread, spread


def normed(values, sums, norms, voxels):
    scaled, _ = scaled_of(values, sums, voxels)
    return scaled, scaled * norms[0:1] + norms[1:2]


def silu(y):
    return y * lax.logistic(y)


def slope(y):
    sigmoid = lax.logistic(y)
    return sigmoid * (1.0 + y * (1.0 - sigmoid))


def norm_back(dy, values, sums, norms, back, voxels):
    scaled, spread = scaled_of(values, sums, voxels)
    scale = norms[0:1] * spread
    return scale * (dy - back[0:1] * (1.0 / voxels) - scaled * (back[1:2] * (1.0 / voxels)))


def add_pair(ref, lanes, first, second):
    ref[0:1, lanes] += jnp.sum(first, 0, keepdims=True)
    ref[1:2, lanes] += jnp.sum(second, 0, keepdims=True)


def shifted(a, side, j, k):
    if j == 0 and k == 0:
        return a
    rows, lanes = a.shape
    area = side * side
    r = iota((area, lanes), 0)
    w, h = r % side + k, r // side + j
    ok = (w >= 0) & (w < side) & (h >= 0) & (h < side)
    moved = pltpu.roll(a, (-(side * j + k)) % rows, 0).reshape(rows // area, area, lanes)
    return jnp.where(ok[None], moved, 0.0).reshape(rows, lanes)


def assemble(me_ref, pieces, buf):
    half = pieces[0].shape[0] // 2
    buf[me_ref[0]] = pieces[0][...]
    for k in range(1, 4):
        place = jnp.bitwise_xor(me_ref[0], k)
        buf[place, pl.ds(pl.multiple_of(half * me_ref[2], half), half), :] = pieces[k][...]
        buf[place, pl.ds(pl.multiple_of(half * (1 - me_ref[2]), half), half), :] = pieces[k + 3][...]


def tap_block(shards, t):
    wide, narrow = [], []
    for w in shards:
        wide.append(w[0:80, B1R * t : B1R * (t + 1)].astype(F32))
        for lane in (B2R * t, NARROW_AT + B2R * t):
            narrow.append(w[80:96, lane : lane + B2R].astype(F32))
    wide = jnp.concatenate(wide, 0)
    narrow = jnp.concatenate(narrow, 0)
    top = jnp.concatenate([wide, jnp.zeros((wide.shape[0], B2R), F32)], 1)
    low = jnp.concatenate([jnp.zeros((narrow.shape[0], B1R), F32), narrow], 1)
    return jnp.concatenate([top, low], 0).astype(BF)


def kernels4_body(me_ref, mine_ref, twin_ref, all_ref, first_ref, last_ref, buf, sems):
    first = pltpu.make_async_copy(all_ref.at[0:9], first_ref, sems.at[0])
    last = pltpu.make_async_copy(all_ref.at[18:27], last_ref, sems.at[1])
    buf[:, pl.ds(pl.multiple_of(48 * me_ref[2], 16), 48), :] = mine_ref[:, :48, :]
    buf[:, pl.ds(pl.multiple_of(48 * (1 - me_ref[2]), 16), 48), :] = twin_ref[:, :48, :]
    for t in range(TAPS):
        all_ref[t] = tap_block([buf.at[z] for z in range(4)], t)
        if t == 8:
            first.start()
    last.start()
    first.wait()
    last.wait()


def kernels5_body(w_ref, all_ref):
    for t in range(TAPS):
        all_ref[t] = jnp.concatenate([tap_block([w_ref], t), jnp.zeros((16, INNER), BF)], 0)


def front_parts(buf, matrix_ref, norms_ref):
    for z in range(4):
        matrix_ref[32 * z : 32 * (z + 1), :] = buf[z, 112:144, :]
        matrix_ref[BP + 112 * z : BP + 112 * (z + 1), :] = buf[z, 0:112, :]
        row = buf[z, 144:160, :].astype(F32)[0:1]
        norms_ref[0:1, 256 * z : 256 * (z + 1)] = row[:, :256]
        norms_ref[1:2, 256 * z : 256 * (z + 1)] = row[:, 256:512]


def total_of(parts):
    return (parts[0][...] + parts[1][...]) + (parts[2][...] + parts[3][...])


def front5_body(me_ref, mine_ref, twin_ref, w_ref, n_ref, own_ref, buf):
    for src, odd in ((mine_ref, me_ref[2]), (twin_ref, 1 - me_ref[2])):
        for j in range(5):
            rows = pl.ds(pl.multiple_of(80 * odd + 16 * j, 16), 16)
            buf[:, rows, :] = src[:, 48:64, LAYER * j : LAYER * (j + 1)]
    front_parts(buf, w_ref, n_ref)
    norms = n_ref[...]
    own = jnp.zeros((2, 256), F32)
    gap = jnp.zeros((2, 16 + POOL_LANE), F32)
    for z in range(4):
        wide = norms[:, REDUCED + 80 * z : REDUCED + 80 * (z + 1)]
        narrow = norms[:, REDUCED + B1 + 32 * z : REDUCED + B1 + 32 * (z + 1)]
        pool = norms[:, REDUCED + OUTER + 32 * z : REDUCED + OUTER + 32 * (z + 1)]
        block = jnp.concatenate([wide, narrow, gap, pool, jnp.zeros((2, 32), F32)], 1)
        own = jnp.where(me_ref[0] == z, block, own)
    own_ref[...] = own


def front4_body(me_ref, x_ref, p0, p1, p2, p3, t1, t2, t3, z_ref, m_ref, w_ref, nf_ref, nb_ref, buf, n_ref):
    assemble(me_ref, (p0, p1, p2, p3, t1, t2, t3), buf)
    front_parts(buf, w_ref, n_ref)
    nf_ref[...] = n_ref[:, :REDUCED]
    nb_ref[:, :BP] = n_ref[:, REDUCED + OUTER :]
    nb_ref[:, BP:] = n_ref[:, REDUCED : REDUCED + OUTER]
    m_ref[...] = jnp.zeros_like(m_ref)
    for f in range(2):
        for h in range(2):
            x = x_ref[4 * h : 4 * h + 4, f].reshape(256, x_ref.shape[3])
            z = mm(x, w_ref[...], NT)
            rows = slice(256 * h, 256 * h + 256)
            z_ref[f, rows, :] = z
            front = z[:, BP:]
            add_pair(m_ref, slice(None), front, front * front)


def act4_body(z_ref, s0, s1, s2, s3, n_ref, a_ref, rim_ref, s_ref, *, voxels):
    s_ref[...] = total_of((s0, s1, s2, s3))
    sums, norms = s_ref[:, B0:], n_ref[:, B0:]
    for f in range(2):
        for h in range(2):
            rows = slice(256 * h, 256 * h + 256)
            _, y = normed(z_ref[f, rows, BP + B0 :], sums, norms, voxels)
            a_ref[f, rows, :] = silu(y).astype(BF)
            rim_ref[f, rows, :BP] = z_ref[f, rows, :BP].astype(BF)
            rim_ref[f, rows, BP:] = silu(y).astype(BF)


def pool4_body(pp_ref, before_ref, after_ref, pool_ref, m_ref):
    matrix = pool_matrix(256, 8)
    m_ref[...] = jnp.zeros_like(m_ref)
    for f in range(2):
        for h in range(2):
            rows = slice(256 * h, 256 * h + 256)
            rim = before_ref if f == 0 else after_ref
            v = pp_ref[0, rows, :BP].astype(F32) + pp_ref[1, rows, :BP].astype(F32)
            v = (v + rim[rows, :BP].astype(F32)).astype(BF)
            out = mm(matrix, v) * (1.0 / 27.0)
            pool_ref[f, rows, :] = out
            add_pair(m_ref, slice(None), out, out * out)


def moments_body(c_ref, p_ref, m_ref):
    m_ref[:, 0:BP] = p_ref[...]
    m_ref[:, BP:] = jnp.zeros((2, OUTER), F32)
    for f in range(2):
        for h in range(2):
            c = c_ref[f, 256 * h : 256 * h + 256, :]
            add_pair(m_ref, slice(BP, None), c, c * c)


def norm4_body(
    z_ref, c_ref, p_ref, sf_ref, s0, s1, s2, s3, nf_ref, nb_ref, w_ref, mid_ref, z5_ref, m_ref, sb_ref, *, voxels
):
    sb_ref[...] = total_of((s0, s1, s2, s3))
    matrix = two_matrix(False)
    sf, sb, nf, nb = sf_ref[:, :B0], sb_ref[...], nf_ref[:, :B0], nb_ref[...]
    for h in range(2):
        rows, outs = slice(256 * h, 256 * h + 256), slice(64 * h, 64 * h + 64)
        pool = direct = conv = 0.0
        for f in range(2):
            pool += silu(normed(p_ref[f, rows, :], sb[:, :BP], nb[:, :BP], voxels)[1])
            direct += silu(normed(z_ref[f, rows, BP : BP + B0], sf, nf, voxels)[1])
            conv += silu(normed(c_ref[f, rows, :], sb[:, BP:], nb[:, BP:], voxels)[1])
        mid_ref[outs, :BP] = exact(matrix, pool).astype(BF)
        mid_ref[outs, BP : BP + B0] = exact(matrix, direct).astype(BF)
        mid_ref[outs, BP + B0 :] = exact(matrix, conv).astype(BF)
    z5 = mm(mid_ref[...], w_ref[...], NT)
    z5_ref[...] = z5
    m_ref[...] = jnp.zeros_like(m_ref)
    add_pair(m_ref, slice(None), z5[:, BP:], z5[:, BP:] * z5[:, BP:])


def act5_body(me_ref, z_ref, s0, s1, s2, s3, n_ref, send_ref, s_ref, *, voxels):
    s_ref[...] = total_of((s0, s1, s2, s3))
    _, y = normed(z_ref[:, BP + B0 :], s_ref[:, B0:], n_ref[:, B0:REDUCED], voxels)
    base = jnp.concatenate([silu(y), jnp.zeros((y.shape[0], 64), F32)], 1)
    pre = z_ref[:, :BP].astype(BF)
    c, lane = iota((BP, 256), 0), iota((BP, 256), 1)
    at = lane - 128 - POOL_LANE
    for k in range(4):
        place = jnp.bitwise_xor(me_ref[0], k)
        pick = ones_where((at >= 0) & (at < 32) & (c == 32 * place + at))
        send_ref[k] = (base + mm(pre, pick)).astype(BF)


def join5_body(me_ref, r0, r1, r2, r3, a_ref, pool_ref, pre):
    pre[0] = jnp.zeros((128, 128), F32)
    pre[5] = jnp.zeros((128, 128), F32)
    for k, r in enumerate((r0, r1, r2, r3)):
        place = jnp.bitwise_xor(me_ref[0], k)
        a_ref[place] = r[:, :INNER]
        pre[place + 1] = r[:, 128:].astype(F32)
    matrix = pool_matrix(128, 4)
    lane = iota((128, 128), 1)
    ok = (lane >= POOL_LANE) & (lane < POOL_LANE + 32)
    for f in range(4):
        v = (pre[f] + pre[f + 1] + pre[f + 2]).astype(BF)
        pool_ref[f] = jnp.where(ok, mm(matrix, v) * (1.0 / 27.0), 0.0)


def moments5_body(c_ref, p_ref, m_ref):
    m_ref[...] = jnp.zeros_like(m_ref)
    for f in range(4):
        c, p = c_ref[f], p_ref[f]
        add_pair(m_ref, slice(0, 128), c, c * c)
        add_pair(m_ref, slice(128, 256), p, p * p)


def cot5_body(me_ref, cot_ref, out_ref):
    for k in range(4):
        pick = own_columns(jnp.bitwise_xor(me_ref[0], k))
        out_ref[k] = mm(cot_ref[...], pick).astype(BF)


def norm5_body(me_ref, c_ref, p_ref, s_ref, n_ref, g0, g1, g2, g3, feat_ref, dy_ref, x_ref, *, voxels):
    x_ref[...] = jnp.zeros_like(x_ref)
    for k, g in enumerate((g0, g1, g2, g3)):
        place = jnp.bitwise_xor(me_ref[0], k)
        for src, lanes in ((c_ref, slice(0, 128)), (p_ref, slice(128, 256))):
            scaled, y = normed(src[place], s_ref[:, lanes], n_ref[:, lanes], voxels)
            sigmoid = lax.logistic(y)
            feat_ref[k, :, lanes] = (y * sigmoid).astype(BF)
            dy = g[:, lanes].astype(F32) * (sigmoid * (1.0 + y * (1.0 - sigmoid)))
            dy_ref[place, :, lanes] = dy
            add_pair(x_ref, lanes, dy, dy * scaled)


def back5_body(c_ref, p_ref, s_ref, n_ref, dy_ref, b_ref, dv_ref, turned_ref, u_ref, *, voxels):
    matrix, turn = pool_matrix(128, 4), turn_matrix(128, 16)
    parts = []
    for f in range(4):
        for src, lanes in ((c_ref, slice(0, 128)), (p_ref, slice(128, 256))):
            dv = norm_back(
                dy_ref[f, :, lanes], src[f], s_ref[:, lanes], n_ref[:, lanes], b_ref[:, lanes],
                voxels,
            )
            if src is c_ref:
                dv_ref[f] = dv.astype(BF)
                turned_ref[3 - f] = mm(turn, dv.astype(BF)).astype(BF)
            else:
                parts.append(dv.astype(BF).astype(F32))
    for f in range(4):
        v = sum(parts[max(f - 1, 0) : f + 2]).astype(BF)
        u_ref[f] = mm(matrix, v) * (1.0 / 27.0)


def send5_body(me_ref, part_ref, u_ref, send_ref):
    turn = turn_matrix(128, 16)
    for k in range(4):
        place = jnp.bitwise_xor(me_ref[0], k)
        part = mm(turn, part_ref[3 - place].astype(BF))
        send_ref[k, :, :128] = part[:, :128].astype(BF)
        tail = jnp.concatenate([part[:, 128:], jnp.zeros((128, 64), F32)], 1)
        send_ref[k, :, 128:] = (tail + u_ref[place]).astype(BF)


def front_back5_body(me_ref, r0, r1, r2, r3, z_ref, s_ref, n_ref, cot_ref, b_ref, dy_ref, u_ref, x_ref, *, voxels):
    x_ref[...] = jnp.zeros_like(x_ref)
    inner = 0.0
    u = 0.0
    c, lane = iota((128, BP), 0) - POOL_LANE, iota((128, BP), 1)
    for k, r in enumerate((r0, r1, r2, r3)):
        place = jnp.bitwise_xor(me_ref[0], k)
        inner = inner + r[:, :INNER].astype(F32)
        u = u + mm(r[:, 128:], ones_where((c >= 0) & (c < 32) & (lane == 32 * place + c)))
    u_ref[...] = u.astype(BF)
    for lanes, grad in ((slice(0, B0), cot_ref[...].astype(F32)), (slice(B0, REDUCED), inner)):
        at = slice(BP + lanes.start, BP + lanes.stop)
        scaled, y = normed(z_ref[:, at], s_ref[:, lanes], n_ref[:, lanes], voxels)
        dy = grad * slope(y)
        dy_ref[:, lanes] = dy
        add_pair(x_ref, lanes, dy, dy * scaled)
    first = jnp.where(me_ref[1] == 0, 1.0, 0.0)
    x_ref[:, pl.ds(pl.multiple_of(512 + 256 * me_ref[0], 128), 256)] = b_ref[...] * first


def mid_back_body(
    dy_ref, z_ref, s_ref, n_ref, b0, b1, b2, b3, u_ref, w_ref, c_ref, p_ref, sb_ref, nb_ref,
    g_ref, gm_ref, x_ref, back_ref, *, voxels,
):
    back_ref[...] = total_of((b0, b1, b2, b3))
    g_ref[:, :BP] = u_ref[...]
    g_ref[:, BP:] = norm_back(
        dy_ref[...], z_ref[:, BP:], s_ref[...], n_ref[:, :REDUCED], back_ref[:, :REDUCED], voxels / 8
    ).astype(BF)
    gm = mm(g_ref[...], w_ref[...])
    gm_ref[...] = gm
    matrix = two_matrix(True)
    x_ref[...] = jnp.zeros_like(x_ref)
    for h in range(2):
        rows = slice(256 * h, 256 * h + 256)
        block = gm[64 * h : 64 * h + 64]
        for src, lanes, at in (
            (p_ref, slice(0, BP), slice(0, BP)),
            (c_ref, slice(BP, BP + OUTER), slice(BP + B0, LAYER)),
        ):
            up = exact(matrix, block[:, at])
            for f in range(2):
                scaled, y = normed(src[f, rows, :], sb_ref[:, lanes], nb_ref[:, lanes], voxels)
                dy = up * slope(y)
                add_pair(x_ref, lanes, dy, dy * scaled)


def front_rows(total, out_ref):
    gap = jnp.zeros((4, total.shape[1]), F32)
    for z in range(4):
        for q in range(4):
            entry, pool = BP + 112 * z + 28 * q, 32 * z + 8 * q
            block = [total[entry : entry + 28], gap, total[pool : pool + 8]]
            out_ref[q, z] = jnp.concatenate(block, 0).astype(BF)


def front_grad5_body(g_ref, mid_ref, out_ref):
    turned = g_ref[...].astype(F32).T.astype(BF)
    front_rows(mm(turned, mid_ref[...]), out_ref)


def branch_grad4_body(
    gm_ref, c_ref, p_ref, s_ref, n_ref, b0, b1, b2, b3, dv_ref, dp_ref, turned_ref, b_ref, *, voxels
):
    turn = turn_matrix(256, 64)
    b_ref[...] = total_of((b0, b1, b2, b3))
    matrix = two_matrix(True)
    for h in range(2):
        rows = slice(256 * h, 256 * h + 256)
        block = gm_ref[64 * h : 64 * h + 64, :]
        for src, dst, lanes, at in (
            (p_ref, dp_ref, slice(0, BP), slice(0, BP)),
            (c_ref, dv_ref, slice(BP, BP + OUTER), slice(BP + B0, LAYER)),
        ):
            up = exact(matrix, block[:, at])
            sums, norms, back = s_ref[:, lanes], n_ref[:, lanes], b_ref[:, lanes]
            for f in range(2):
                values = src[f, rows, :]
                _, y = normed(values, sums, norms, voxels)
                dv = norm_back(up * slope(y), values, sums, norms, back, voxels)
                dst[f, rows, :] = dv.astype(BF)
                if dst is dv_ref:
                    turned_ref[1 - f, rows, :] = mm(turn, dv.astype(BF)).astype(BF)


def put(out_ref, place, rows, lane, value):
    size = out_ref.shape[-1]
    done, width = 0, value.shape[1]
    while done < width:
        part, at = divmod(lane + done, size)
        step = min(width - done, size - at)
        out_ref[part, place, rows, at : at + step] = value[:, done : done + step].astype(BF)
        done += step


def taps_out(out_ref, t, grad, slots):
    places = len(slots)
    for z, slot in enumerate(slots):
        put(out_ref, slot, slice(0, 80), B1R * t, grad[80 * z : 80 * z + 80, :B1R])
        low = grad[80 * places + 32 * z : 80 * places + 32 * z + 32, B1R:INNER]
        put(out_ref, slot, slice(80, 96), B2R * t, low[:16])
        put(out_ref, slot, slice(80, 96), NARROW_AT + B2R * t, low[16:])


def wide_lanes(a):
    return jnp.concatenate([a.astype(F32), jnp.zeros((a.shape[0], 64), F32)], 1)


def kernel_grad4_body(me_ref, a_ref, before_ref, after_ref, dv_ref, out_ref, patches, turned):
    out_ref[...] = jnp.zeros_like(out_ref)
    slots = [jnp.bitwise_xor(me_ref[0], z) for z in range(4)]
    for f in range(2):
        turned[:, 512 * f : 512 * f + 512] = dv_ref[f].astype(F32).T.astype(BF)
    for n in range(9):
        for q in range(4):
            a = before_ref[...] if q == 0 else after_ref[...] if q == 3 else a_ref[q - 1]
            patches[n % 2, q] = shifted(wide_lanes(a), 8, n // 3 - 1, n % 3 - 1).astype(BF)
        for i in range(3):
            window = patches[n % 2, i : i + 2].reshape(1024, 256)
            taps_out(out_ref, 9 * i + n, mm(turned[...], window), slots)


def kernel_grad5_body(a_ref, dv_ref, out_ref, patches, turned):
    out_ref[...] = jnp.zeros_like(out_ref)
    for q in (0, 5):
        patches[q] = jnp.zeros(patches.shape[1:], BF)
    for q in range(4):
        a = wide_lanes(a_ref[q])
        for n in range(9):
            patches[q + 1, :, 256 * n : 256 * n + 256] = shifted(a, 4, n // 3 - 1, n % 3 - 1).astype(BF)
        turned[:, 128 * q : 128 * q + 128] = dv_ref[q].astype(F32).T.astype(BF)
    for t in range(TAPS):
        i, n = t // 9, t % 9
        window = patches[i : i + 4, :, 256 * n : 256 * n + 256].reshape(512, 256)
        taps_out(out_ref, t, mm(turned[...], window), [0])


def front_back4_body(
    gm_ref, z_ref, s_ref, n_ref, own_ref, before_ref, after_ref, dp_ref, dy_ref, u_ref, x_ref, *, voxels
):
    two, pool, turn = two_matrix(True), pool_matrix(256, 8), turn_matrix(256, 64)
    x_ref[...] = jnp.zeros_like(x_ref)
    for h in range(2):
        rows = slice(256 * h, 256 * h + 256)
        up = exact(two, gm_ref[64 * h : 64 * h + 64, BP : BP + B0])
        for f in range(2):
            rim = before_ref if f == 0 else after_ref
            v = dp_ref[0, rows, :].astype(F32) + dp_ref[1, rows, :].astype(F32)
            v = (v + rim[rows, :BP].astype(F32)).astype(BF)
            u_ref[f, rows, :] = (mm(pool, v) * (1.0 / 27.0)).astype(BF)
            inner = exact(turn, own_ref[1 - f, rows, :] + rim[rows, BP:].astype(F32))
            for lanes, grad in ((slice(0, B0), up), (slice(B0, REDUCED), inner)):
                at = slice(BP + lanes.start, BP + lanes.stop)
                scaled, y = normed(z_ref[f, rows, at], s_ref[:, lanes], n_ref[:, lanes], voxels)
                dy = grad * slope(y)
                dy_ref[f, rows, lanes] = dy
                add_pair(x_ref, lanes, dy, dy * scaled)


def front_grad4_body(z_ref, s_ref, n_ref, dy_ref, b0, b1, b2, b3, u_ref, x_ref, g_ref, out_ref, b_ref, *, voxels):
    b_ref[...] = total_of((b0, b1, b2, b3))
    total = 0.0
    for f in range(2):
        for h in range(2):
            rows = slice(256 * h, 256 * h + 256)
            g_ref[f, rows, :BP] = u_ref[f, rows, :]
            g_ref[f, rows, BP:] = norm_back(
                dy_ref[f, rows, :], z_ref[f, rows, BP:], s_ref[...], n_ref[...], b_ref[...], voxels
            ).astype(BF)
        turned = g_ref[f].astype(F32).T.astype(BF)
        total = total + mm(turned, x_ref[:, f].reshape(512, x_ref.shape[3]))
    front_rows(total, out_ref)


def clips_grad_body(g_ref, w_ref, out_ref):
    for f in range(2):
        for h in range(2):
            grad = mm(g_ref[f, 256 * h : 256 * h + 256, :], w_ref[...])
            out_ref[4 * h : 4 * h + 4, f] = grad.reshape(4, 64, out_ref.shape[3])


def lines(buf, first, count, starts, width):
    out = []
    for r in range(4):
        rows = pl.ds(first + r, count, stride=4)
        part = []
        for at in starts:
            tiles = [buf[at + n, rows, :] for n in range(-(-width // 128))]
            part.append(jnp.concatenate(tiles, 1)[:, :width])
        out.append(jnp.concatenate(part, 0) if len(part) > 1 else part[0])
    return jnp.concatenate(out, 1)


def rows_body(me_ref, mine_ref, twin_ref, wide_ref, narrow_ref, buf):
    wide, narrow = [], []
    for t in range(2):
        for q in range(4):
            same = me_ref[2] == q % 2
            for n in range(9):
                lanes = slice(128 * n, 128 * (n + 1))
                mine, twin = mine_ref[t, q // 2, :, lanes], twin_ref[t, q // 2, :, lanes]
                buf[9 * q + n] = jnp.where(same, mine.astype(F32), twin.astype(F32))
        wide.append(lines(buf, 0, 20, (0,), TAPS * B1R))
        narrow.append(lines(buf, 80, 4, (0, NARROW_AT // 128), TAPS * B2R))
    for pair, out_ref in ((wide, wide_ref), (narrow, narrow_ref)):
        count, size = pair[0].shape
        for n in range(count):
            rows = [part[n : n + 1] for part in pair]
            out_ref[:, size * n : size * (n + 1)] = jnp.concatenate(rows, 0)


def fronts_body(both_ref, entry4_ref, pool4_ref, entry5_ref, pool5_ref):
    for q in range(4):
        pair = [both_ref[t, q].astype(F32) for t in range(2)]
        for lanes, entry_ref, pool_ref in (
            (slice(0, 528), entry4_ref, pool4_ref),
            (slice(576, 1408), entry5_ref, pool5_ref),
        ):
            size = lanes.stop - lanes.start
            for n in range(36):
                row = n if n < 28 else n + 4
                value = jnp.concatenate([p[row : row + 1, lanes] for p in pair], 0)
                at = 28 * q + n if n < 28 else 8 * q + n - 28
                (entry_ref if n < 28 else pool_ref)[:, size * at : size * (at + 1)] = value


def features_body(me_ref, z_ref, s_ref, n_ref, r0, r1, r2, r3, out_ref, *, voxels):
    rest = 0.0
    for k, r in enumerate((r0, r1, r2, r3)):
        rest = rest + mm(r[...], own_columns(jnp.bitwise_xor(me_ref[0], k), True))
    _, y = normed(z_ref[:, BP : BP + B0], s_ref[:, :B0], n_ref[:, :B0], voxels)
    out_ref[:, :B0] = silu(y)
    out_ref[:, B0:] = rest[:, B0:]


def xor_pairs(axis, step):
    return [(i, i ^ step) for i in range(lax.axis_size(axis))]


def tower_steps():
    steps, step = [], 1
    while step < lax.axis_size("dp") // 2:
        steps.append(step)
        step *= 2
    return steps


def other_tower(value):
    return lax.ppermute(value, "dp", xor_pairs("dp", lax.axis_size("dp") // 2))


def blk_peers(value):
    count = lax.axis_size("blk")
    return [value] + [lax.ppermute(value, "blk", xor_pairs("blk", k)) for k in range(1, count)]


def by_place(parts):
    me, step = lax.axis_index("blk"), 1
    while step < len(parts):
        hit = (me & step) != 0
        parts = [jnp.where(hit, parts[k ^ step], parts[k]) for k in range(len(parts))]
        step *= 2
    return parts


def swap_blk(mine):
    return [mine[0]] + [
        lax.ppermute(mine[k], "blk", xor_pairs("blk", k)) for k in range(1, lax.axis_size("blk"))
    ]


def dp_sum(value):
    for step in tower_steps():
        value = value + lax.ppermute(value, "dp", xor_pairs("dp", step))
    return value


def tower_parts(value):
    return blk_peers(dp_sum(value))


def gather_pieces(shard):
    rows = shard.shape[0] // 2
    odd = lax.axis_index("dp") % 2
    half = lax.dynamic_slice_in_dim(shard, odd * rows, rows, 0)
    mine = blk_peers(half)[1:]
    twins = [lax.ppermute(piece, "dp", xor_pairs("dp", 1)) for piece in mine]
    return [shard] + mine + twins


def fours():
    return [list(range(i, i + 4)) for i in range(0, lax.axis_size("dp"), 4)]


def scatter_four(value):
    value = lax.psum_scatter(
        value, "dp", scatter_dimension=0, axis_index_groups=fours(), tiled=False
    )
    for step in tower_steps()[2:]:
        got = lax.ppermute(value, "dp", xor_pairs("dp", step))
        value = (value.astype(F32) + got.astype(F32)).astype(BF)
    return value


def gather_eight(value):
    half = lax.axis_size("dp") // 2
    groups = [
        [b + i for i in range(4)] + [half + b + i for i in range(4)] for b in range(0, half, 4)
    ]
    return lax.all_gather(value, "dp", axis_index_groups=groups, tiled=False)


def after(values, first):
    values, _ = lax.optimization_barrier((values, first))
    return values


def rim_swap(first, last):
    count = lax.axis_size("blk")
    ahead = [(i, i + 1) for i in range(count - 1)]
    back = [(i + 1, i) for i in range(count - 1)]
    return lax.ppermute(last, "blk", ahead), lax.ppermute(first, "blk", back)


def step_rows(value, axis, step, first=None):
    if step in tower_steps()[:2]:
        rows = value.shape[axis] // 2
        high = (lax.axis_index("dp") & step) != 0
        keep = lax.dynamic_slice_in_dim(value, jnp.where(high, rows, 0), rows, axis)
        give = lax.dynamic_slice_in_dim(value, jnp.where(high, 0, rows), rows, axis)
    else:
        keep = give = value
    got = lax.ppermute(give, "dp", xor_pairs("dp", step))
    if first is not None:
        got = after(got, first)
    return (keep.astype(F32) + got.astype(F32)).astype(BF)


def reduce_rows(value, axis, steps=None):
    for step in tower_steps() if steps is None else steps:
        value = step_rows(value, axis, step)
    return value


def reduce_blk(value):
    count = value.shape[0]
    got = swap_blk(by_place([value[j] for j in range(count)]))
    total = got[0].astype(F32)
    for piece in got[1:]:
        total = total + piece.astype(F32)
    return total.astype(BF)


def spread_rows(value):
    stream = lax.axis_index("dp") // (lax.axis_size("dp") // 2)
    other = other_tower(value)
    both = jnp.where(stream == 0, jnp.stack([value, other]), jnp.stack([other, value]))
    for step in (2, 1):
        got = lax.ppermute(both, "dp", xor_pairs("dp", step))
        high = (lax.axis_index("dp") & step) != 0
        both = jnp.where(
            high, jnp.concatenate([got, both], 1), jnp.concatenate([both, got], 1)
        )
    return both


def branch_rows(me, mine, twin):
    return call(
        rows_body,
        (shape_of((2, 80 * TAPS * B1R)), shape_of((2, 32 * TAPS * B2R))),
        me, mine, twin,
        micros=3, mib=16, scratch=[pltpu.VMEM((36, 96, 128), F32)],
    )


def pick_row(param, stream):
    size = param.shape[1]
    return lax.dynamic_index_in_dim(param.reshape(2, size // 128, 128), stream, 0, keepdims=False)


def on_device(clips, cotangent, *params):
    groups = lax.axis_size("dp")
    count = lax.axis_size("blk")
    stream = lax.axis_index("dp") // (groups // 2)
    place = lax.axis_index("blk")
    index = lax.axis_index("dp")
    me = jnp.stack([place, index % (groups // 2), index % 2, index // 2 % 2]).astype(jnp.int32)
    own = [pick_row(p, stream) for p in params]
    early, late = own[:6], own[6:]
    n, frames, height, breadth, c_first = clips.shape
    voxels = groups // 2 * count * n * frames * height * breadth
    late_voxels = voxels // 8
    x = clips.reshape(n, frames, height * breadth, c_first)
    e, p = REDUCED // count, BP // count
    g = (REDUCED + OUTER + BP) // count

    def pack_front(layer, c, turn=0):
        norms = jnp.concatenate([layer[4].reshape(-1), layer[5].reshape(-1)])
        row = jnp.pad(norms, (0, c - 2 * g)).reshape(1, c)
        rows = jnp.concatenate([layer[0].reshape(e, c), layer[3].reshape(p, c)])
        if turn:
            rows = jnp.concatenate([rows[:, c - turn :], rows[:, : c - turn]], 1)
        return jnp.pad(jnp.concatenate([rows, row]), ((0, 160 - e - p - 1), (0, 0)))

    def pack_branch(layer):
        wide = layer[1].reshape(80, -1)
        narrow = layer[2].reshape(32, -1)
        gap = jnp.zeros((16, NARROW_AT - narrow.shape[1]), BF)
        low = jnp.concatenate([narrow[:16], gap, narrow[16:]], 1)
        low = jnp.pad(low, ((0, 0), (0, wide.shape[1] - low.shape[1])))
        return jnp.concatenate([wide, low])

    packed = lax.dynamic_slice_in_dim(pack_branch(early), index % 2 * 48, 48, 0)
    pieces = gather_pieces(pack_front(after(early, packed), c_first))
    late_front = lax.dynamic_slice_in_dim(pack_front(late, LAYER, BP), index % 2 * 80, 80, 0)
    late_front = late_front.reshape(5, 16, LAYER).transpose(1, 0, 2).reshape(16, 5 * LAYER)
    late_front = jnp.pad(late_front, ((0, 0), (0, packed.shape[1] - 5 * LAYER)))
    packed = jnp.concatenate([packed, late_front])
    packed = lax.all_gather(packed, "blk", tiled=False)
    late = after(late, pieces[0])
    taps_5 = call(kernels5_body, shape_of((TAPS, 128, INNER), BF), pack_branch(late), micros=2)
    x = after(x, taps_5)
    z, m, front_4, nf4, nb4 = call(
        front4_body,
        (
            shape_of((2, 512, 576)), shape_of((2, REDUCED)), shape_of((576, c_first), BF),
            shape_of((2, REDUCED)), shape_of((2, 576)),
        ),
        me, x, *pieces, micros=0,
        scratch=[pltpu.VMEM((4, 160, c_first), BF), pltpu.VMEM((2, 1024), F32)],
    )
    late, cotangent = after((late, cotangent), m)
    cot = cotangent.reshape(128, LAYER)
    cot_mine = call(cot5_body, shape_of((4, 128, 256), BF), me, cot, micros=2)

    def conv(values, kernel, pads, order):
        return lax.conv_general_dilated(
            values,
            kernel.reshape(-1, 3, 3, *kernel.shape[1:]),
            (1, 1, 1),
            pads,
            dimension_numbers=("DNHWC", order, "DNHWC"),
            preferred_element_type=F32,
        )

    forth, back = "DHWOI", "DHWIO"
    flat_pads = ((0, 0), (1, 1), (1, 1))
    same = ((1, 1), (1, 1), (1, 1))
    at4 = functools.partial(functools.partial, voxels=voxels)
    at5 = functools.partial(functools.partial, voxels=late_voxels)

    parts = tower_parts(m)
    z_then = after(z, cot_mine)
    a, rims, sf4 = call(
        at4(act4_body),
        (shape_of((2, 512, INNER), BF), shape_of((2, 512, BP + INNER), BF), shape_of((2, REDUCED))),
        z_then, *parts, nf4, micros=0,
    )
    before, behind = rim_swap(rims[0], rims[1])
    packed = after(packed, a)
    twin = lax.ppermute(packed, "dp", xor_pairs("dp", 1))
    taps_4, taps_first, taps_last = call(
        kernels4_body,
        (
            shape_of((TAPS, OUTER, INNER), BF),
            shape_of((9, OUTER, INNER), BF), shape_of((9, OUTER, INNER), BF),
        ),
        me, packed, twin, micros=5, mib=12, away=(1, 2),
        scratch=[pltpu.VMEM((4, 96, 4320), BF), pltpu.SemaphoreType.DMA((2,))],
    )
    before, behind = after((before, behind), taps_4)
    pool, m_pool = call(
        pool4_body, (shape_of((2, 512, BP)), shape_of((2, BP))), rims, before, behind, micros=2
    )
    before, behind = before[:, BP:], behind[:, BP:]
    a_pad = jnp.concatenate([before[None], a, behind[None]]).reshape(4, n, height, breadth, INNER)
    c = conv(a_pad, taps_4, flat_pads, forth).reshape(2, 512, OUTER)
    front_5, n5f, n5 = call(
        front5_body,
        (shape_of((576, LAYER), BF), shape_of((2, 1024)), shape_of((2, 256))),
        me, packed, twin, micros=1, scratch=[pltpu.VMEM((4, 160, LAYER), BF)],
    )
    cots = swap_blk([after(cot_mine, c)[k] for k in range(4)])
    parts = tower_parts(call(moments_body, shape_of((2, 576)), c, m_pool, micros=1))

    mid, z5, m, sb4 = call(
        at4(norm4_body),
        (shape_of((128, LAYER), BF), shape_of((128, 576)), shape_of((2, REDUCED)), shape_of((2, 576))),
        z, c, pool, sf4, *parts, nf4, nb4, front_5, micros=4, lazy=(0, 2, 3, 8, 9, 10),
    )
    send, sf5 = call(
        at5(act5_body),
        (shape_of((4, 128, 256), BF), shape_of((2, REDUCED))),
        me, z5, *tower_parts(m), n5f, micros=1,
    )
    a5, pool5 = call(
        join5_body,
        (shape_of((4, 128, INNER), BF), shape_of((4, 128, 128))),
        me, *swap_blk([send[k] for k in range(4)]),
        micros=1, scratch=[pltpu.VMEM((6, 128, 128), F32)],
    )
    small = (4, n, height // 2, breadth // 2, -1)
    c5 = conv(a5.reshape(small), taps_5, same, forth).reshape(4, 128, 128)
    s5 = dp_sum(call(moments5_body, shape_of((2, 256)), c5, pool5, micros=1))
    feat, dy5, m = call(
        at5(norm5_body),
        (shape_of((4, 128, 256), BF), shape_of((4, 128, 256)), shape_of((2, 256))),
        me, c5, pool5, s5, n5, *cots, micros=1, lazy=(2, 4, 5, 6, 7, 8),
    )

    feat = swap_blk([feat[k] for k in range(4)])
    b5 = after(dp_sum(m), feat)
    dv5, turned5, u5 = call(
        at5(back5_body),
        (shape_of((4, 128, 128), BF), shape_of((4, 128, 128), BF), shape_of((4, 128, 128))),
        c5, pool5, s5, n5, dy5, b5, micros=1, lazy=(0, 1, 2, 3, 4),
    )
    part = conv(turned5.reshape(small), taps_5, same, back).reshape(4, 128, INNER)
    send = call(send5_body, shape_of((4, 128, 256), BF), me, part, u5, micros=1)
    dv5 = after(dv5, send)
    got5 = swap_blk([send[k] for k in range(4)])
    branch_part5 = call(
        kernel_grad5_body,
        shape_of((4, 1, 96, 1152), BF),
        a5, dv5,
        micros=2, mib=16,
        scratch=[pltpu.VMEM((6, 128, 2304), BF), pltpu.VMEM((128, 512), BF)],
    )
    z5 = after(z5, branch_part5)
    branch_5 = scatter_four(branch_part5)
    dyf5, u5, m = call(
        at5(front_back5_body),
        (shape_of((128, REDUCED)), shape_of((128, BP), BF), shape_of((2, 1536))),
        me, *got5, z5, sf5, n5f, cot[:, :B0], b5, micros=1,
        lazy=(5, 6, 7, 8, 9),
    )
    parts = tower_parts(m)
    g5, gm, m, back5 = call(
        at4(mid_back_body),
        (shape_of((128, 576), BF), shape_of((128, LAYER)), shape_of((2, 576)), shape_of((2, 1536))),
        dyf5, z5, sf5, n5f, *parts, u5, front_5, c, pool, sb4, nb4, micros=4,
        lazy=(0, 1, 2, 3, 8, 9, 10, 11, 12, 13),
    )

    parts = tower_parts(m)
    front_part5 = call(
        front_grad5_body, shape_of((4, 4, 40, LAYER), BF), after(g5, parts[0]), mid, micros=1
    )
    front_part5 = jnp.concatenate([front_part5[..., BP:], front_part5[..., :BP]], 3)
    front_5_sum = step_rows(front_part5, 0, 1)
    gm = after(gm, front_5_sum)
    both5 = gather_eight(after(branch_5, parts[0])[0]).reshape(2, 4, 96, 1152)
    dv, dp, turned4, bb4 = call(
        at4(branch_grad4_body),
        (
            shape_of((2, 512, OUTER), BF), shape_of((2, 512, BP), BF),
            shape_of((2, 512, OUTER), BF), shape_of((2, 576)),
        ),
        gm, c, pool, sb4, nb4, *parts, micros=3, lazy=(0, 1, 2, 3, 4),
    )
    image = (1, n, height, breadth, OUTER)
    rim_first = conv(turned4[1].reshape(image), taps_first, flat_pads, back).reshape(512, INNER)
    rim_last = conv(turned4[0].reshape(image), taps_last, flat_pads, back).reshape(512, INNER)
    rim_first = jnp.concatenate([dp[0], rim_first.astype(BF)], 1)
    rim_last = jnp.concatenate([dp[1], rim_last.astype(BF)], 1)
    got_before, got_after = rim_swap(rim_first, rim_last)
    branch_part4 = call(
        kernel_grad4_body,
        shape_of((4, 4, 96, 1152), BF),
        me, a, before, behind, after(dv, (rim_first, rim_last)),
        micros=8, mib=10,
        scratch=[pltpu.VMEM((2, 4, 512, 256), BF), pltpu.VMEM((OUTER, 1024), BF)],
    )
    turned4 = after(turned4, (branch_part4, both5))
    branch_part4 = scatter_four(branch_part4)
    front_5_sum = reduce_rows(front_5_sum, 0, tower_steps()[1:])[0]
    inner = conv(turned4.reshape(2, n, height, breadth, OUTER), taps_4, same, back)
    dyf4, u4, m = call(
        at4(front_back4_body),
        (shape_of((2, 512, REDUCED)), shape_of((2, 512, BP), BF), shape_of((2, REDUCED))),
        gm, z, sf4, nf4, inner.reshape(2, 512, INNER), got_before, got_after, dp, micros=4,
        lazy=(0, 1, 2, 3, 5, 6, 7),
    )
    parts = tower_parts(m)
    branch_4 = after(branch_part4, parts[3])
    both5 = both5.reshape(2, 2, 2, 96, 1152)
    wide_5, narrow_5 = branch_rows(jnp.zeros_like(me), both5[:, :, 0], both5[:, :, 1])
    z = after(z, (front_5_sum, wide_5, narrow_5))
    g4, front_part4, bf4 = call(
        at4(front_grad4_body),
        (shape_of((2, 512, 576), BF), shape_of((4, 4, 40, c_first), BF), shape_of((2, REDUCED))),
        z, sf4, nf4, dyf4, *parts, u4, x, micros=4, lazy=(1, 2),
    )
    clips_grad = call(
        clips_grad_body, shape_of((n, frames, height * breadth, c_first)), g4, front_4, micros=3
    )

    norms4 = jnp.concatenate([bf4, bb4[:, BP:], bb4[:, :BP]], 1)
    all5 = back5[:, 512:].reshape(2, count, 256)
    norms5 = jnp.concatenate(
        [
            back5[:, :REDUCED],
            all5[:, :, :80].reshape(2, -1),
            all5[:, :, 80:112].reshape(2, -1),
            all5[:, :, 128 + POOL_LANE : 160 + POOL_LANE].reshape(2, -1),
        ],
        axis=1,
    )
    norms = jnp.stack([norms4, norms5])
    theirs = other_tower(norms)
    fronts = after(step_rows(front_part4, 0, 1), branch_4)
    got = swap_blk([branch_4[k] for k in range(4)])
    fronts = step_rows(fronts, 0, 2, got)
    fronts = reduce_rows(fronts, 0, tower_steps()[2:])[0]
    fronts = jnp.concatenate([fronts, jnp.zeros((4, 40, 48), BF), front_5_sum], 2)
    branch_4 = sum(piece.astype(F32) for piece in got).astype(BF)
    features = call(
        at5(features_body), shape_of((128, LAYER)), me, z5, sf5, n5f, *feat, micros=2
    ).reshape(cotangent.shape)

    side = lax.ppermute(branch_4, "dp", xor_pairs("dp", 2))
    other = other_tower(branch_4)
    fronts = after(fronts, (branch_4, theirs, features, clips_grad))
    norms = jnp.where(stream == 0, jnp.stack([norms, theirs]), jnp.stack([theirs, norms]))
    norms = lax.dynamic_slice_in_dim(norms, place * g, g, 3)
    gains_4, shifts_4, gains_5, shifts_5 = (norms[:, 0, 1], norms[:, 0, 0], norms[:, 1, 1], norms[:, 1, 0])
    got = swap_blk(by_place([fronts[j] for j in range(count)]))
    fronts = sum(piece.astype(F32) for piece in got).astype(BF)
    corner = jnp.concatenate(
        [
            lax.ppermute(other[:48], "dp", xor_pairs("dp", 2)),
            other_tower(side[48:]),
        ]
    )
    corner = after(corner, (gains_4, shifts_4, gains_5, shifts_5))
    right = index // 2 % 2 == 1
    ours = jnp.where(right, jnp.stack([side, branch_4]), jnp.stack([branch_4, side]))
    others = jnp.where(right, jnp.stack([corner, other]), jnp.stack([other, corner]))
    both = jnp.where(stream == 0, jnp.stack([ours, others]), jnp.stack([others, ours]))
    wide_4, narrow_4 = branch_rows(me, both, lax.ppermute(both, "dp", xor_pairs("dp", 1)))
    entry_4, poolproj_4, entry_5, poolproj_5 = call(
        fronts_body,
        (
            shape_of((2, 112 * c_first)), shape_of((2, 32 * c_first)),
            shape_of((2, 112 * LAYER)), shape_of((2, 32 * LAYER)),
        ),
        spread_rows(fronts[None]), micros=2, mib=10,
    )

    return (
        features, clips_grad.reshape(clips.shape),
        entry_4, wide_4, narrow_4, poolproj_4, gains_4, shifts_4,
        entry_5, wide_5, narrow_5, poolproj_5, gains_5, shifts_5,
    )


def solution(mesh):
    spec = P("dp", "blk", None, None, None)
    flat = P(None, "blk")
    return jax.shard_map(
        on_device,
        mesh=mesh,
        in_specs=(spec, spec) + (flat,) * 12,
        out_specs=(spec, spec) + (flat,) * 12,
        check_vma=False,
    )
```

```python
import functools

import jax
import jax.numpy as jnp
from jax import lax
from jax.experimental import pallas as pl
from jax.experimental.pallas import tpu as pltpu
from jax.sharding import PartitionSpec as P

B0 = 256
B1R = 160
B1 = 320
B2R = 32
B2 = 128
BP = 128
INNER = B1R + B2R
REDUCED = B0 + INNER
OUTER = B1 + B2
LAYER = B0 + OUTER + BP
EPS = 1e-05
BF = jnp.bfloat16
F32 = jnp.float32
TAPS = 27
NARROW_AT = 896
POOL_LANE = 64

NT = (((1,), (1,)), ((), ()))
NN = (((1,), (0,)), ((), ()))
VMEM = pl.BlockSpec(memory_space=pltpu.VMEM)
SMEM = pl.BlockSpec(memory_space=pltpu.SMEM)


def mm(a, b, dims=NN):
    return lax.dot_general(a, b, dims, preferred_element_type=F32)


def shape_of(shape, kind=F32):
    return jax.ShapeDtypeStruct(shape, kind)


def call(body, outs, *args, micros=2, scratch=(), mib=6, lazy=(), away=()):
    def whole(*refs):
        bufs, sems = refs[len(refs) - len(lazy) - 1 : -1], refs[-1]
        copies = [
            pltpu.make_async_copy(refs[i], bufs[n], sems.at[n]) for n, i in enumerate(lazy)
        ]
        for copy in copies:
            copy.start()
        for copy in copies:
            copy.wait()
        ins = list(refs[: len(args)])
        for n, i in enumerate(lazy):
            ins[i] = bufs[n]
        body(*ins, *refs[len(args) : len(refs) - len(lazy) - 1])

    lazy = [i % len(args) for i in lazy]
    specs = [SMEM if a.dtype == jnp.int32 else VMEM for a in args]
    scratch, size = list(scratch), 0
    for i in lazy:
        specs[i] = pl.BlockSpec(memory_space=pl.ANY)
        scratch.append(pltpu.VMEM(args[i].shape, args[i].dtype))
        size += args[i].size * args[i].dtype.itemsize
    if lazy:
        scratch.append(pltpu.SemaphoreType.DMA((len(lazy),)))
    spots = [VMEM] * (len(outs) if isinstance(outs, tuple) else 1)
    for i in away:
        spots[i] = pl.BlockSpec(memory_space=pltpu.HBM)
    return pl.pallas_call(
        whole if lazy else body,
        out_shape=outs,
        in_specs=specs,
        out_specs=spots if isinstance(outs, tuple) else spots[0],
        scratch_shapes=scratch,
        compiler_params=pltpu.CompilerParams(vmem_limit_bytes=(mib << 20) + 5 * size // 4),
        cost_estimate=pl.CostEstimate(
            flops=int(micros * 1.0e9), bytes_accessed=1 << 20 if micros else 0, transcendentals=0
        ),
    )(*args)


def iota(shape, axis):
    return lax.broadcasted_iota(jnp.int32, shape, axis)


def ones_where(ok, value=1.0):
    return jnp.where(ok, value, 0.0).astype(BF)


def pool_matrix(n, side):
    r, c = iota((n, n), 0), iota((n, n), 1)
    area = side * side
    near_w = jnp.abs(r % side - c % side) <= 1
    near_h = jnp.abs((r // side) % side - (c // side) % side) <= 1
    return ones_where((r // area == c // area) & near_w & near_h)


def turn_matrix(n, area):
    r, c = iota((n, n), 0), iota((n, n), 1)
    return ones_where((r // area == c // area) & (r % area + c % area == area - 1))


def two_matrix(transposed):
    shape = (256, 64) if transposed else (64, 256)
    big, small = (iota(shape, 0), iota(shape, 1)) if transposed else (iota(shape, 1), iota(shape, 0))
    ok = (small // 16 == big // 64) & ((small // 4) % 4 == (big // 16) % 4)
    return ones_where(ok & (small % 4 == (big // 2) % 4), 0.125)


def exact(matrix, values):
    high = values.astype(BF)
    low = (values - high.astype(F32)).astype(BF)
    return mm(matrix, high) + mm(matrix, low)


def own_columns(place, transposed=False):
    shape = (256, LAYER) if transposed else (LAYER, 256)
    lane, col = (iota(shape, 0), iota(shape, 1)) if transposed else (iota(shape, 1), iota(shape, 0))
    wide = (lane < 80) & (col == B0 + 80 * place + lane)
    narrow = (lane >= 80) & (lane < 112) & (col == B0 + B1 + 32 * place + lane - 80)
    at = lane - 128 - POOL_LANE
    pool = (at >= 0) & (at < 32) & (col == B0 + OUTER + 32 * place + at)
    return ones_where(wide | narrow | pool)


def scaled_of(values, sums, voxels):
    centre = sums[0:1] * (1.0 / voxels)
    spread = lax.rsqrt(sums[1:2] * (1.0 / voxels) - centre * centre + EPS)
    return (values - centre) * spread, spread


def normed(values, sums, norms, voxels):
    scaled, _ = scaled_of(values, sums, voxels)
    return scaled, scaled * norms[0:1] + norms[1:2]


def silu(y):
    return y * lax.logistic(y)


def slope(y):
    sigmoid = lax.logistic(y)
    return sigmoid * (1.0 + y * (1.0 - sigmoid))


def norm_back(dy, values, sums, norms, back, voxels):
    scaled, spread = scaled_of(values, sums, voxels)
    scale = norms[0:1] * spread
    return scale * (dy - back[0:1] * (1.0 / voxels) - scaled * (back[1:2] * (1.0 / voxels)))


def add_pair(ref, lanes, first, second):
    ref[0:1, lanes] += jnp.sum(first, 0, keepdims=True)
    ref[1:2, lanes] += jnp.sum(second, 0, keepdims=True)


def shifted(a, side, j, k):
    if j == 0 and k == 0:
        return a
    rows, lanes = a.shape
    area = side * side
    r = iota((area, lanes), 0)
    w, h = r % side + k, r // side + j
    ok = (w >= 0) & (w < side) & (h >= 0) & (h < side)
    moved = pltpu.roll(a, (-(side * j + k)) % rows, 0).reshape(rows // area, area, lanes)
    return jnp.where(ok[None], moved, 0.0).reshape(rows, lanes)


def assemble(me_ref, pieces, buf):
    half = pieces[0].shape[0] // 2
    buf[me_ref[0]] = pieces[0][...]
    for k in range(1, 4):
        place = jnp.bitwise_xor(me_ref[0], k)
        buf[place, pl.ds(pl.multiple_of(half * me_ref[2], half), half), :] = pieces[k][...]
        buf[place, pl.ds(pl.multiple_of(half * (1 - me_ref[2]), half), half), :] = pieces[k + 3][...]


def tap_block(shards, t):
    wide, narrow = [], []
    for w in shards:
        wide.append(w[0:80, B1R * t : B1R * (t + 1)].astype(F32))
        for lane in (B2R * t, NARROW_AT + B2R * t):
            narrow.append(w[80:96, lane : lane + B2R].astype(F32))
    wide = jnp.concatenate(wide, 0)
    narrow = jnp.concatenate(narrow, 0)
    top = jnp.concatenate([wide, jnp.zeros((wide.shape[0], B2R), F32)], 1)
    low = jnp.concatenate([jnp.zeros((narrow.shape[0], B1R), F32), narrow], 1)
    return jnp.concatenate([top, low], 0).astype(BF)


def kernels4_body(me_ref, mine_ref, twin_ref, all_ref, first_ref, last_ref, buf, sems):
    first = pltpu.make_async_copy(all_ref.at[0:9], first_ref, sems.at[0])
    last = pltpu.make_async_copy(all_ref.at[18:27], last_ref, sems.at[1])
    buf[:, pl.ds(pl.multiple_of(48 * me_ref[2], 16), 48), :] = mine_ref[...]
    buf[:, pl.ds(pl.multiple_of(48 * (1 - me_ref[2]), 16), 48), :] = twin_ref[...]
    for t in range(TAPS):
        all_ref[t] = tap_block([buf.at[z] for z in range(4)], t)
        if t == 8:
            first.start()
    last.start()
    first.wait()
    last.wait()


def kernels5_body(w_ref, all_ref):
    for t in range(TAPS):
        all_ref[t] = jnp.concatenate([tap_block([w_ref], t), jnp.zeros((16, INNER), BF)], 0)


def front_parts(buf, matrix_ref, norms_ref):
    for z in range(4):
        matrix_ref[32 * z : 32 * (z + 1), :] = buf[z, 112:144, :]
        matrix_ref[BP + 112 * z : BP + 112 * (z + 1), :] = buf[z, 0:112, :]
        row = buf[z, 144:160, :].astype(F32)[0:1]
        norms_ref[0:1, 256 * z : 256 * (z + 1)] = row[:, :256]
        norms_ref[1:2, 256 * z : 256 * (z + 1)] = row[:, 256:512]


def total_of(parts):
    return (parts[0][...] + parts[1][...]) + (parts[2][...] + parts[3][...])


def front5_body(me_ref, shards_ref, w_ref, n_ref, own_ref):
    front_parts(shards_ref, w_ref, n_ref)
    norms = n_ref[...]
    own = jnp.zeros((2, 256), F32)
    gap = jnp.zeros((2, 16 + POOL_LANE), F32)
    for z in range(4):
        wide = norms[:, REDUCED + 80 * z : REDUCED + 80 * (z + 1)]
        narrow = norms[:, REDUCED + B1 + 32 * z : REDUCED + B1 + 32 * (z + 1)]
        pool = norms[:, REDUCED + OUTER + 32 * z : REDUCED + OUTER + 32 * (z + 1)]
        block = jnp.concatenate([wide, narrow, gap, pool, jnp.zeros((2, 32), F32)], 1)
        own = jnp.where(me_ref[0] == z, block, own)
    own_ref[...] = own


def front4_body(me_ref, x_ref, p0, p1, p2, p3, t1, t2, t3, z_ref, m_ref, w_ref, nf_ref, nb_ref, buf, n_ref):
    assemble(me_ref, (p0, p1, p2, p3, t1, t2, t3), buf)
    front_parts(buf, w_ref, n_ref)
    nf_ref[...] = n_ref[:, :REDUCED]
    nb_ref[:, :BP] = n_ref[:, REDUCED + OUTER :]
    nb_ref[:, BP:] = n_ref[:, REDUCED : REDUCED + OUTER]
    m_ref[...] = jnp.zeros_like(m_ref)
    for f in range(2):
        for h in range(2):
            x = x_ref[4 * h : 4 * h + 4, f].reshape(256, x_ref.shape[3])
            z = mm(x, w_ref[...], NT)
            rows = slice(256 * h, 256 * h + 256)
            z_ref[f, rows, :] = z
            front = z[:, BP:]
            add_pair(m_ref, slice(None), front, front * front)


def act4_body(z_ref, s0, s1, s2, s3, n_ref, a_ref, rim_ref, s_ref, *, voxels):
    s_ref[...] = total_of((s0, s1, s2, s3))
    sums, norms = s_ref[:, B0:], n_ref[:, B0:]
    for f in range(2):
        for h in range(2):
            rows = slice(256 * h, 256 * h + 256)
            _, y = normed(z_ref[f, rows, BP + B0 :], sums, norms, voxels)
            a_ref[f, rows, :] = silu(y).astype(BF)
            rim_ref[f, rows, :BP] = z_ref[f, rows, :BP].astype(BF)
            rim_ref[f, rows, BP:] = silu(y).astype(BF)


def pool4_body(pp_ref, before_ref, after_ref, pool_ref, m_ref, pad_ref):
    pad_ref[0] = before_ref[:, BP:]
    pad_ref[1:3] = pp_ref[:, :, BP:]
    pad_ref[3] = after_ref[:, BP:]
    matrix = pool_matrix(256, 8)
    m_ref[...] = jnp.zeros_like(m_ref)
    for f in range(2):
        for h in range(2):
            rows = slice(256 * h, 256 * h + 256)
            rim = before_ref if f == 0 else after_ref
            v = pp_ref[0, rows, :BP].astype(F32) + pp_ref[1, rows, :BP].astype(F32)
            v = (v + rim[rows, :BP].astype(F32)).astype(BF)
            out = mm(matrix, v) * (1.0 / 27.0)
            pool_ref[f, rows, :] = out
            add_pair(m_ref, slice(None), out, out * out)


def moments_body(c_ref, p_ref, m_ref):
    m_ref[:, 0:BP] = p_ref[...]
    m_ref[:, BP:] = jnp.zeros((2, OUTER), F32)
    for f in range(2):
        for h in range(2):
            c = c_ref[f, 256 * h : 256 * h + 256, :]
            add_pair(m_ref, slice(BP, None), c, c * c)


def norm4_body(
    z_ref, c_ref, p_ref, sf_ref, s0, s1, s2, s3, nf_ref, nb_ref, w_ref, mid_ref, z5_ref, m_ref, sb_ref, *, voxels
):
    sb_ref[...] = total_of((s0, s1, s2, s3))
    matrix = two_matrix(False)
    sf, sb, nf, nb = sf_ref[:, :B0], sb_ref[...], nf_ref[:, :B0], nb_ref[...]
    for h in range(2):
        rows, outs = slice(256 * h, 256 * h + 256), slice(64 * h, 64 * h + 64)
        pool = direct = conv = 0.0
        for f in range(2):
            pool += silu(normed(p_ref[f, rows, :], sb[:, :BP], nb[:, :BP], voxels)[1])
            direct += silu(normed(z_ref[f, rows, BP : BP + B0], sf, nf, voxels)[1])
            conv += silu(normed(c_ref[f, rows, :], sb[:, BP:], nb[:, BP:], voxels)[1])
        mid_ref[outs, :BP] = exact(matrix, pool).astype(BF)
        mid_ref[outs, BP : BP + B0] = exact(matrix, direct).astype(BF)
        mid_ref[outs, BP + B0 :] = exact(matrix, conv).astype(BF)
    z5 = mm(mid_ref[...], w_ref[...], NT)
    z5_ref[...] = z5
    m_ref[...] = jnp.zeros_like(m_ref)
    add_pair(m_ref, slice(None), z5[:, BP:], z5[:, BP:] * z5[:, BP:])


def act5_body(me_ref, z_ref, s0, s1, s2, s3, n_ref, send_ref, s_ref, *, voxels):
    s_ref[...] = total_of((s0, s1, s2, s3))
    _, y = normed(z_ref[:, BP + B0 :], s_ref[:, B0:], n_ref[:, B0:REDUCED], voxels)
    base = jnp.concatenate([silu(y), jnp.zeros((y.shape[0], 64), F32)], 1)
    pre = z_ref[:, :BP].astype(BF)
    c, lane = iota((BP, 256), 0), iota((BP, 256), 1)
    at = lane - 128 - POOL_LANE
    for k in range(4):
        place = jnp.bitwise_xor(me_ref[0], k)
        pick = ones_where((at >= 0) & (at < 32) & (c == 32 * place + at))
        send_ref[k] = (base + mm(pre, pick)).astype(BF)


def join5_body(me_ref, r0, r1, r2, r3, a_ref, pool_ref, pre):
    pre[0] = jnp.zeros((128, 128), F32)
    pre[5] = jnp.zeros((128, 128), F32)
    for k, r in enumerate((r0, r1, r2, r3)):
        place = jnp.bitwise_xor(me_ref[0], k)
        a_ref[place] = r[:, :INNER]
        pre[place + 1] = r[:, 128:].astype(F32)
    matrix = pool_matrix(128, 4)
    lane = iota((128, 128), 1)
    ok = (lane >= POOL_LANE) & (lane < POOL_LANE + 32)
    for f in range(4):
        v = (pre[f] + pre[f + 1] + pre[f + 2]).astype(BF)
        pool_ref[f] = jnp.where(ok, mm(matrix, v) * (1.0 / 27.0), 0.0)


def moments5_body(c_ref, p_ref, m_ref):
    m_ref[...] = jnp.zeros_like(m_ref)
    for f in range(4):
        c, p = c_ref[f], p_ref[f]
        add_pair(m_ref, slice(0, 128), c, c * c)
        add_pair(m_ref, slice(128, 256), p, p * p)


def cot5_body(me_ref, cot_ref, out_ref):
    for k in range(4):
        pick = own_columns(jnp.bitwise_xor(me_ref[0], k))
        out_ref[k] = mm(cot_ref[...], pick).astype(BF)


def norm5_body(me_ref, c_ref, p_ref, s_ref, n_ref, g0, g1, g2, g3, feat_ref, dy_ref, x_ref, *, voxels):
    x_ref[...] = jnp.zeros_like(x_ref)
    for k, g in enumerate((g0, g1, g2, g3)):
        place = jnp.bitwise_xor(me_ref[0], k)
        for src, lanes in ((c_ref, slice(0, 128)), (p_ref, slice(128, 256))):
            scaled, y = normed(src[place], s_ref[:, lanes], n_ref[:, lanes], voxels)
            sigmoid = lax.logistic(y)
            feat_ref[k, :, lanes] = (y * sigmoid).astype(BF)
            dy = g[:, lanes].astype(F32) * (sigmoid * (1.0 + y * (1.0 - sigmoid)))
            dy_ref[place, :, lanes] = dy
            add_pair(x_ref, lanes, dy, dy * scaled)


def back5_body(c_ref, p_ref, s_ref, n_ref, dy_ref, b_ref, dv_ref, turned_ref, u_ref, *, voxels):
    matrix, turn = pool_matrix(128, 4), turn_matrix(128, 16)
    parts = []
    for f in range(4):
        for src, lanes in ((c_ref, slice(0, 128)), (p_ref, slice(128, 256))):
            dv = norm_back(
                dy_ref[f, :, lanes], src[f], s_ref[:, lanes], n_ref[:, lanes], b_ref[:, lanes],
                voxels,
            )
            if src is c_ref:
                dv_ref[f] = dv.astype(BF)
                turned_ref[3 - f] = mm(turn, dv.astype(BF)).astype(BF)
            else:
                parts.append(dv.astype(BF).astype(F32))
    for f in range(4):
        v = sum(parts[max(f - 1, 0) : f + 2]).astype(BF)
        u_ref[f] = mm(matrix, v) * (1.0 / 27.0)


def send5_body(me_ref, part_ref, u_ref, send_ref):
    turn = turn_matrix(128, 16)
    for k in range(4):
        place = jnp.bitwise_xor(me_ref[0], k)
        part = mm(turn, part_ref[3 - place].astype(BF))
        send_ref[k, :, :128] = part[:, :128].astype(BF)
        tail = jnp.concatenate([part[:, 128:], jnp.zeros((128, 64), F32)], 1)
        send_ref[k, :, 128:] = (tail + u_ref[place]).astype(BF)


def front_back5_body(me_ref, r0, r1, r2, r3, z_ref, s_ref, n_ref, cot_ref, b_ref, dy_ref, u_ref, x_ref, *, voxels):
    x_ref[...] = jnp.zeros_like(x_ref)
    inner = 0.0
    u = 0.0
    c, lane = iota((128, BP), 0) - POOL_LANE, iota((128, BP), 1)
    for k, r in enumerate((r0, r1, r2, r3)):
        place = jnp.bitwise_xor(me_ref[0], k)
        inner = inner + r[:, :INNER].astype(F32)
        u = u + mm(r[:, 128:], ones_where((c >= 0) & (c < 32) & (lane == 32 * place + c)))
    u_ref[...] = u.astype(BF)
    for lanes, grad in ((slice(0, B0), cot_ref[...].astype(F32)), (slice(B0, REDUCED), inner)):
        at = slice(BP + lanes.start, BP + lanes.stop)
        scaled, y = normed(z_ref[:, at], s_ref[:, lanes], n_ref[:, lanes], voxels)
        dy = grad * slope(y)
        dy_ref[:, lanes] = dy
        add_pair(x_ref, lanes, dy, dy * scaled)
    first = jnp.where(me_ref[1] == 0, 1.0, 0.0)
    x_ref[:, pl.ds(pl.multiple_of(512 + 256 * me_ref[0], 128), 256)] = b_ref[...] * first


def mid_back_body(
    dy_ref, z_ref, s_ref, n_ref, b0, b1, b2, b3, u_ref, w_ref, c_ref, p_ref, sb_ref, nb_ref,
    g_ref, gm_ref, x_ref, back_ref, *, voxels,
):
    back_ref[...] = total_of((b0, b1, b2, b3))
    g_ref[:, :BP] = u_ref[...]
    g_ref[:, BP:] = norm_back(
        dy_ref[...], z_ref[:, BP:], s_ref[...], n_ref[:, :REDUCED], back_ref[:, :REDUCED], voxels / 8
    ).astype(BF)
    gm = mm(g_ref[...], w_ref[...])
    gm_ref[...] = gm
    matrix = two_matrix(True)
    x_ref[...] = jnp.zeros_like(x_ref)
    for h in range(2):
        rows = slice(256 * h, 256 * h + 256)
        block = gm[64 * h : 64 * h + 64]
        for src, lanes, at in (
            (p_ref, slice(0, BP), slice(0, BP)),
            (c_ref, slice(BP, BP + OUTER), slice(BP + B0, LAYER)),
        ):
            up = exact(matrix, block[:, at])
            for f in range(2):
                scaled, y = normed(src[f, rows, :], sb_ref[:, lanes], nb_ref[:, lanes], voxels)
                dy = up * slope(y)
                add_pair(x_ref, lanes, dy, dy * scaled)


def front_rows(total, out_ref):
    gap = jnp.zeros((4, total.shape[1]), F32)
    for z in range(4):
        for q in range(4):
            entry, pool = BP + 112 * z + 28 * q, 32 * z + 8 * q
            block = [total[entry : entry + 28], gap, total[pool : pool + 8]]
            out_ref[q, z] = jnp.concatenate(block, 0).astype(BF)


def front_grad5_body(g_ref, mid_ref, out_ref):
    turned = g_ref[...].astype(F32).T.astype(BF)
    front_rows(mm(turned, mid_ref[...]), out_ref)


def branch_grad4_body(
    gm_ref, c_ref, p_ref, s_ref, n_ref, b0, b1, b2, b3, dv_ref, dp_ref, turned_ref, b_ref, *, voxels
):
    turn = turn_matrix(256, 64)
    b_ref[...] = total_of((b0, b1, b2, b3))
    matrix = two_matrix(True)
    for h in range(2):
        rows = slice(256 * h, 256 * h + 256)
        block = gm_ref[64 * h : 64 * h + 64, :]
        for src, dst, lanes, at in (
            (p_ref, dp_ref, slice(0, BP), slice(0, BP)),
            (c_ref, dv_ref, slice(BP, BP + OUTER), slice(BP + B0, LAYER)),
        ):
            up = exact(matrix, block[:, at])
            sums, norms, back = s_ref[:, lanes], n_ref[:, lanes], b_ref[:, lanes]
            for f in range(2):
                values = src[f, rows, :]
                _, y = normed(values, sums, norms, voxels)
                dv = norm_back(up * slope(y), values, sums, norms, back, voxels)
                dst[f, rows, :] = dv.astype(BF)
                if dst is dv_ref:
                    turned_ref[1 - f, rows, :] = mm(turn, dv.astype(BF)).astype(BF)


def put(out_ref, place, rows, lane, value):
    size = out_ref.shape[-1]
    done, width = 0, value.shape[1]
    while done < width:
        part, at = divmod(lane + done, size)
        step = min(width - done, size - at)
        out_ref[part, place, rows, at : at + step] = value[:, done : done + step].astype(BF)
        done += step


def taps_out(out_ref, t, grad, slots):
    places = len(slots)
    for z, slot in enumerate(slots):
        put(out_ref, slot, slice(0, 80), B1R * t, grad[80 * z : 80 * z + 80, :B1R])
        low = grad[80 * places + 32 * z : 80 * places + 32 * z + 32, B1R:INNER]
        put(out_ref, slot, slice(80, 96), B2R * t, low[:16])
        put(out_ref, slot, slice(80, 96), NARROW_AT + B2R * t, low[16:])


def wide_lanes(a):
    return jnp.concatenate([a.astype(F32), jnp.zeros((a.shape[0], 64), F32)], 1)


def kernel_grad4_body(me_ref, a_ref, before_ref, after_ref, dv_ref, out_ref, patches, turned):
    out_ref[...] = jnp.zeros_like(out_ref)
    slots = [jnp.bitwise_xor(me_ref[0], z) for z in range(4)]
    for f in range(2):
        turned[:, 512 * f : 512 * f + 512] = dv_ref[f].astype(F32).T.astype(BF)
    for n in range(9):
        for q in range(4):
            rim = before_ref if q == 0 else after_ref
            a = rim[:, BP:] if q in (0, 3) else a_ref[q - 1]
            patches[n % 2, q] = shifted(wide_lanes(a), 8, n // 3 - 1, n % 3 - 1).astype(BF)
        for i in range(3):
            window = patches[n % 2, i : i + 2].reshape(1024, 256)
            taps_out(out_ref, 9 * i + n, mm(turned[...], window), slots)


def kernel_grad5_body(a_ref, dv_ref, out_ref, patches, turned):
    out_ref[...] = jnp.zeros_like(out_ref)
    for q in (0, 5):
        patches[q] = jnp.zeros(patches.shape[1:], BF)
    for q in range(4):
        a = wide_lanes(a_ref[q])
        for n in range(9):
            patches[q + 1, :, 256 * n : 256 * n + 256] = shifted(a, 4, n // 3 - 1, n % 3 - 1).astype(BF)
        turned[:, 128 * q : 128 * q + 128] = dv_ref[q].astype(F32).T.astype(BF)
    for t in range(TAPS):
        i, n = t // 9, t % 9
        window = patches[i : i + 4, :, 256 * n : 256 * n + 256].reshape(512, 256)
        taps_out(out_ref, t, mm(turned[...], window), [0])


def front_back4_body(
    gm_ref, z_ref, s_ref, n_ref, own_ref, before_ref, after_ref, dp_ref, dy_ref, u_ref, x_ref, *, voxels
):
    two, pool, turn = two_matrix(True), pool_matrix(256, 8), turn_matrix(256, 64)
    x_ref[...] = jnp.zeros_like(x_ref)
    for h in range(2):
        rows = slice(256 * h, 256 * h + 256)
        up = exact(two, gm_ref[64 * h : 64 * h + 64, BP : BP + B0])
        for f in range(2):
            rim = before_ref if f == 0 else after_ref
            v = dp_ref[0, rows, :].astype(F32) + dp_ref[1, rows, :].astype(F32)
            v = (v + rim[rows, :BP].astype(F32)).astype(BF)
            u_ref[f, rows, :] = (mm(pool, v) * (1.0 / 27.0)).astype(BF)
            inner = exact(turn, own_ref[1 - f, rows, :] + rim[rows, BP:].astype(F32))
            for lanes, grad in ((slice(0, B0), up), (slice(B0, REDUCED), inner)):
                at = slice(BP + lanes.start, BP + lanes.stop)
                scaled, y = normed(z_ref[f, rows, at], s_ref[:, lanes], n_ref[:, lanes], voxels)
                dy = grad * slope(y)
                dy_ref[f, rows, lanes] = dy
                add_pair(x_ref, lanes, dy, dy * scaled)


def front_grad4_body(z_ref, s_ref, n_ref, dy_ref, b0, b1, b2, b3, u_ref, x_ref, g_ref, out_ref, b_ref, *, voxels):
    b_ref[...] = total_of((b0, b1, b2, b3))
    total = 0.0
    for f in range(2):
        for h in range(2):
            rows = slice(256 * h, 256 * h + 256)
            g_ref[f, rows, :BP] = u_ref[f, rows, :]
            g_ref[f, rows, BP:] = norm_back(
                dy_ref[f, rows, :], z_ref[f, rows, BP:], s_ref[...], n_ref[...], b_ref[...], voxels
            ).astype(BF)
        turned = g_ref[f].astype(F32).T.astype(BF)
        total = total + mm(turned, x_ref[:, f].reshape(512, x_ref.shape[3]))
    front_rows(total, out_ref)


def clips_grad_body(g_ref, w_ref, out_ref):
    for f in range(2):
        for h in range(2):
            grad = mm(g_ref[f, 256 * h : 256 * h + 256, :], w_ref[...])
            out_ref[4 * h : 4 * h + 4, f] = grad.reshape(4, 64, out_ref.shape[3])


def lines(buf, first, count, starts, width):
    out = []
    for r in range(4):
        rows = pl.ds(first + r, count, stride=4)
        part = []
        for at in starts:
            tiles = [buf[at + n, rows, :] for n in range(-(-width // 128))]
            part.append(jnp.concatenate(tiles, 1)[:, :width])
        out.append(jnp.concatenate(part, 0) if len(part) > 1 else part[0])
    return jnp.concatenate(out, 1)


def rows_body(me_ref, mine_ref, twin_ref, wide_ref, narrow_ref, buf):
    wide, narrow = [], []
    for t in range(2):
        for q in range(4):
            same = me_ref[2] == q % 2
            for n in range(9):
                lanes = slice(128 * n, 128 * (n + 1))
                mine, twin = mine_ref[t, q // 2, :, lanes], twin_ref[t, q // 2, :, lanes]
                buf[9 * q + n] = jnp.where(same, mine.astype(F32), twin.astype(F32))
        wide.append(lines(buf, 0, 20, (0,), TAPS * B1R))
        narrow.append(lines(buf, 80, 4, (0, NARROW_AT // 128), TAPS * B2R))
    for pair, out_ref in ((wide, wide_ref), (narrow, narrow_ref)):
        count, size = pair[0].shape
        for n in range(count):
            rows = [part[n : n + 1] for part in pair]
            out_ref[:, size * n : size * (n + 1)] = jnp.concatenate(rows, 0)


def fronts_body(both_ref, entry4_ref, pool4_ref, entry5_ref, pool5_ref):
    for q in range(4):
        pair = [both_ref[t, q].astype(F32) for t in range(2)]
        for lanes, entry_ref, pool_ref in (
            (slice(0, 528), entry4_ref, pool4_ref),
            (slice(576, 1408), entry5_ref, pool5_ref),
        ):
            size = lanes.stop - lanes.start
            for n in range(36):
                row = n if n < 28 else n + 4
                value = jnp.concatenate([p[row : row + 1, lanes] for p in pair], 0)
                at = 28 * q + n if n < 28 else 8 * q + n - 28
                (entry_ref if n < 28 else pool_ref)[:, size * at : size * (at + 1)] = value


def features_body(me_ref, z_ref, s_ref, n_ref, r0, r1, r2, r3, out_ref, *, voxels):
    rest = 0.0
    for k, r in enumerate((r0, r1, r2, r3)):
        rest = rest + mm(r[...], own_columns(jnp.bitwise_xor(me_ref[0], k), True))
    _, y = normed(z_ref[:, BP : BP + B0], s_ref[:, :B0], n_ref[:, :B0], voxels)
    out_ref[:, :B0] = silu(y)
    out_ref[:, B0:] = rest[:, B0:]


def xor_pairs(axis, step):
    return [(i, i ^ step) for i in range(lax.axis_size(axis))]


def tower_steps():
    steps, step = [], 1
    while step < lax.axis_size("dp") // 2:
        steps.append(step)
        step *= 2
    return steps


def other_tower(value):
    return lax.ppermute(value, "dp", xor_pairs("dp", lax.axis_size("dp") // 2))


def blk_peers(value):
    count = lax.axis_size("blk")
    return [value] + [lax.ppermute(value, "blk", xor_pairs("blk", k)) for k in range(1, count)]


def by_place(parts):
    me, step = lax.axis_index("blk"), 1
    while step < len(parts):
        hit = (me & step) != 0
        parts = [jnp.where(hit, parts[k ^ step], parts[k]) for k in range(len(parts))]
        step *= 2
    return parts


def swap_blk(mine):
    return [mine[0]] + [
        lax.ppermute(mine[k], "blk", xor_pairs("blk", k)) for k in range(1, lax.axis_size("blk"))
    ]


def dp_sum(value):
    for step in tower_steps():
        value = value + lax.ppermute(value, "dp", xor_pairs("dp", step))
    return value


def tower_parts(value):
    return blk_peers(dp_sum(value))


def gather_pieces(shard):
    rows = shard.shape[0] // 2
    odd = lax.axis_index("dp") % 2
    half = lax.dynamic_slice_in_dim(shard, odd * rows, rows, 0)
    mine = blk_peers(half)[1:]
    twins = [lax.ppermute(piece, "dp", xor_pairs("dp", 1)) for piece in mine]
    return [shard] + mine + twins


def fours():
    return [list(range(i, i + 4)) for i in range(0, lax.axis_size("dp"), 4)]


def scatter_four(value):
    value = lax.psum_scatter(
        value, "dp", scatter_dimension=0, axis_index_groups=fours(), tiled=False
    )
    for step in tower_steps()[2:]:
        got = lax.ppermute(value, "dp", xor_pairs("dp", step))
        value = (value.astype(F32) + got.astype(F32)).astype(BF)
    return value


def gather_eight(value):
    half = lax.axis_size("dp") // 2
    groups = [
        [b + i for i in range(4)] + [half + b + i for i in range(4)] for b in range(0, half, 4)
    ]
    return lax.all_gather(value, "dp", axis_index_groups=groups, tiled=False)


def after(values, first):
    values, _ = lax.optimization_barrier((values, first))
    return values


def rim_swap(first, last):
    count = lax.axis_size("blk")
    ahead = [(i, i + 1) for i in range(count - 1)]
    back = [(i + 1, i) for i in range(count - 1)]
    return lax.ppermute(last, "blk", ahead), lax.ppermute(first, "blk", back)


def step_rows(value, axis, step, first=None):
    if step in tower_steps()[:2]:
        rows = value.shape[axis] // 2
        high = (lax.axis_index("dp") & step) != 0
        keep = lax.dynamic_slice_in_dim(value, jnp.where(high, rows, 0), rows, axis)
        give = lax.dynamic_slice_in_dim(value, jnp.where(high, 0, rows), rows, axis)
    else:
        keep = give = value
    got = lax.ppermute(give, "dp", xor_pairs("dp", step))
    if first is not None:
        got = after(got, first)
    return (keep.astype(F32) + got.astype(F32)).astype(BF)


def reduce_rows(value, axis, steps=None):
    for step in tower_steps() if steps is None else steps:
        value = step_rows(value, axis, step)
    return value


def reduce_blk(value):
    count = value.shape[0]
    got = swap_blk(by_place([value[j] for j in range(count)]))
    total = got[0].astype(F32)
    for piece in got[1:]:
        total = total + piece.astype(F32)
    return total.astype(BF)


def spread_rows(value):
    stream = lax.axis_index("dp") // (lax.axis_size("dp") // 2)
    other = other_tower(value)
    both = jnp.where(stream == 0, jnp.stack([value, other]), jnp.stack([other, value]))
    for step in (2, 1):
        got = lax.ppermute(both, "dp", xor_pairs("dp", step))
        high = (lax.axis_index("dp") & step) != 0
        both = jnp.where(
            high, jnp.concatenate([got, both], 1), jnp.concatenate([both, got], 1)
        )
    return both


def branch_rows(me, mine, twin):
    return call(
        rows_body,
        (shape_of((2, 80 * TAPS * B1R)), shape_of((2, 32 * TAPS * B2R))),
        me, mine, twin,
        micros=3, mib=16, scratch=[pltpu.VMEM((36, 96, 128), F32)],
    )


def pick_row(param, stream):
    size = param.shape[1]
    return lax.dynamic_index_in_dim(param.reshape(2, size // 128, 128), stream, 0, keepdims=False)


def on_device(clips, cotangent, *params):
    groups = lax.axis_size("dp")
    count = lax.axis_size("blk")
    stream = lax.axis_index("dp") // (groups // 2)
    place = lax.axis_index("blk")
    index = lax.axis_index("dp")
    me = jnp.stack([place, index % (groups // 2), index % 2, index // 2 % 2]).astype(jnp.int32)
    own = [pick_row(p, stream) for p in params]
    early, late = own[:6], own[6:]
    n, frames, height, breadth, c_first = clips.shape
    voxels = groups // 2 * count * n * frames * height * breadth
    late_voxels = voxels // 8
    x = clips.reshape(n, frames, height * breadth, c_first)
    e, p = REDUCED // count, BP // count
    g = (REDUCED + OUTER + BP) // count

    def pack_front(layer, c, turn=0):
        norms = jnp.concatenate([layer[4].reshape(-1), layer[5].reshape(-1)])
        row = jnp.pad(norms, (0, c - 2 * g)).reshape(1, c)
        rows = jnp.concatenate([layer[0].reshape(e, c), layer[3].reshape(p, c)])
        if turn:
            rows = jnp.concatenate([rows[:, c - turn :], rows[:, : c - turn]], 1)
        return jnp.pad(jnp.concatenate([rows, row]), ((0, 160 - e - p - 1), (0, 0)))

    def pack_branch(layer):
        wide = layer[1].reshape(80, -1)
        narrow = layer[2].reshape(32, -1)
        gap = jnp.zeros((16, NARROW_AT - narrow.shape[1]), BF)
        low = jnp.concatenate([narrow[:16], gap, narrow[16:]], 1)
        low = jnp.pad(low, ((0, 0), (0, wide.shape[1] - low.shape[1])))
        return jnp.concatenate([wide, low])

    packed = lax.dynamic_slice_in_dim(pack_branch(early), index % 2 * 48, 48, 0)
    pieces = gather_pieces(pack_front(after(early, packed), c_first))
    packed = lax.all_gather(packed, "blk", tiled=False)
    late_front = pack_front(late, LAYER, BP)
    late = after(late, pieces[0])
    taps_5 = call(kernels5_body, shape_of((TAPS, 128, INNER), BF), pack_branch(late), micros=2)
    x = after(x, taps_5)
    z, m, front_4, nf4, nb4 = call(
        front4_body,
        (
            shape_of((2, 512, 576)), shape_of((2, REDUCED)), shape_of((576, c_first), BF),
            shape_of((2, REDUCED)), shape_of((2, 576)),
        ),
        me, x, *pieces, micros=0,
        scratch=[pltpu.VMEM((4, 160, c_first), BF), pltpu.VMEM((2, 1024), F32)],
    )
    late, cotangent = after((late, cotangent), m)
    cot = cotangent.reshape(128, LAYER)
    cot_mine = call(cot5_body, shape_of((4, 128, 256), BF), me, cot, micros=2)

    def conv(values, kernel, pads, order):
        return lax.conv_general_dilated(
            values,
            kernel.reshape(-1, 3, 3, *kernel.shape[1:]),
            (1, 1, 1),
            pads,
            dimension_numbers=("DNHWC", order, "DNHWC"),
            preferred_element_type=F32,
        )

    forth, back = "DHWOI", "DHWIO"
    flat_pads = ((0, 0), (1, 1), (1, 1))
    same = ((1, 1), (1, 1), (1, 1))
    at4 = functools.partial(functools.partial, voxels=voxels)
    at5 = functools.partial(functools.partial, voxels=late_voxels)

    parts = tower_parts(m)
    z_then = after(z, (cot_mine, late_front))
    a, rims, sf4 = call(
        at4(act4_body),
        (shape_of((2, 512, INNER), BF), shape_of((2, 512, BP + INNER), BF), shape_of((2, REDUCED))),
        z_then, *parts, nf4, micros=0,
    )
    before, behind = rim_swap(rims[0], rims[1])
    packed = after(packed, a)
    late_front = lax.all_gather(after(late_front, packed), "blk", tiled=False)
    twin = lax.ppermute(packed, "dp", xor_pairs("dp", 1))
    taps_4, taps_first, taps_last = call(
        kernels4_body,
        (
            shape_of((TAPS, OUTER, INNER), BF),
            shape_of((9, OUTER, INNER), BF), shape_of((9, OUTER, INNER), BF),
        ),
        me, packed, twin, micros=5, mib=12, away=(1, 2),
        scratch=[pltpu.VMEM((4, 96, 4320), BF), pltpu.SemaphoreType.DMA((2,))],
    )
    before, behind = after((before, behind), taps_4)
    pool, m_pool, a_pad = call(
        pool4_body,
        (shape_of((2, 512, BP)), shape_of((2, BP)), shape_of((4, 512, INNER), BF)),
        rims, before, behind, micros=1,
    )
    a_pad = a_pad.reshape(4, n, height, breadth, INNER)
    c = conv(a_pad, taps_4, flat_pads, forth).reshape(2, 512, OUTER)
    front_5, n5f, n5 = call(
        front5_body,
        (shape_of((576, LAYER), BF), shape_of((2, 1024)), shape_of((2, 256))),
        me, late_front, micros=1,
    )
    cots = swap_blk([after(cot_mine, c)[k] for k in range(4)])
    parts = tower_parts(call(moments_body, shape_of((2, 576)), c, m_pool, micros=1))

    mid, z5, m, sb4 = call(
        at4(norm4_body),
        (shape_of((128, LAYER), BF), shape_of((128, 576)), shape_of((2, REDUCED)), shape_of((2, 576))),
        z, c, pool, sf4, *parts, nf4, nb4, front_5, micros=4, lazy=(0, 2, 3, 8, 9, 10),
    )
    send, sf5 = call(
        at5(act5_body),
        (shape_of((4, 128, 256), BF), shape_of((2, REDUCED))),
        me, z5, *tower_parts(m), n5f, micros=1,
    )
    a5, pool5 = call(
        join5_body,
        (shape_of((4, 128, INNER), BF), shape_of((4, 128, 128))),
        me, *swap_blk([send[k] for k in range(4)]),
        micros=1, scratch=[pltpu.VMEM((6, 128, 128), F32)],
    )
    small = (4, n, height // 2, breadth // 2, -1)
    c5 = conv(a5.reshape(small), taps_5, same, forth).reshape(4, 128, 128)
    s5 = dp_sum(call(moments5_body, shape_of((2, 256)), c5, pool5, micros=1))
    feat, dy5, m = call(
        at5(norm5_body),
        (shape_of((4, 128, 256), BF), shape_of((4, 128, 256)), shape_of((2, 256))),
        me, c5, pool5, s5, n5, *cots, micros=1, lazy=(2, 4, 5, 6, 7, 8),
    )

    feat = swap_blk([feat[k] for k in range(4)])
    b5 = after(dp_sum(m), feat)
    dv5, turned5, u5 = call(
        at5(back5_body),
        (shape_of((4, 128, 128), BF), shape_of((4, 128, 128), BF), shape_of((4, 128, 128))),
        c5, pool5, s5, n5, dy5, b5, micros=1, lazy=(0, 1, 2, 3, 4),
    )
    part = conv(turned5.reshape(small), taps_5, same, back).reshape(4, 128, INNER)
    send = call(send5_body, shape_of((4, 128, 256), BF), me, part, u5, micros=1)
    dv5 = after(dv5, send)
    got5 = swap_blk([send[k] for k in range(4)])
    branch_part5 = call(
        kernel_grad5_body,
        shape_of((4, 1, 96, 1152), BF),
        a5, dv5,
        micros=2, mib=16,
        scratch=[pltpu.VMEM((6, 128, 2304), BF), pltpu.VMEM((128, 512), BF)],
    )
    z5 = after(z5, branch_part5)
    branch_5 = scatter_four(branch_part5)
    dyf5, u5, m = call(
        at5(front_back5_body),
        (shape_of((128, REDUCED)), shape_of((128, BP), BF), shape_of((2, 1536))),
        me, *got5, z5, sf5, n5f, cot[:, :B0], b5, micros=1,
        lazy=(5, 6, 7, 8, 9),
    )
    parts = tower_parts(m)
    g5, gm, m, back5 = call(
        at4(mid_back_body),
        (shape_of((128, 576), BF), shape_of((128, LAYER)), shape_of((2, 576)), shape_of((2, 1536))),
        dyf5, z5, sf5, n5f, *parts, u5, front_5, c, pool, sb4, nb4, micros=4,
        lazy=(0, 1, 2, 3, 8, 9, 10, 11, 12, 13),
    )

    parts = tower_parts(m)
    front_part5 = call(
        front_grad5_body, shape_of((4, 4, 40, LAYER), BF), after(g5, parts[0]), mid, micros=1
    )
    front_part5 = jnp.concatenate([front_part5[..., BP:], front_part5[..., :BP]], 3)
    front_5_sum = step_rows(front_part5, 0, 1)
    gm = after(gm, front_5_sum)
    both5 = gather_eight(after(branch_5, parts[0])[0]).reshape(2, 4, 96, 1152)
    dv, dp, turned4, bb4 = call(
        at4(branch_grad4_body),
        (
            shape_of((2, 512, OUTER), BF), shape_of((2, 512, BP), BF),
            shape_of((2, 512, OUTER), BF), shape_of((2, 576)),
        ),
        gm, c, pool, sb4, nb4, *parts, micros=0, lazy=(1, 2, 3, 4),
    )
    image = (1, n, height, breadth, OUTER)
    rim_first = conv(turned4[1].reshape(image), taps_first, flat_pads, back).reshape(512, INNER)
    rim_last = conv(turned4[0].reshape(image), taps_last, flat_pads, back).reshape(512, INNER)
    rim_first = jnp.concatenate([dp[0], rim_first.astype(BF)], 1)
    rim_last = jnp.concatenate([dp[1], rim_last.astype(BF)], 1)
    got_before, got_after = rim_swap(rim_first, rim_last)
    branch_part4 = call(
        kernel_grad4_body,
        shape_of((4, 4, 96, 1152), BF),
        me, a, before, behind, after(dv, (rim_first, rim_last)),
        micros=0, mib=10,
        scratch=[pltpu.VMEM((2, 4, 512, 256), BF), pltpu.VMEM((OUTER, 1024), BF)],
    )
    turned4 = after(turned4, (branch_part4, both5))
    branch_part4 = scatter_four(branch_part4)
    front_5_sum = reduce_rows(front_5_sum, 0, tower_steps()[1:])[0]
    inner = conv(turned4.reshape(2, n, height, breadth, OUTER), taps_4, same, back)
    dyf4, u4, m = call(
        at4(front_back4_body),
        (shape_of((2, 512, REDUCED)), shape_of((2, 512, BP), BF), shape_of((2, REDUCED))),
        gm, z, sf4, nf4, inner.reshape(2, 512, INNER), got_before, got_after, dp, micros=4,
        lazy=(0, 1, 2, 3, 5, 6, 7),
    )
    parts = tower_parts(m)
    branch_4 = after(branch_part4, parts[3])
    both5 = both5.reshape(2, 2, 2, 96, 1152)
    wide_5, narrow_5 = branch_rows(jnp.zeros_like(me), both5[:, :, 0], both5[:, :, 1])
    z = after(z, (front_5_sum, wide_5, narrow_5))
    g4, front_part4, bf4 = call(
        at4(front_grad4_body),
        (shape_of((2, 512, 576), BF), shape_of((4, 4, 40, c_first), BF), shape_of((2, REDUCED))),
        z, sf4, nf4, dyf4, *parts, u4, x, micros=4, lazy=(1, 2),
    )
    clips_grad = call(
        clips_grad_body, shape_of((n, frames, height * breadth, c_first)), g4, front_4, micros=3
    )

    norms4 = jnp.concatenate([bf4, bb4[:, BP:], bb4[:, :BP]], 1)
    all5 = back5[:, 512:].reshape(2, count, 256)
    norms5 = jnp.concatenate(
        [
            back5[:, :REDUCED],
            all5[:, :, :80].reshape(2, -1),
            all5[:, :, 80:112].reshape(2, -1),
            all5[:, :, 128 + POOL_LANE : 160 + POOL_LANE].reshape(2, -1),
        ],
        axis=1,
    )
    norms = jnp.stack([norms4, norms5])
    theirs = other_tower(norms)
    fronts = after(step_rows(front_part4, 0, 1), branch_4)
    got = swap_blk([branch_4[k] for k in range(4)])
    fronts = step_rows(fronts, 0, 2, got)
    fronts = reduce_rows(fronts, 0, tower_steps()[2:])[0]
    fronts = jnp.concatenate([fronts, jnp.zeros((4, 40, 48), BF), front_5_sum], 2)
    branch_4 = sum(piece.astype(F32) for piece in got).astype(BF)
    features = call(
        at5(features_body), shape_of((128, LAYER)), me, z5, sf5, n5f, *feat, micros=2
    ).reshape(cotangent.shape)

    side = lax.ppermute(branch_4, "dp", xor_pairs("dp", 2))
    other = other_tower(branch_4)
    fronts = after(fronts, (branch_4, theirs, features, clips_grad))
    norms = jnp.where(stream == 0, jnp.stack([norms, theirs]), jnp.stack([theirs, norms]))
    norms = lax.dynamic_slice_in_dim(norms, place * g, g, 3)
    gains_4, shifts_4, gains_5, shifts_5 = (norms[:, 0, 1], norms[:, 0, 0], norms[:, 1, 1], norms[:, 1, 0])
    got = swap_blk(by_place([fronts[j] for j in range(count)]))
    fronts = sum(piece.astype(F32) for piece in got).astype(BF)
    corner = jnp.concatenate(
        [
            lax.ppermute(other[:48], "dp", xor_pairs("dp", 2)),
            other_tower(side[48:]),
        ]
    )
    corner = after(corner, (gains_4, shifts_4, gains_5, shifts_5))
    right = index // 2 % 2 == 1
    ours = jnp.where(right, jnp.stack([side, branch_4]), jnp.stack([branch_4, side]))
    others = jnp.where(right, jnp.stack([corner, other]), jnp.stack([other, corner]))
    both = jnp.where(stream == 0, jnp.stack([ours, others]), jnp.stack([others, ours]))
    wide_4, narrow_4 = branch_rows(me, both, lax.ppermute(both, "dp", xor_pairs("dp", 1)))
    entry_4, poolproj_4, entry_5, poolproj_5 = call(
        fronts_body,
        (
            shape_of((2, 112 * c_first)), shape_of((2, 32 * c_first)),
            shape_of((2, 112 * LAYER)), shape_of((2, 32 * LAYER)),
        ),
        spread_rows(fronts[None]), micros=2, mib=10,
    )

    return (
        features, clips_grad.reshape(clips.shape),
        entry_4, wide_4, narrow_4, poolproj_4, gains_4, shifts_4,
        entry_5, wide_5, narrow_5, poolproj_5, gains_5, shifts_5,
    )


def solution(mesh):
    spec = P("dp", "blk", None, None, None)
    flat = P(None, "blk")
    return jax.shard_map(
        on_device,
        mesh=mesh,
        in_specs=(spec, spec) + (flat,) * 12,
        out_specs=(spec, spec) + (flat,) * 12,
        check_vma=False,
    )
```
